32 devices in a mesh: rhs: 16 (over z, y, x), node: 2 (over core).
Axes of the slice: x: 2, y: 2, z: 4, core: 2. Of those that a mesh axis runs over, the one named last changes fastest.
Arguments:
- right_side: float32 [2048, 4096], P('node', 'rhs'), may hold values from -6 to 6
- diag_inv: float32 [8, 256, 256], P('node', 'rhs'), may hold values from -1 to 1
- lower: float32 [8, 256, 256], P('node', 'rhs'), may hold values from -0.4375 to 0.4375
- factor_pattern: int32 [8, 4, 4], P('node'), may hold values 0 or 1
- jacobian: float32 [8, 256, 768], P('node', 'rhs'), may hold values from -0.078125 to 0.078125
- jacobian_pattern: int32 [8, 4, 12], P('node'), may hold values 0 or 1
Outputs:
- solution: float32 [2048, 4096], P('node', 'rhs')
- residual: float32 [2048, 4096], P('node', 'rhs')
The draws below stay inside these ranges and needn't reach their ends.
All inputs are finite; a program needn't handle non-finite values. No bound on the sum of `factor_pattern` or of `jacobian_pattern` on one device may be relied on, other than what follows from the above.
Results may differ from the reference program's by a relative error of at most 0.00021.
Values sent between devices are 32-bit elements; how exact they have to be, the bound alone decides.
No kernel may reach another device: no remote copies, remote signals or barrier semaphores. Data moves between devices by JAX's collectives and lax.ppermute only.
A program may use at most 64 MiB of HBM per device.

```python
import jax
import jax.numpy as jnp
from jax import lax

B = 64
SN = 4
PANEL = 256
SUPER = 8
ORDER = 2048
RHS = 4096


def draw_diag_inv(key, part):
    key_diag, key_off = jax.random.split(key)
    diagonal_part = jax.random.uniform(key_diag, (SUPER, PANEL), jnp.float32, 0.75, 1.0)
    spread = jax.random.normal(key_off, (SUPER, PANEL, PANEL), jnp.float32) * (0.3 / PANEL ** 0.5)
    unit_matrix = jnp.eye(PANEL, dtype=jnp.float32)
    return spread * (1.0 - unit_matrix) + diagonal_part[:, :, None] * unit_matrix


def set_ends(values, key, least, high):
    extent = values.shape
    spot = [jax.random.randint(jax.random.fold_in(key, axis), (), 0, extent[axis]) for axis in range(len(extent))]
    values = values.at[tuple(spot)].set(least)
    longest = extent.index(max(extent))
    spot[longest] = (spot[longest] + 1) % extent[longest]
    return values.at[tuple(spot)].set(high)


def level_of(key, extent, cuts, smallest, high):
    loudness = 1.0
    for axis_at, parts in cuts:
        steps = jax.random.uniform(jax.random.fold_in(jax.random.fold_in(key, 6), axis_at), (parts,), jnp.float32, smallest / len(cuts), high / len(cuts))
        loudness = loudness * jnp.repeat(jnp.exp(steps), extent[axis_at] // parts).reshape((-1,) + (1,) * (len(extent) - 1 - axis_at))
    return loudness


def normal_values(rng, extent, scale, bound, cuts=(), held_as=jnp.bfloat16):
    loudness = level_of(rng, extent, cuts, -0.22, 0.18) if cuts else 1.0
    array = jax.random.normal(rng, extent, jnp.float32) * scale * loudness
    return jnp.minimum(jnp.maximum(array, -bound), bound).astype(held_as)


def setup_inputs(seed: int = 0) -> dict:
    seeds = jax.random.split(jax.random.key(seed), 7)
    right_side = normal_values(seeds[0], (ORDER, RHS), 1.0, 6.0, ((0, 2), (1, 16)), jnp.float32)
    diag_inv = draw_diag_inv(jax.random.fold_in(seeds[6], 71), 0)
    lower = normal_values(seeds[2], (SUPER, PANEL, PANEL), (SN * B * 4 // 5) ** -0.5, 0.4375, ((0, 2), (1, 16)), jnp.float32)
    factor_pattern = set_ends((jax.random.randint(seeds[3], (SUPER, SN, SN), 0, 4) < 3).astype(jnp.int32), jax.random.fold_in(seeds[3], 1), 0, 1)
    jacobian = normal_values(seeds[4], (SUPER, PANEL, 3 * PANEL), (24 * SN * B) ** -0.5, 0.078125, ((0, 2), (1, 16)), jnp.float32)
    jacobian_pattern = set_ends((jax.random.randint(seeds[5], (SUPER, SN, 3 * SN), 0, 4) < 3).astype(jnp.int32), jax.random.fold_in(seeds[5], 1), 0, 1)
    return {"right_side": right_side, "diag_inv": diag_inv, "lower": lower, "factor_pattern": factor_pattern, "jacobian": jacobian, "jacobian_pattern": jacobian_pattern}


HIGHEST_PREC = lax.Precision.HIGHEST
TRANSPOSED = (((0,), (0,)), ((), ()))


def expand_pattern(pattern):
    return jnp.repeat(jnp.repeat(pattern, B, axis=1), B, axis=2).astype(jnp.float32)


def reference(right_side, diag_inv, lower, factor_pattern, jacobian, jacobian_pattern):
    columns = right_side.shape[1]
    rhs_blocks = right_side.reshape(SUPER, PANEL, columns)
    masked_lower = lower * expand_pattern(factor_pattern)
    masked_jacobian = jacobian * expand_pattern(jacobian_pattern)

    def advance_down(previous, inputs):
        inv_block, low_block, rhs_block = inputs
        coupled = jnp.dot(low_block, previous, precision=HIGHEST_PREC)
        solved = jnp.dot(inv_block, rhs_block - coupled, precision=HIGHEST_PREC)
        return solved, solved

    zero_state = jnp.zeros((PANEL, columns), jnp.float32)
    unused, forward = lax.scan(advance_down, zero_state, (diag_inv, masked_lower, rhs_blocks))

    def advance_up(incoming, inputs):
        inv_block, low_block, forward_block = inputs
        solved = lax.dot_general(inv_block, forward_block - incoming, TRANSPOSED, precision=HIGHEST_PREC)
        passed = lax.dot_general(low_block, solved, TRANSPOSED, precision=HIGHEST_PREC)
        return passed, solved

    unused, solution = lax.scan(advance_up, zero_state, (diag_inv, masked_lower, forward), reverse=True)

    zero_block = jnp.zeros((1, PANEL, columns), jnp.float32)
    padded = jnp.concatenate([zero_block, solution, zero_block], axis=0)

    def residual_block(position):
        window = lax.dynamic_slice_in_dim(padded, position, 3, 0).reshape(3 * PANEL, columns)
        jac_block = lax.dynamic_index_in_dim(masked_jacobian, position, 0, keepdims=False)
        rhs_block = lax.dynamic_index_in_dim(rhs_blocks, position, 0, keepdims=False)
        return rhs_block - jnp.dot(jac_block, window, precision=HIGHEST_PREC)

    residual = lax.map(residual_block, jnp.arange(SUPER, dtype=jnp.int32))
    return solution.reshape(ORDER, columns), residual.reshape(ORDER, columns)
```

```python
import functools

import jax
import jax.numpy as jnp
from jax import lax
from jax.experimental import pallas as pl
from jax.experimental.pallas import tpu as pltpu
from jax.sharding import PartitionSpec as P

VMEM = pl.BlockSpec(memory_space=pltpu.VMEM)
SMEM = pl.BlockSpec(memory_space=pltpu.SMEM)
ANY = pl.BlockSpec(memory_space=pl.ANY)
VMEM_LIMIT = 48 * 2**20
PLAIN = (((1,), (0,)), ((), ()))


def split(value):
    high = value.astype(jnp.bfloat16)
    return high, (value - high.astype(jnp.float32)).astype(jnp.bfloat16)


def product(left, right, dims=PLAIN):
    dot = functools.partial(lax.dot_general, dimension_numbers=dims, preferred_element_type=jnp.float32)
    return dot(left[0], right[1]) + dot(left[1], right[0]) + dot(left[0], right[0])


def gather_rows(part, axis):
    count = lax.axis_size(axis)
    parts = part.shape[0]
    half = parts // 2
    if count < 4 or count & (count - 1):
        everything = lax.all_gather(part, axis, axis=1)
        return [(everything, 0, [(place, place) for place in range(count)])], False

    def across(value, mask):
        return lax.ppermute(value, axis, [(i, i ^ mask) for i in range(count)])

    lines = [0] + [high << 2 for high in range(1, count >> 2)]
    own = jnp.stack([part] + [across(part, mask) for mask in lines[1:]], axis=1)
    first, second = across(own, 1), across(own, 2)
    third = [across(first[:half], 2), across(second[half:], 1)]

    def slots(low):
        return [(place, mask | low) for place, mask in enumerate(lines)]

    return [
        (own, 0, slots(0)),
        (first, 0, slots(1)),
        (second, 0, slots(2)),
        (third[0], 0, slots(3)),
        (third[1], half, slots(3)),
    ], True


def place_rows(pieces, refs, relative, axis, panels, sem):
    me = lax.axis_index(axis)
    rows = pieces[0][0].shape[2]
    copies = []
    for (array, start, slots), ref in zip(pieces, refs):
        for place, mask in slots:
            owner = me ^ mask if relative else mask
            at = pl.multiple_of(owner * rows, rows) if relative else owner * rows
            copies.append(
                pltpu.make_async_copy(
                    ref.at[:, place],
                    panels.at[pl.ds(start, array.shape[0]), pl.ds(at, rows), :],
                    sem.at[len(copies)],
                )
            )
    for copy in copies:
        copy.start()
    return copies


def shapes(arrays):
    return [jax.ShapeDtypeStruct(shape, jnp.float32) for shape in arrays]


def solve(pieces, relative, right_side, weights, node, nodes, supers, size):
    columns = right_side.shape[1]
    extra = 0 if nodes == 1 else 1 if nodes == 2 else 2
    width = columns + extra * size
    n = len(pieces)
    n_copies = sum(len(slots) for _, _, slots in pieces)

    def kernel(*refs):
        node_ref, weights_ref, rhs_ref = refs[:3]
        piece_refs = refs[3 : 3 + n]
        sol_ref = refs[3 + n]
        extra_refs = refs[4 + n : 4 + n + extra]
        down_ref, up_ref, panels, forward, sem = refs[4 + n + extra :]
        copies = place_rows(pieces, piece_refs, relative, "rhs", panels, sem)
        index = node_ref[0]
        below = jnp.where(index > 0, 1.0, 0.0)
        above = jnp.where(index < nodes - 1, 1.0, 0.0)
        on_diagonal = lax.broadcasted_iota(jnp.int32, (size, size), 0) == lax.broadcasted_iota(
            jnp.int32, (size, size), 1
        )
        zeros = jnp.zeros((size, size), jnp.float32)
        for copy in copies:
            copy.wait()

        def masked(s):
            tall = panels[supers + s]
            blocks = weights_ref.shape[1]
            step = size // blocks
            return jnp.concatenate(
                [tall[a * step : (a + 1) * step] * weights_ref[s, a : a + 1, :] for a in range(blocks)], axis=0
            )

        previous = None
        for s in range(supers):
            own = rhs_ref[s * size : (s + 1) * size, :]
            low = masked(s)
            panels[supers + s] = low
            if s == 0:
                parts = [own]
                if extra:
                    parts.append(low * -below)
                if extra == 2:
                    parts.append(zeros)
                target = jnp.concatenate(parts, axis=1)
            else:
                target = jnp.concatenate([own] + [zeros] * extra, axis=1) - product(split(low), split(previous))
            previous = product(split(panels[s]), split(target))
            forward[s] = previous
        down_ref[...] = previous

        entering = None
        for s in reversed(range(supers)):
            target = forward[s]
            if s == supers - 1:
                if extra:
                    unit = jnp.where(on_diagonal, above, 0.0)
                    shift = [jnp.zeros((size, columns), jnp.float32)] + [zeros] * (extra - 1) + [unit]
                    target = target - jnp.concatenate(shift, axis=1)
            else:
                target = target - entering
            solved = product(split(panels[s].T), split(target))
            sol_ref[s * size : (s + 1) * size, :] = solved[:, :columns]
            for e, ref in enumerate(extra_refs):
                ref[s * size : (s + 1) * size, :] = solved[:, columns + e * size : columns + (e + 1) * size]
            if s > 0 or nodes > 1:
                entering = product(split(panels[supers + s].T), split(solved))
        up_ref[...] = entering if nodes > 1 else previous

    span = supers * size
    out = pl.pallas_call(
        kernel,
        out_shape=shapes([(span, columns)] + [(span, size)] * extra + [(size, width)] * 2),
        in_specs=[SMEM, VMEM, VMEM] + [ANY] * n,
        out_specs=[VMEM] * (3 + extra),
        scratch_shapes=[
            pltpu.VMEM((2 * supers, size, size), jnp.float32),
            pltpu.VMEM((supers, size, width), jnp.float32),
            pltpu.SemaphoreType.DMA((n_copies,)),
        ],
        compiler_params=pltpu.CompilerParams(vmem_limit_bytes=VMEM_LIMIT),
        cost_estimate=pl.CostEstimate(
            flops=6 * 4 * supers * size * size * width, bytes_accessed=16 * span * size, transcendentals=0
        ),
        name="solve",
    )(node, weights, right_side, *[array for array, _, _ in pieces])
    return out[0], out[1 : 1 + extra], out[1 + extra], out[2 + extra]


def finish(sol, part, own_mail, mail, node, size):
    span, columns = sol.shape

    def kernel(node_ref, sol_ref, part_ref, own_ref, mail_ref, out_ref, before_ref, after_ref):
        lower_one = node_ref[0] == 0
        down = jnp.where(lower_one, own_ref[0], mail_ref[0])
        offset = jnp.where(lower_one, mail_ref[0], own_ref[0])
        matrix = jnp.where(lower_one, mail_ref[1], own_ref[1])
        up = offset + product(split(matrix), split(down))
        mine = split(jnp.where(lower_one, up, down))
        other = split(jnp.where(lower_one, down, up))
        for at in range(0, span, size):
            out_ref[at : at + size, :] = sol_ref[at : at + size, :] + product(
                split(part_ref[at : at + size, :]), mine
            )
        beside = mail_ref[2] + product(split(mail_ref[3]), other)
        before_ref[...] = jnp.where(lower_one, 0.0, beside)
        after_ref[...] = jnp.where(lower_one, beside, 0.0)

    return pl.pallas_call(
        kernel,
        out_shape=shapes([(span, columns), (size, columns), (size, columns)]),
        in_specs=[SMEM] + [VMEM] * 4,
        out_specs=[VMEM] * 3,
        compiler_params=pltpu.CompilerParams(vmem_limit_bytes=VMEM_LIMIT),
        cost_estimate=pl.CostEstimate(
            flops=6 * (span + 2 * size) * size * columns, bytes_accessed=20 * span * columns, transcendentals=0
        ),
        name="finish",
    )(node, sol, part, own_mail, mail)


def subtract_product(pieces, relative, right_side, sol, before, after, weights, supers, size):
    span, columns = sol.shape
    wide = weights.shape[2]
    blocks = weights.shape[1]
    step = size // blocks
    n = len(pieces)
    n_copies = sum(len(slots) for _, _, slots in pieces)

    def kernel(*refs):
        weights_ref, rhs_ref, sol_ref, before_ref, after_ref = refs[:5]
        piece_refs = refs[5 : 5 + n]
        out_ref, panels, high, low, sem = refs[5 + n :]
        copies = place_rows(pieces, piece_refs, relative, "rhs", panels, sem)
        for at, value in (
            (0, before_ref[...]),
            (size + span, after_ref[...]),
            *((size + s * size, sol_ref[s * size : (s + 1) * size, :]) for s in range(supers)),
        ):
            high[at : at + size, :], low[at : at + size, :] = split(value)
        for copy in copies:
            copy.wait()
        for s in range(supers):
            rows = panels[s]
            panel = jnp.concatenate(
                [rows[a * step : (a + 1) * step] * weights_ref[s, a : a + 1, :] for a in range(blocks)], axis=0
            )
            window = pl.ds(s * size, wide)
            out_ref[s * size : (s + 1) * size, :] = rhs_ref[s * size : (s + 1) * size, :] - product(
                split(panel), (high[window, :], low[window, :])
            )

    return pl.pallas_call(
        kernel,
        out_shape=shapes([(span, columns)])[0],
        in_specs=[VMEM] * 5 + [ANY] * n,
        out_specs=VMEM,
        scratch_shapes=[
            pltpu.VMEM((supers, size, wide), jnp.float32),
            pltpu.VMEM((span + 2 * size, columns), jnp.bfloat16),
            pltpu.VMEM((span + 2 * size, columns), jnp.bfloat16),
            pltpu.SemaphoreType.DMA((n_copies,)),
        ],
        compiler_params=pltpu.CompilerParams(vmem_limit_bytes=VMEM_LIMIT),
        cost_estimate=pl.CostEstimate(
            flops=6 * span * wide * columns, bytes_accessed=4 * span * (wide + 3 * columns), transcendentals=0
        ),
        name="residual",
    )(weights, right_side, sol, before, after, *[array for array, _, _ in pieces])


def dot(left, right):
    return jnp.dot(left, right, precision=lax.Precision.HIGHEST)


def on_device(right_side, diag_inv, lower, factor_pattern, jacobian, jacobian_pattern):
    supers, rows, size = diag_inv.shape
    columns = right_side.shape[1]
    span = supers * size
    nodes = lax.axis_size("node")
    node = jnp.reshape(lax.axis_index("node").astype(jnp.int32), (1,))

    def widened(pattern):
        return jnp.repeat(pattern.astype(jnp.float32), size // factor_pattern.shape[2], axis=2)

    factor, relative = gather_rows(jnp.concatenate([diag_inv, lower], axis=0), "rhs")
    jacobians, _ = gather_rows(jacobian, "rhs")

    sol, parts, down, up = solve(
        factor, relative, right_side, widened(factor_pattern), node, nodes, supers, size
    )
    empty = jnp.zeros((size, columns), jnp.float32)
    if nodes == 1:
        before, after = empty, empty
    elif nodes == 2:
        last, first = slice(span - size, span), slice(0, size)
        is_lower = lax.axis_index("node") == 0
        own_mail = jnp.where(
            is_lower,
            jnp.stack([down[:, :columns], down[:, columns:], sol[last], parts[0][last]]),
            jnp.stack([up[:, :columns], up[:, columns:], sol[first], parts[0][first]]),
        )
        mail = lax.ppermute(own_mail, "node", [(0, 1), (1, 0)])
        sol, before, after = finish(sol, parts[0], own_mail, mail, node, size)
    else:
        upwards = [(i, i + 1) for i in range(nodes - 1)]
        downwards = [(i + 1, i) for i in range(nodes - 1)]
        below = above = empty
        for _ in range(nodes - 1):
            below = lax.ppermute(
                down[:, :columns] + dot(down[:, columns : columns + size], below), "node", upwards
            )
        for _ in range(nodes - 1):
            leaving = up[:, :columns] + dot(up[:, columns : columns + size], below)
            above = lax.ppermute(leaving + dot(up[:, columns + size :], above), "node", downwards)
        sol = sol + dot(parts[0], below) + dot(parts[1], above)
        before = lax.ppermute(sol[span - size :], "node", upwards)
        after = lax.ppermute(sol[:size], "node", downwards)
    residual = subtract_product(
        jacobians, relative, right_side, sol, before, after, widened(jacobian_pattern), supers, size
    )
    return sol, residual


def solution(mesh):
    in_specs = (
        P("node", "rhs"),
        P("node", "rhs", None),
        P("node", "rhs", None),
        P("node", None, None),
        P("node", "rhs", None),
        P("node", None, None),
    )
    out_specs = (P("node", "rhs"), P("node", "rhs"))
    return jax.shard_map(on_device, mesh=mesh, in_specs=in_specs, out_specs=out_specs, check_vma=False)
```

```python
import functools

import jax
import jax.numpy as jnp
from jax import lax
from jax.experimental import pallas as pl
from jax.experimental.pallas import tpu as pltpu
from jax.sharding import PartitionSpec as P

VMEM = pl.BlockSpec(memory_space=pltpu.VMEM)
SMEM = pl.BlockSpec(memory_space=pltpu.SMEM)
ANY = pl.BlockSpec(memory_space=pl.ANY)
VMEM_LIMIT = 48 * 2**20
PLAIN = (((1,), (0,)), ((), ()))


def split(value):
    high = value.astype(jnp.bfloat16)
    return high, (value - high.astype(jnp.float32)).astype(jnp.bfloat16)


def product(left, right, dims=PLAIN):
    dot = functools.partial(lax.dot_general, dimension_numbers=dims, preferred_element_type=jnp.float32)
    return dot(left[0], right[1]) + dot(left[1], right[0]) + dot(left[0], right[0])


def across(value, axis, mask):
    return lax.ppermute(value, axis, [(i, i ^ mask) for i in range(lax.axis_size(axis))])


def line_masks(axis):
    high = lax.axis_size(axis) // 4
    return [4 * (step - 1) for step in iter_halves(high)]


def iter_halves(step):
    while step > 1:
        yield step
        step //= 2


def spread(held, masks, axis):
    for mask in masks:
        held = jnp.concatenate([held, across(held, axis, mask)])
    return held


def line_order(masks):
    order = [0]
    for mask in masks:
        order += [mask ^ other for other in order]
    return order


def around(held, axis):
    return across(held, axis, 1), across(held, axis, 2)


def onward(first, second, axis):
    half = first.shape[1] // 2
    return across(first[:, :half], axis, 2), across(second[:, half:], axis, 1)


def piece(array, order, low, start=0, column=0):
    return array, [mask | low for mask in order], start, column


def pieces_of(own, first, second, third, order, column=0):
    half = third[0].shape[1]
    return ([piece(own, order, 0, 0, column)] if own is not None else []) + [
        piece(first, order, 1, 0, column),
        piece(second, order, 2, 0, column),
        piece(third[0], order, 3, 0, column),
        piece(third[1], order, 3, half, column),
    ]


def gather_whole(part, axis):
    everything = lax.all_gather(part, axis)
    return [piece(everything, list(range(lax.axis_size(axis))), 0)]


def gather_panels(factor_part, jacobian, right_side, axis):
    masks = line_masks(axis)
    order = line_order(masks)
    factor_part, jacobian = factor_part[None], jacobian[None]
    everything = jnp.concatenate([factor_part, jacobian], axis=3)
    split_at = factor_part.shape[3]

    factor_line = spread(factor_part, masks[:1], axis)
    own = around(everything, axis)
    jacobian, factor_line = lax.optimization_barrier((jacobian, factor_line))
    factor_line = spread(factor_line, masks[1:], axis)
    jacobian_line = spread(jacobian, masks[:1], axis)
    factor_line, own = lax.optimization_barrier((factor_line, own))
    own_third = onward(*own, axis)
    factor_rest = around(factor_line[1:], axis)
    jacobian_line = spread(jacobian_line, masks[1:], axis)
    factor_rest, jacobian_line = lax.optimization_barrier((factor_rest, jacobian_line))
    factor_third = onward(*factor_rest, axis)
    jacobian_rest = around(jacobian_line[1:], axis)
    late, jacobian_line = lax.optimization_barrier((right_side, jacobian_line))
    jacobian_third = onward(*jacobian_rest, axis)

    factor = [piece(factor_line, order, 0)]
    factor += pieces_of(None, *own, own_third, order[:1])
    factor += pieces_of(None, *factor_rest, factor_third, order[1:])
    jacobians = [piece(jacobian_line, order, 0)]
    jacobians += pieces_of(None, *own, own_third, order[:1], split_at)
    jacobians += pieces_of(None, *jacobian_rest, jacobian_third, order[1:])
    return factor, jacobians, late


def place_rows(pieces, refs, relative, axis, panels, sem):
    me = lax.axis_index(axis)
    wide = panels.shape[2]
    copies = []
    for (array, owners, start, column), ref in zip(pieces, refs):
        parts, rows = array.shape[1:3]
        for place, owner in enumerate(owners):
            at = pl.multiple_of((me ^ owner) * rows, rows) if relative else owner * rows
            copies.append(
                pltpu.make_async_copy(
                    ref.at[place, :, :, pl.ds(column, wide)],
                    panels.at[pl.ds(start, parts), pl.ds(at, rows), :],
                    sem.at[len(copies)],
                )
            )
    for copy in copies:
        copy.start()
    return copies


def shapes(arrays):
    return [jax.ShapeDtypeStruct(shape, jnp.float32) for shape in arrays]


def solve(pieces, relative, right_side, weights, node, nodes, supers, size):
    columns = right_side.shape[1]
    extra = 0 if nodes == 1 else 1 if nodes == 2 else 2
    width = columns + extra * size
    n = len(pieces)
    n_copies = sum(len(owners) for _, owners, _, _ in pieces)

    def kernel(*refs):
        node_ref, weights_ref, rhs_ref = refs[:3]
        piece_refs = refs[3 : 3 + n]
        sol_ref = refs[3 + n]
        extra_refs = refs[4 + n : 4 + n + extra]
        down_ref, up_ref, panels, forward, sem = refs[4 + n + extra :]
        copies = place_rows(pieces, piece_refs, relative, "rhs", panels, sem)
        index = node_ref[0]
        below = jnp.where(index > 0, 1.0, 0.0)
        above = jnp.where(index < nodes - 1, 1.0, 0.0)
        on_diagonal = lax.broadcasted_iota(jnp.int32, (size, size), 0) == lax.broadcasted_iota(
            jnp.int32, (size, size), 1
        )
        zeros = jnp.zeros((size, size), jnp.float32)
        for copy in copies:
            copy.wait()

        def masked(s):
            tall = panels[s, :, size:]
            blocks = weights_ref.shape[1]
            step = size // blocks
            return jnp.concatenate(
                [tall[a * step : (a + 1) * step] * weights_ref[s, a : a + 1, :] for a in range(blocks)], axis=0
            )

        previous = None
        for s in range(supers):
            own = rhs_ref[s * size : (s + 1) * size, :]
            low = masked(s)
            panels[s, :, size:] = low
            if s == 0:
                parts = [own]
                if extra:
                    parts.append(low * -below)
                if extra == 2:
                    parts.append(zeros)
                target = jnp.concatenate(parts, axis=1)
            else:
                target = jnp.concatenate([own] + [zeros] * extra, axis=1) - product(split(low), split(previous))
            previous = product(split(panels[s, :, :size]), split(target))
            forward[s] = previous
        down_ref[...] = previous

        entering = None
        for s in reversed(range(supers)):
            target = forward[s]
            if s == supers - 1:
                if extra:
                    unit = jnp.where(on_diagonal, above, 0.0)
                    shift = [jnp.zeros((size, columns), jnp.float32)] + [zeros] * (extra - 1) + [unit]
                    target = target - jnp.concatenate(shift, axis=1)
            else:
                target = target - entering
            solved = product(split(panels[s, :, :size].T), split(target))
            sol_ref[s * size : (s + 1) * size, :] = solved[:, :columns]
            for e, ref in enumerate(extra_refs):
                ref[s * size : (s + 1) * size, :] = solved[:, columns + e * size : columns + (e + 1) * size]
            if s > 0 or nodes > 1:
                entering = product(split(panels[s, :, size:].T), split(solved))
        up_ref[...] = entering if nodes > 1 else previous

    span = supers * size
    out = pl.pallas_call(
        kernel,
        out_shape=shapes([(span, columns)] + [(span, size)] * extra + [(size, width)] * 2),
        in_specs=[SMEM, VMEM, VMEM] + [ANY] * n,
        out_specs=[VMEM] * (3 + extra),
        scratch_shapes=[
            pltpu.VMEM((supers, size, 2 * size), jnp.float32),
            pltpu.VMEM((supers, size, width), jnp.float32),
            pltpu.SemaphoreType.DMA((n_copies,)),
        ],
        compiler_params=pltpu.CompilerParams(vmem_limit_bytes=VMEM_LIMIT),
        cost_estimate=pl.CostEstimate(
            flops=4 * supers * size * size * width, bytes_accessed=span * size, transcendentals=0
        ),
        name="solve",
    )(node, weights, right_side, *[array for array, *_ in pieces])
    return out[0], out[1 : 1 + extra], out[1 + extra], out[2 + extra]


def finish(sol, part, own_mail, mail, beside_mail, node, size):
    span, columns = sol.shape

    def kernel(node_ref, sol_ref, part_ref, own_ref, mail_ref, beside_ref, out_ref, before_ref, after_ref):
        lower_one = node_ref[0] == 0
        down = jnp.where(lower_one, own_ref[0], mail_ref[0])
        offset = jnp.where(lower_one, mail_ref[0], own_ref[0])
        matrix = jnp.where(lower_one, mail_ref[1], own_ref[1])
        up = offset + product(split(matrix), split(down))
        mine = split(jnp.where(lower_one, up, down))
        other = split(jnp.where(lower_one, down, up))
        for at in range(0, span, size):
            out_ref[at : at + size, :] = sol_ref[at : at + size, :] + product(
                split(part_ref[at : at + size, :]), mine
            )
        beside = beside_ref[0] + product(split(beside_ref[1]), other)
        before_ref[...] = jnp.where(lower_one, 0.0, beside)
        after_ref[...] = jnp.where(lower_one, beside, 0.0)

    return pl.pallas_call(
        kernel,
        out_shape=shapes([(span, columns), (size, columns), (size, columns)]),
        in_specs=[SMEM] + [VMEM] * 5,
        out_specs=[VMEM] * 3,
        compiler_params=pltpu.CompilerParams(vmem_limit_bytes=VMEM_LIMIT),
        cost_estimate=pl.CostEstimate(
            flops=1 * (span + 2 * size) * size * columns, bytes_accessed=span * columns, transcendentals=0
        ),
        name="finish",
    )(node, sol, part, own_mail, mail, beside_mail)


def subtract_product(pieces, relative, right_side, sol, before, after, weights, supers, size):
    span, columns = sol.shape
    wide = weights.shape[2]
    blocks = weights.shape[1]
    step = size // blocks
    n = len(pieces)
    n_copies = sum(len(owners) for _, owners, _, _ in pieces)

    def kernel(*refs):
        weights_ref, rhs_ref, sol_ref, before_ref, after_ref = refs[:5]
        piece_refs = refs[5 : 5 + n]
        out_ref, panels, high, low, sem = refs[5 + n :]
        copies = place_rows(pieces, piece_refs, relative, "rhs", panels, sem)
        for at, value in (
            (0, before_ref[...]),
            (size + span, after_ref[...]),
            *((size + s * size, sol_ref[s * size : (s + 1) * size, :]) for s in range(supers)),
        ):
            high[at : at + size, :], low[at : at + size, :] = split(value)
        for copy in copies:
            copy.wait()
        for s in range(supers):
            rows = panels[s]
            panel = jnp.concatenate(
                [rows[a * step : (a + 1) * step] * weights_ref[s, a : a + 1, :] for a in range(blocks)], axis=0
            )
            window = pl.ds(s * size, wide)
            out_ref[s * size : (s + 1) * size, :] = rhs_ref[s * size : (s + 1) * size, :] - product(
                split(panel), (high[window, :], low[window, :])
            )

    return pl.pallas_call(
        kernel,
        out_shape=shapes([(span, columns)])[0],
        in_specs=[VMEM] * 5 + [ANY] * n,
        out_specs=VMEM,
        scratch_shapes=[
            pltpu.VMEM((supers, size, wide), jnp.float32),
            pltpu.VMEM((span + 2 * size, columns), jnp.bfloat16),
            pltpu.VMEM((span + 2 * size, columns), jnp.bfloat16),
            pltpu.SemaphoreType.DMA((n_copies,)),
        ],
        compiler_params=pltpu.CompilerParams(vmem_limit_bytes=VMEM_LIMIT),
        cost_estimate=pl.CostEstimate(
            flops=6 * span * wide * columns, bytes_accessed=4 * span * (wide + 3 * columns), transcendentals=0
        ),
        name="residual",
    )(weights, right_side, sol, before, after, *[array for array, *_ in pieces])


def dot(left, right):
    return jnp.dot(left, right, precision=lax.Precision.HIGHEST)


def on_device(right_side, diag_inv, lower, factor_pattern, jacobian, jacobian_pattern):
    supers, rows, size = diag_inv.shape
    columns = right_side.shape[1]
    span = supers * size
    nodes = lax.axis_size("node")
    node = jnp.reshape(lax.axis_index("node").astype(jnp.int32), (1,))

    def widened(pattern):
        return jnp.repeat(pattern.astype(jnp.float32), size // factor_pattern.shape[2], axis=2)

    factor_part = jnp.concatenate([diag_inv, lower], axis=2)
    count = lax.axis_size("rhs")
    relative = count >= 8 and not count & (count - 1)
    late = right_side
    if relative:
        factor, jacobians, late = gather_panels(factor_part, jacobian, right_side, "rhs")
    else:
        factor = gather_whole(factor_part, "rhs")
        jacobians = gather_whole(jacobian, "rhs")

    sol, parts, down, up = solve(
        factor, relative, late, widened(factor_pattern), node, nodes, supers, size
    )
    empty = jnp.zeros((size, columns), jnp.float32)
    if nodes == 1:
        before, after = empty, empty
    elif nodes == 2:
        last, first = slice(span - size, span), slice(0, size)
        is_lower = lax.axis_index("node") == 0
        own_mail = [
            jnp.where(is_lower, jnp.stack(lower_mail), jnp.stack(upper_mail))
            for lower_mail, upper_mail in (
                ([down[:, :columns], down[:, columns:]], [up[:, :columns], up[:, columns:]]),
                ([sol[last], parts[0][last]], [sol[first], parts[0][first]]),
            )
        ]
        mail = [lax.ppermute(letter, "node", [(0, 1), (1, 0)]) for letter in own_mail]
        sol, before, after = finish(sol, parts[0], own_mail[0], *mail, node, size)
    else:
        upwards = [(i, i + 1) for i in range(nodes - 1)]
        downwards = [(i + 1, i) for i in range(nodes - 1)]
        below = above = empty
        for _ in range(nodes - 1):
            below = lax.ppermute(
                down[:, :columns] + dot(down[:, columns : columns + size], below), "node", upwards
            )
        for _ in range(nodes - 1):
            leaving = up[:, :columns] + dot(up[:, columns : columns + size], below)
            above = lax.ppermute(leaving + dot(up[:, columns + size :], above), "node", downwards)
        sol = sol + dot(parts[0], below) + dot(parts[1], above)
        before = lax.ppermute(sol[span - size :], "node", upwards)
        after = lax.ppermute(sol[:size], "node", downwards)
    residual = subtract_product(
        jacobians, relative, right_side, sol, before, after, widened(jacobian_pattern), supers, size
    )
    return sol, residual


def solution(mesh):
    in_specs = (
        P("node", "rhs"),
        P("node", "rhs", None),
        P("node", "rhs", None),
        P("node", None, None),
        P("node", "rhs", None),
        P("node", None, None),
    )
    out_specs = (P("node", "rhs"), P("node", "rhs"))
    return jax.shard_map(on_device, mesh=mesh, in_specs=in_specs, out_specs=out_specs, check_vma=False)
```

```python
import functools

import jax
import jax.numpy as jnp
from jax import lax
from jax.experimental import pallas as pl
from jax.experimental.pallas import tpu as pltpu
from jax.sharding import PartitionSpec as P

VMEM = pl.BlockSpec(memory_space=pltpu.VMEM)
SMEM = pl.BlockSpec(memory_space=pltpu.SMEM)
ANY = pl.BlockSpec(memory_space=pl.ANY)
VMEM_LIMIT = 20 * 2**20
PLAIN = (((1,), (0,)), ((), ()))


def split(value):
    high = value.astype(jnp.bfloat16)
    return high, (value - high.astype(jnp.float32)).astype(jnp.bfloat16)


def product(left, right, dims=PLAIN):
    dot = functools.partial(lax.dot_general, dimension_numbers=dims, preferred_element_type=jnp.float32)
    return dot(left[0], right[1]) + dot(left[1], right[0]) + dot(left[0], right[0])


def across(value, axis, mask):
    return lax.ppermute(value, axis, [(i, i ^ mask) for i in range(lax.axis_size(axis))])


def line_masks(axis):
    high = lax.axis_size(axis) // 4
    return [4 * (step - 1) for step in iter_halves(high)]


def iter_halves(step):
    while step > 1:
        yield step
        step //= 2


def spread(held, masks, axis):
    for mask in masks:
        held = jnp.concatenate([held, across(held, axis, mask)])
    return held


def line_order(masks):
    order = [0]
    for mask in masks:
        order += [mask ^ other for other in order]
    return order


def around(held, axis):
    return across(held, axis, 1), across(held, axis, 2)


def onward(first, second, axis):
    half = first.shape[1] // 2
    return (first,), (second,), (across(first[:, :half], axis, 2), across(second[:, half:], axis, 1))


def piece(array, order, low, start=0, column=0):
    return array, [mask | low for mask in order], start, column


def pieces_of(neighbours, order, column=0):
    return [
        piece(array, order, low, start, column)
        for low, halves in enumerate(neighbours, 1)
        for array, start in zip(halves, (0, halves[0].shape[1]))
    ]


def gather_whole(part, axis):
    everything = lax.all_gather(part, axis)
    return [piece(everything, list(range(lax.axis_size(axis))), 0)]


def gather_panels(factor_part, jacobian, right_side, axis):
    masks = line_masks(axis)
    order = line_order(masks)
    factor_part, jacobian = factor_part[None], jacobian[None]
    everything = jnp.concatenate([factor_part, jacobian], axis=3)
    split_at = factor_part.shape[3]

    factor_line = spread(factor_part, masks[:1], axis)
    own = around(everything, axis)
    (jacobian, factor_line), own = lax.optimization_barrier(((jacobian, factor_line), own))
    factor_line = spread(factor_line, masks[1:], axis)
    jacobian_line = spread(jacobian, masks, axis)
    own = onward(*own, axis)
    factor_line, own = lax.optimization_barrier((factor_line, own))
    factor_rest = onward(*around(factor_line[1:], axis), axis)
    late, jacobian_line = lax.optimization_barrier((right_side, jacobian_line))
    jacobian_rest = onward(*around(jacobian_line[1:], axis), axis)

    factor = [piece(factor_line, order, 0)]
    factor += pieces_of(own, order[:1])
    factor += pieces_of(factor_rest, order[1:])
    jacobians = [piece(jacobian_line, order, 0)]
    jacobians += pieces_of(own, order[:1], split_at)
    jacobians += pieces_of(jacobian_rest, order[1:])
    return factor, jacobians, late


def place_rows(pieces, refs, relative, axis, panels, sem):
    me = lax.axis_index(axis)
    wide = panels.shape[2]
    copies = []
    for (array, owners, start, column), ref in zip(pieces, refs):
        parts, rows = array.shape[1:3]
        for place, owner in enumerate(owners):
            at = pl.multiple_of((me ^ owner) * rows, rows) if relative else owner * rows
            copies.append(
                pltpu.make_async_copy(
                    ref.at[place, :, :, pl.ds(column, wide)],
                    panels.at[pl.ds(start, parts), pl.ds(at, rows), :],
                    sem.at[len(copies)],
                )
            )
    for copy in copies:
        copy.start()
    return copies


def shapes(arrays):
    return [jax.ShapeDtypeStruct(shape, jnp.float32) for shape in arrays]


def solve(pieces, relative, right_side, weights, node, nodes, supers, size):
    columns = right_side.shape[1]
    extra = 0 if nodes == 1 else 1 if nodes == 2 else 2
    width = columns + extra * size
    n = len(pieces)
    n_copies = sum(len(owners) for _, owners, _, _ in pieces)

    def kernel(*refs):
        node_ref, weights_ref, rhs_ref = refs[:3]
        piece_refs = refs[3 : 3 + n]
        sol_ref = refs[3 + n]
        extra_refs = refs[4 + n : 4 + n + extra]
        down_ref, up_ref, panels, forward, sem = refs[4 + n + extra :]
        copies = place_rows(pieces, piece_refs, relative, "rhs", panels, sem)
        index = node_ref[0]
        below = jnp.where(index > 0, 1.0, 0.0)
        above = jnp.where(index < nodes - 1, 1.0, 0.0)
        on_diagonal = lax.broadcasted_iota(jnp.int32, (size, size), 0) == lax.broadcasted_iota(
            jnp.int32, (size, size), 1
        )
        zeros = jnp.zeros((size, size), jnp.float32)
        for copy in copies:
            copy.wait()

        def masked(s):
            tall = panels[s, :, size:]
            blocks = weights_ref.shape[1]
            step = size // blocks
            return jnp.concatenate(
                [tall[a * step : (a + 1) * step] * weights_ref[s, a : a + 1, :] for a in range(blocks)], axis=0
            )

        previous = None
        for s in range(supers):
            own = rhs_ref[s * size : (s + 1) * size, :]
            low = masked(s)
            panels[s, :, size:] = low
            if s == 0:
                parts = [own]
                if extra:
                    parts.append(low * -below)
                if extra == 2:
                    parts.append(zeros)
                target = jnp.concatenate(parts, axis=1)
            else:
                target = jnp.concatenate([own] + [zeros] * extra, axis=1) - product(split(low), split(previous))
            previous = product(split(panels[s, :, :size]), split(target))
            forward[s] = previous
        down_ref[...] = previous

        entering = None
        for s in reversed(range(supers)):
            target = forward[s]
            if s == supers - 1:
                if extra:
                    unit = jnp.where(on_diagonal, above, 0.0)
                    shift = [jnp.zeros((size, columns), jnp.float32)] + [zeros] * (extra - 1) + [unit]
                    target = target - jnp.concatenate(shift, axis=1)
            else:
                target = target - entering
            solved = product(split(panels[s, :, :size].T), split(target))
            sol_ref[s * size : (s + 1) * size, :] = solved[:, :columns]
            for e, ref in enumerate(extra_refs):
                ref[s * size : (s + 1) * size, :] = solved[:, columns + e * size : columns + (e + 1) * size]
            if s > 0 or nodes > 1:
                entering = product(split(panels[s, :, size:].T), split(solved))
        up_ref[...] = entering if nodes > 1 else previous

    span = supers * size
    out = pl.pallas_call(
        kernel,
        out_shape=shapes([(span, columns)] + [(span, size)] * extra + [(size, width)] * 2),
        in_specs=[SMEM, VMEM, VMEM] + [ANY] * n,
        out_specs=[VMEM] * (3 + extra),
        scratch_shapes=[
            pltpu.VMEM((supers, size, 2 * size), jnp.float32),
            pltpu.VMEM((supers, size, width), jnp.float32),
            pltpu.SemaphoreType.DMA((n_copies,)),
        ],
        compiler_params=pltpu.CompilerParams(vmem_limit_bytes=VMEM_LIMIT),
        cost_estimate=pl.CostEstimate(
            flops=4 * supers * size * size * width, bytes_accessed=span * size, transcendentals=0
        ),
        name="solve",
    )(node, weights, right_side, *[array for array, *_ in pieces])
    return out[0], out[1 : 1 + extra], out[1 + extra], out[2 + extra]


def finish(sol, part, own_mail, mail, beside_mail, node, size):
    span, columns = sol.shape

    def kernel(node_ref, sol_ref, part_ref, own_ref, mail_ref, beside_ref, out_ref, before_ref, after_ref):
        lower_one = node_ref[0] == 0
        down = jnp.where(lower_one, own_ref[0], mail_ref[0])
        offset = jnp.where(lower_one, mail_ref[0], own_ref[0])
        matrix = jnp.where(lower_one, mail_ref[1], own_ref[1])
        up = offset + product(split(matrix), split(down))
        mine = split(jnp.where(lower_one, up, down))
        other = split(jnp.where(lower_one, down, up))
        for at in range(0, span, size):
            out_ref[at : at + size, :] = sol_ref[at : at + size, :] + product(
                split(part_ref[at : at + size, :]), mine
            )
        beside = beside_ref[0] + product(split(beside_ref[1]), other)
        before_ref[...] = jnp.where(lower_one, 0.0, beside)
        after_ref[...] = jnp.where(lower_one, beside, 0.0)

    return pl.pallas_call(
        kernel,
        out_shape=shapes([(span, columns), (size, columns), (size, columns)]),
        in_specs=[SMEM] + [VMEM] * 5,
        out_specs=[VMEM] * 3,
        compiler_params=pltpu.CompilerParams(vmem_limit_bytes=VMEM_LIMIT),
        cost_estimate=pl.CostEstimate(
            flops=1 * (span + 2 * size) * size * columns, bytes_accessed=span * columns, transcendentals=0
        ),
        name="finish",
    )(node, sol, part, own_mail, mail, beside_mail)


def subtract_product(pieces, relative, right_side, sol, before, after, weights, supers, size):
    span, columns = sol.shape
    wide = weights.shape[2]
    blocks = weights.shape[1]
    step = size // blocks
    n = len(pieces)
    n_copies = sum(len(owners) for _, owners, _, _ in pieces)

    def kernel(*refs):
        weights_ref, rhs_ref, sol_ref, before_ref, after_ref = refs[:5]
        piece_refs = refs[5 : 5 + n]
        out_ref, panels, high, low, sem = refs[5 + n :]
        copies = place_rows(pieces, piece_refs, relative, "rhs", panels, sem)
        for at, value in (
            (0, before_ref[...]),
            (size + span, after_ref[...]),
            *((size + s * size, sol_ref[s * size : (s + 1) * size, :]) for s in range(supers)),
        ):
            high[at : at + size, :], low[at : at + size, :] = split(value)
        for copy in copies:
            copy.wait()
        for s in range(supers):
            rows = panels[s]
            panel = jnp.concatenate(
                [rows[a * step : (a + 1) * step] * weights_ref[s, a : a + 1, :] for a in range(blocks)], axis=0
            )
            window = pl.ds(s * size, wide)
            out_ref[s * size : (s + 1) * size, :] = rhs_ref[s * size : (s + 1) * size, :] - product(
                split(panel), (high[window, :], low[window, :])
            )

    return pl.pallas_call(
        kernel,
        out_shape=shapes([(span, columns)])[0],
        in_specs=[VMEM] * 5 + [ANY] * n,
        out_specs=VMEM,
        scratch_shapes=[
            pltpu.VMEM((supers, size, wide), jnp.float32),
            pltpu.VMEM((span + 2 * size, columns), jnp.bfloat16),
            pltpu.VMEM((span + 2 * size, columns), jnp.bfloat16),
            pltpu.SemaphoreType.DMA((n_copies,)),
        ],
        compiler_params=pltpu.CompilerParams(vmem_limit_bytes=VMEM_LIMIT),
        cost_estimate=pl.CostEstimate(
            flops=6 * span * wide * columns, bytes_accessed=4 * span * (wide + 3 * columns), transcendentals=0
        ),
        name="residual",
    )(weights, right_side, sol, before, after, *[array for array, *_ in pieces])


def dot(left, right):
    return jnp.dot(left, right, precision=lax.Precision.HIGHEST)


def on_device(right_side, diag_inv, lower, factor_pattern, jacobian, jacobian_pattern):
    supers, rows, size = diag_inv.shape
    columns = right_side.shape[1]
    span = supers * size
    nodes = lax.axis_size("node")
    node = jnp.reshape(lax.axis_index("node").astype(jnp.int32), (1,))

    def widened(pattern):
        return jnp.repeat(pattern.astype(jnp.float32), size // factor_pattern.shape[2], axis=2)

    factor_part = jnp.concatenate([diag_inv, lower], axis=2)
    count = lax.axis_size("rhs")
    relative = count >= 8 and not count & (count - 1)
    late = right_side
    if relative:
        factor, jacobians, late = gather_panels(factor_part, jacobian, right_side, "rhs")
    else:
        factor = gather_whole(factor_part, "rhs")
        jacobians = gather_whole(jacobian, "rhs")

    sol, parts, down, up = solve(
        factor, relative, late, widened(factor_pattern), node, nodes, supers, size
    )
    empty = jnp.zeros((size, columns), jnp.float32)
    if nodes == 1:
        before, after = empty, empty
    elif nodes == 2:
        last, first = slice(span - size, span), slice(0, size)
        is_lower = lax.axis_index("node") == 0
        own_mail = [
            jnp.where(is_lower, jnp.stack(lower_mail), jnp.stack(upper_mail))
            for lower_mail, upper_mail in (
                ([down[:, :columns], down[:, columns:]], [up[:, :columns], up[:, columns:]]),
                ([sol[last], parts[0][last]], [sol[first], parts[0][first]]),
            )
        ]
        mail = [lax.ppermute(letter, "node", [(0, 1), (1, 0)]) for letter in own_mail]
        sol, before, after = finish(sol, parts[0], own_mail[0], *mail, node, size)
    else:
        upwards = [(i, i + 1) for i in range(nodes - 1)]
        downwards = [(i + 1, i) for i in range(nodes - 1)]
        below = above = empty
        for _ in range(nodes - 1):
            below = lax.ppermute(
                down[:, :columns] + dot(down[:, columns : columns + size], below), "node", upwards
            )
        for _ in range(nodes - 1):
            leaving = up[:, :columns] + dot(up[:, columns : columns + size], below)
            above = lax.ppermute(leaving + dot(up[:, columns + size :], above), "node", downwards)
        sol = sol + dot(parts[0], below) + dot(parts[1], above)
        before = lax.ppermute(sol[span - size :], "node", upwards)
        after = lax.ppermute(sol[:size], "node", downwards)
    residual = subtract_product(
        jacobians, relative, right_side, sol, before, after, widened(jacobian_pattern), supers, size
    )
    return sol, residual


def solution(mesh):
    in_specs = (
        P("node", "rhs"),
        P("node", "rhs", None),
        P("node", "rhs", None),
        P("node", None, None),
        P("node", "rhs", None),
        P("node", None, None),
    )
    out_specs = (P("node", "rhs"), P("node", "rhs"))
    return jax.shard_map(on_device, mesh=mesh, in_specs=in_specs, out_specs=out_specs, check_vma=False)
```

```python
import functools

import jax
import jax.numpy as jnp
from jax import lax
from jax.experimental import pallas as pl
from jax.experimental.pallas import tpu as pltpu
from jax.sharding import PartitionSpec as P

VMEM = pl.BlockSpec(memory_space=pltpu.VMEM)
SMEM = pl.BlockSpec(memory_space=pltpu.SMEM)
ANY = pl.BlockSpec(memory_space=pl.ANY)
VMEM_LIMIT = 20 * 2**20
PLAIN = (((1,), (0,)), ((), ()))


def split(value):
    high = value.astype(jnp.bfloat16)
    return high, (value - high.astype(jnp.float32)).astype(jnp.bfloat16)


def product(left, right, dims=PLAIN):
    dot = functools.partial(lax.dot_general, dimension_numbers=dims, preferred_element_type=jnp.float32)
    return dot(left[0], right[1]) + dot(left[1], right[0]) + dot(left[0], right[0])


def across(value, axis, mask):
    return lax.ppermute(value, axis, [(i, i ^ mask) for i in range(lax.axis_size(axis))])


def line_masks(axis):
    high = lax.axis_size(axis) // 4
    return [4 * (step - 1) for step in iter_halves(high)]


def iter_halves(step):
    while step > 1:
        yield step
        step //= 2


def spread(held, masks, axis):
    for mask in masks:
        held = jnp.concatenate([held, across(held, axis, mask)])
    return held


def line_order(masks):
    order = [0]
    for mask in masks:
        order += [mask ^ other for other in order]
    return order


def around(held, axis):
    return across(held, axis, 1), across(held, axis, 2)


def onward(first, second, axis):
    half = first.shape[1] // 2
    return (first,), (second,), (across(first[:, :half], axis, 2), across(second[:, half:], axis, 1))


def piece(array, order, low, start=0, column=0):
    return array, [mask | low for mask in order], start, column


def pieces_of(neighbours, order, column=0):
    return [
        piece(array, order, low, start, column)
        for low, halves in enumerate(neighbours, 1)
        for array, start in zip(halves, (0, halves[0].shape[1]))
    ]


def gather_whole(part, axis):
    everything = lax.all_gather(part, axis)
    return [piece(everything, list(range(lax.axis_size(axis))), 0)]


def gather_panels(factor_part, jacobian, right_side, axis):
    masks = line_masks(axis)
    order = line_order(masks)
    factor_part, jacobian = factor_part[None], jacobian[None]
    everything = jnp.concatenate([factor_part, jacobian], axis=3)
    split_at = factor_part.shape[3]

    factor_line = spread(factor_part, masks[:1], axis)
    own = around(everything, axis)
    (jacobian, factor_line), own = lax.optimization_barrier(((jacobian, factor_line), own))
    factor_line = spread(factor_line, masks[1:], axis)
    jacobian_line = spread(jacobian, masks[:1], axis)
    own = onward(*own, axis)
    factor_line, jacobian_line, own = lax.optimization_barrier((factor_line, jacobian_line, own))
    factor_rest = around(factor_line[1:], axis)
    jacobian_line = spread(jacobian_line, masks[1:], axis)
    late, jacobian_line, _ = lax.optimization_barrier((right_side, jacobian_line, factor_rest))
    factor_rest = onward(*factor_rest, axis)
    jacobian_rest = onward(*around(jacobian_line[1:], axis), axis)

    factor = [piece(factor_line, order, 0)]
    factor += pieces_of(own, order[:1])
    factor += pieces_of(factor_rest, order[1:])
    jacobians = [piece(jacobian_line, order, 0)]
    jacobians += pieces_of(own, order[:1], split_at)
    jacobians += pieces_of(jacobian_rest, order[1:])
    return factor, jacobians, late


def place_rows(pieces, refs, relative, axis, panels, sem):
    me = lax.axis_index(axis)
    wide = panels.shape[2]
    copies = []
    for (array, owners, start, column), ref in zip(pieces, refs):
        parts, rows = array.shape[1:3]
        for place, owner in enumerate(owners):
            at = pl.multiple_of((me ^ owner) * rows, rows) if relative else owner * rows
            copies.append(
                pltpu.make_async_copy(
                    ref.at[place, :, :, pl.ds(column, wide)],
                    panels.at[pl.ds(start, parts), pl.ds(at, rows), :],
                    sem.at[len(copies)],
                )
            )
    for copy in copies:
        copy.start()
    return copies


def shapes(arrays):
    return [jax.ShapeDtypeStruct(shape, jnp.float32) for shape in arrays]


def masked(rows, pattern_ref, s, block_rows):
    wide = rows.shape[1]
    blocks = wide // pattern_ref.shape[2]
    together = max(1, 128 // blocks)
    lane = lax.broadcasted_iota(jnp.int32, (1, together * blocks), 1)
    bands = []
    for a in range(pattern_ref.shape[1]):
        weights = []
        for first in range(0, pattern_ref.shape[2], together):
            chosen = pattern_ref[s, a, first]
            weight = jnp.full(lane.shape, chosen.astype(jnp.float32))
            for c in range(1, min(together, pattern_ref.shape[2] - first)):
                weight = jnp.where(lane >= c * blocks, pattern_ref[s, a, first + c].astype(jnp.float32), weight)
            weights.append(weight)
        weights = jnp.concatenate(weights, axis=1)[:, :wide]
        bands.append(rows[a * block_rows : (a + 1) * block_rows] * weights)
    return jnp.concatenate(bands, axis=0)


def solve(pieces, relative, right_side, pattern, nodes, supers, size):
    columns = right_side.shape[1]
    extra = 0 if nodes == 1 else 1 if nodes == 2 else 2
    width = columns + extra * size
    n = len(pieces)
    n_copies = sum(len(owners) for _, owners, _, _ in pieces)

    def kernel(*refs):
        pattern_ref, rhs_ref = refs[:2]
        piece_refs = refs[2 : 2 + n]
        sol_ref = refs[2 + n]
        extra_refs = refs[3 + n : 3 + n + extra]
        down_ref, up_ref, panels, forward, sem = refs[3 + n + extra :]
        copies = place_rows(pieces, piece_refs, relative, "rhs", panels, sem)
        index = lax.axis_index("node")
        below = jnp.where(index > 0, 1.0, 0.0)
        above = jnp.where(index < nodes - 1, 1.0, 0.0)
        on_diagonal = lax.broadcasted_iota(jnp.int32, (size, size), 0) == lax.broadcasted_iota(
            jnp.int32, (size, size), 1
        )
        zeros = jnp.zeros((size, size), jnp.float32)
        for copy in copies:
            copy.wait()

        previous = None
        for s in range(supers):
            own = rhs_ref[s * size : (s + 1) * size, :]
            low = masked(panels[s, :, size:], pattern_ref, s, size // pattern_ref.shape[1])
            panels[s, :, size:] = low
            if s == 0:
                parts = [own]
                if extra:
                    parts.append(low * -below)
                if extra == 2:
                    parts.append(zeros)
                target = jnp.concatenate(parts, axis=1)
            else:
                target = jnp.concatenate([own] + [zeros] * extra, axis=1) - product(split(low), split(previous))
            previous = product(split(panels[s, :, :size]), split(target))
            forward[s] = previous

        entering = None
        for s in reversed(range(supers)):
            target = forward[s]
            if s == supers - 1:
                if extra:
                    unit = jnp.where(on_diagonal, above, 0.0)
                    shift = [jnp.zeros((size, columns), jnp.float32)] + [zeros] * (extra - 1) + [unit]
                    target = target - jnp.concatenate(shift, axis=1)
            else:
                target = target - entering
            solved = product(split(panels[s, :, :size].T), split(target))
            sol_ref[s * size : (s + 1) * size, :] = solved[:, :columns]
            for e, ref in enumerate(extra_refs):
                ref[s * size : (s + 1) * size, :] = solved[:, columns + e * size : columns + (e + 1) * size]
            if s > 0 or nodes > 1:
                entering = product(split(panels[s, :, size:].T), split(solved))

        if nodes == 2:
            upper = index == 1
            span = supers * size
            down_ref[0] = jnp.where(upper, entering[:, :columns], forward[supers - 1, :, :columns])
            down_ref[1] = entering[:, columns:]
            up_ref[0] = jnp.where(upper, sol_ref[:size, :], sol_ref[span - size :, :])
            up_ref[1] = jnp.where(upper, extra_refs[0][:size, :], extra_refs[0][span - size :, :])
        else:
            down_ref[...] = forward[supers - 1]
            up_ref[...] = entering if nodes > 1 else forward[0]

    span = supers * size
    leaving = (2, size, columns) if nodes == 2 else (size, width)
    out = pl.pallas_call(
        kernel,
        out_shape=shapes([(span, columns)] + [(span, size)] * extra + [leaving] * 2),
        in_specs=[SMEM, VMEM] + [ANY] * n,
        out_specs=[VMEM] * (3 + extra),
        scratch_shapes=[
            pltpu.VMEM((supers, size, 2 * size), jnp.float32),
            pltpu.VMEM((supers, size, width), jnp.float32),
            pltpu.SemaphoreType.DMA((n_copies,)),
        ],
        compiler_params=pltpu.CompilerParams(vmem_limit_bytes=VMEM_LIMIT),
        cost_estimate=pl.CostEstimate(
            flops=4 * supers * size * size * width, bytes_accessed=span * size, transcendentals=0
        ),
        name="solve",
    )(pattern, right_side, *[array for array, *_ in pieces])
    return out[0], out[1 : 1 + extra], out[1 + extra], out[2 + extra]


def finish(sol, part, own_mail, mail, beside_mail, supers):
    span, columns = sol.shape
    size = span // supers

    def kernel(sol_ref, part_ref, own_ref, mail_ref, beside_ref, out_ref, high_ref, low_ref):
        lower_one = lax.axis_index("node") == 0
        down = jnp.where(lower_one, own_ref[0], mail_ref[0])
        offset = jnp.where(lower_one, mail_ref[0], own_ref[0])
        matrix = jnp.where(lower_one, mail_ref[1], own_ref[1])
        up = offset + product(split(matrix), split(down))
        mine = split(jnp.where(lower_one, up, down))
        other = split(jnp.where(lower_one, down, up))

        def window(at, value):
            high_ref[at : at + size, :], low_ref[at : at + size, :] = split(value)

        for at in range(0, span, size):
            value = sol_ref[at : at + size, :] + product(split(part_ref[at : at + size, :]), mine)
            out_ref[at : at + size, :] = value
            window(at + size, value)
        beside = beside_ref[0] + product(split(beside_ref[1]), other)
        window(0, jnp.where(lower_one, 0.0, beside))
        window(size + span, jnp.where(lower_one, beside, 0.0))

    windows = jax.ShapeDtypeStruct((span + 2 * size, columns), jnp.bfloat16)
    return pl.pallas_call(
        kernel,
        out_shape=shapes([(span, columns)]) + [windows, windows],
        in_specs=[VMEM] * 5,
        out_specs=[VMEM] * 3,
        compiler_params=pltpu.CompilerParams(vmem_limit_bytes=VMEM_LIMIT),
        cost_estimate=pl.CostEstimate(
            flops=(span + 2 * size) * size * columns, bytes_accessed=span * columns, transcendentals=0
        ),
        name="finish",
    )(sol, part, own_mail, mail, beside_mail)


def split_windows(sol, before, after):
    span, columns = sol.shape
    size = before.shape[0]

    def kernel(sol_ref, before_ref, after_ref, high_ref, low_ref):
        for at, value in ((0, before_ref[...]), (size, sol_ref[...]), (size + span, after_ref[...])):
            high, low = split(value)
            high_ref[at : at + value.shape[0], :], low_ref[at : at + value.shape[0], :] = high, low

    windows = jax.ShapeDtypeStruct((span + 2 * size, columns), jnp.bfloat16)
    return pl.pallas_call(kernel, out_shape=[windows, windows], name="windows")(sol, before, after)


def subtract_product(pieces, relative, right_side, high, low, pattern, supers, size):
    span, columns = right_side.shape
    wide = 3 * size
    n = len(pieces)
    n_copies = sum(len(owners) for _, owners, _, _ in pieces)

    def kernel(*refs):
        pattern_ref, rhs_ref, high_ref, low_ref = refs[:4]
        piece_refs = refs[4 : 4 + n]
        out_ref, panels, sem = refs[4 + n :]
        for copy in place_rows(pieces, piece_refs, relative, "rhs", panels, sem):
            copy.wait()
        for s in range(supers):
            panel = masked(panels[s], pattern_ref, s, size // pattern_ref.shape[1])
            window = pl.ds(s * size, wide)
            out_ref[s * size : (s + 1) * size, :] = rhs_ref[s * size : (s + 1) * size, :] - product(
                split(panel), (high_ref[window, :], low_ref[window, :])
            )

    return pl.pallas_call(
        kernel,
        out_shape=shapes([(span, columns)])[0],
        in_specs=[SMEM] + [VMEM] * 3 + [ANY] * n,
        out_specs=VMEM,
        scratch_shapes=[
            pltpu.VMEM((supers, size, wide), jnp.float32),
            pltpu.SemaphoreType.DMA((n_copies,)),
        ],
        compiler_params=pltpu.CompilerParams(vmem_limit_bytes=VMEM_LIMIT),
        cost_estimate=pl.CostEstimate(
            flops=6 * span * wide * columns, bytes_accessed=4 * span * (wide + 3 * columns), transcendentals=0
        ),
        name="residual",
    )(pattern, right_side, high, low, *[array for array, *_ in pieces])


def dot(left, right):
    return jnp.dot(left, right, precision=lax.Precision.HIGHEST)


def on_device(right_side, diag_inv, lower, factor_pattern, jacobian, jacobian_pattern):
    supers, rows, size = diag_inv.shape
    columns = right_side.shape[1]
    span = supers * size
    nodes = lax.axis_size("node")

    factor_part = jnp.concatenate([diag_inv, lower], axis=2)
    count = lax.axis_size("rhs")
    relative = count >= 8 and not count & (count - 1)
    late = right_side
    if relative:
        factor, jacobians, late = gather_panels(factor_part, jacobian, right_side, "rhs")
    else:
        factor = gather_whole(factor_part, "rhs")
        jacobians = gather_whole(jacobian, "rhs")

    sol, parts, down, up = solve(factor, relative, late, factor_pattern, nodes, supers, size)
    if nodes == 2:
        mail = [lax.ppermute(letter, "node", [(0, 1), (1, 0)]) for letter in (down, up)]
        sol, high, low = finish(sol, parts[0], down, *mail, supers)
    else:
        before = after = jnp.zeros((size, columns), jnp.float32)
        if nodes > 1:
            upwards = [(i, i + 1) for i in range(nodes - 1)]
            downwards = [(i + 1, i) for i in range(nodes - 1)]
            below = above = before
            for _ in range(nodes - 1):
                below = lax.ppermute(
                    down[:, :columns] + dot(down[:, columns : columns + size], below), "node", upwards
                )
            for _ in range(nodes - 1):
                leaving = up[:, :columns] + dot(up[:, columns : columns + size], below)
                above = lax.ppermute(leaving + dot(up[:, columns + size :], above), "node", downwards)
            sol = sol + dot(parts[0], below) + dot(parts[1], above)
            before = lax.ppermute(sol[span - size :], "node", upwards)
            after = lax.ppermute(sol[:size], "node", downwards)
        high, low = split_windows(sol, before, after)
    residual = subtract_product(jacobians, relative, right_side, high, low, jacobian_pattern, supers, size)
    return sol, residual


def solution(mesh):
    in_specs = (
        P("node", "rhs"),
        P("node", "rhs", None),
        P("node", "rhs", None),
        P("node", None, None),
        P("node", "rhs", None),
        P("node", None, None),
    )
    out_specs = (P("node", "rhs"), P("node", "rhs"))
    return jax.shard_map(on_device, mesh=mesh, in_specs=in_specs, out_specs=out_specs, check_vma=False)
```

```python
import functools

import jax
import jax.numpy as jnp
from jax import lax
from jax.experimental import pallas as pl
from jax.experimental.pallas import tpu as pltpu
from jax.sharding import PartitionSpec as P

VMEM = pl.BlockSpec(memory_space=pltpu.VMEM)
SMEM = pl.BlockSpec(memory_space=pltpu.SMEM)
ANY = pl.BlockSpec(memory_space=pl.ANY)
VMEM_LIMIT = 20 * 2**20
PLAIN = (((1,), (0,)), ((), ()))


def split(value):
    high = value.astype(jnp.bfloat16)
    return high, (value - high.astype(jnp.float32)).astype(jnp.bfloat16)


def product(left, right, dims=PLAIN):
    dot = functools.partial(lax.dot_general, dimension_numbers=dims, preferred_element_type=jnp.float32)
    return dot(left[0], right[1]) + dot(left[1], right[0]) + dot(left[0], right[0])


def across(value, axis, mask):
    return lax.ppermute(value, axis, [(i, i ^ mask) for i in range(lax.axis_size(axis))])


def line_masks(axis):
    high = lax.axis_size(axis) // 4
    return [4 * (step - 1) for step in iter_halves(high)]


def iter_halves(step):
    while step > 1:
        yield step
        step //= 2


def spread(held, masks, axis):
    for mask in masks:
        held = jnp.concatenate([held, across(held, axis, mask)])
    return held


def line_order(masks):
    order = [0]
    for mask in masks:
        order += [mask ^ other for other in order]
    return order


def around(held, axis):
    return across(held, axis, 1), across(held, axis, 2)


def onward(first, second, axis):
    half = first.shape[1] // 2
    return (first,), (second,), (across(first[:, :half], axis, 2), across(second[:, half:], axis, 1))


def piece(array, order, low, start=0, column=0):
    return array, [mask | low for mask in order], start, column


def pieces_of(neighbours, order, column=0):
    return [
        piece(array, order, low, start, column)
        for low, halves in enumerate(neighbours, 1)
        for array, start in zip(halves, (0, halves[0].shape[1]))
    ]


def gather_whole(part, axis):
    everything = lax.all_gather(part, axis)
    return [piece(everything, list(range(lax.axis_size(axis))), 0)]


def gather_panels(factor_part, jacobian, right_side, axis):
    masks = line_masks(axis)
    order = line_order(masks)
    factor_part, jacobian = factor_part[None], jacobian[None]
    everything = jnp.concatenate([factor_part, jacobian], axis=3)
    split_at = factor_part.shape[3]

    factor_line = spread(factor_part, masks[:1], axis)
    jacobian_line = spread(jacobian, masks[:1], axis)
    own = around(everything, axis)
    jacobian_line, own = lax.optimization_barrier((jacobian_line, own))
    own = onward(*own, axis)
    factor_line = spread(factor_line, masks[1:], axis)
    factor_line, own = lax.optimization_barrier((factor_line, own))
    factor_rest = onward(*around(factor_line[1:], axis), axis)
    jacobian_line = spread(jacobian_line, masks[1:], axis)
    late, jacobian_line = lax.optimization_barrier((right_side, jacobian_line))
    jacobian_rest = onward(*around(jacobian_line[1:], axis), axis)

    factor = [piece(factor_line, order, 0)]
    factor += pieces_of(own, order[:1])
    factor += pieces_of(factor_rest, order[1:])
    jacobians = [piece(jacobian_line, order, 0)]
    jacobians += pieces_of(own, order[:1], split_at)
    jacobians += pieces_of(jacobian_rest, order[1:])
    return factor, jacobians, late


def place_rows(pieces, refs, relative, axis, panels, sem):
    me = lax.axis_index(axis)
    wide = panels.shape[2]
    copies = []
    for (array, owners, start, column), ref in zip(pieces, refs):
        parts, rows = array.shape[1:3]
        for place, owner in enumerate(owners):
            at = pl.multiple_of((me ^ owner) * rows, rows) if relative else owner * rows
            copies.append(
                pltpu.make_async_copy(
                    ref.at[place, :, :, pl.ds(column, wide)],
                    panels.at[pl.ds(start, parts), pl.ds(at, rows), :],
                    sem.at[len(copies)],
                )
            )
    for copy in copies:
        copy.start()
    return copies


def shapes(arrays):
    return [jax.ShapeDtypeStruct(shape, jnp.float32) for shape in arrays]


def masked(rows, pattern_ref, s, block_rows):
    wide = rows.shape[1]
    blocks = wide // pattern_ref.shape[2]
    together = max(1, 128 // blocks)
    lane = lax.broadcasted_iota(jnp.int32, (1, together * blocks), 1)
    bands = []
    for a in range(pattern_ref.shape[1]):
        weights = []
        for first in range(0, pattern_ref.shape[2], together):
            chosen = pattern_ref[s, a, first]
            weight = jnp.full(lane.shape, chosen.astype(jnp.float32))
            for c in range(1, min(together, pattern_ref.shape[2] - first)):
                weight = jnp.where(lane >= c * blocks, pattern_ref[s, a, first + c].astype(jnp.float32), weight)
            weights.append(weight)
        weights = jnp.concatenate(weights, axis=1)[:, :wide]
        bands.append(rows[a * block_rows : (a + 1) * block_rows] * weights)
    return jnp.concatenate(bands, axis=0)


def solve(pieces, relative, right_side, pattern, nodes, supers, size):
    columns = right_side.shape[1]
    extra = 0 if nodes == 1 else 1 if nodes == 2 else 2
    width = columns + extra * size
    n = len(pieces)
    n_copies = sum(len(owners) for _, owners, _, _ in pieces)

    def kernel(*refs):
        pattern_ref, rhs_ref = refs[:2]
        piece_refs = refs[2 : 2 + n]
        sol_ref = refs[2 + n]
        extra_refs = refs[3 + n : 3 + n + extra]
        down_ref, up_ref, panels, forward, sem = refs[3 + n + extra :]
        copies = place_rows(pieces, piece_refs, relative, "rhs", panels, sem)
        index = lax.axis_index("node")
        below = jnp.where(index > 0, 1.0, 0.0)
        above = jnp.where(index < nodes - 1, 1.0, 0.0)
        on_diagonal = lax.broadcasted_iota(jnp.int32, (size, size), 0) == lax.broadcasted_iota(
            jnp.int32, (size, size), 1
        )
        zeros = jnp.zeros((size, size), jnp.float32)
        for copy in copies:
            copy.wait()

        previous = None
        for s in range(supers):
            own = rhs_ref[s * size : (s + 1) * size, :]
            low = masked(panels[s, :, size:], pattern_ref, s, size // pattern_ref.shape[1])
            panels[s, :, size:] = low
            if s == 0:
                parts = [own]
                if extra:
                    parts.append(low * -below)
                if extra == 2:
                    parts.append(zeros)
                target = jnp.concatenate(parts, axis=1)
            else:
                target = jnp.concatenate([own] + [zeros] * extra, axis=1) - product(split(low), split(previous))
            previous = product(split(panels[s, :, :size]), split(target))
            forward[s] = previous

        entering = None
        for s in reversed(range(supers)):
            target = forward[s]
            if s == supers - 1:
                if extra:
                    unit = jnp.where(on_diagonal, above, 0.0)
                    shift = [jnp.zeros((size, columns), jnp.float32)] + [zeros] * (extra - 1) + [unit]
                    target = target - jnp.concatenate(shift, axis=1)
            else:
                target = target - entering
            solved = product(split(panels[s, :, :size].T), split(target))
            sol_ref[s * size : (s + 1) * size, :] = solved[:, :columns]
            for e, ref in enumerate(extra_refs):
                ref[s * size : (s + 1) * size, :] = solved[:, columns + e * size : columns + (e + 1) * size]
            if s > 0 or nodes > 1:
                entering = product(split(panels[s, :, size:].T), split(solved))

        if nodes == 2:
            upper = index == 1
            span = supers * size
            down_ref[0] = jnp.where(upper, entering[:, :columns], forward[supers - 1, :, :columns])
            down_ref[1] = entering[:, columns:]
            up_ref[0] = jnp.where(upper, sol_ref[:size, :], sol_ref[span - size :, :])
            up_ref[1] = jnp.where(upper, extra_refs[0][:size, :], extra_refs[0][span - size :, :])
        else:
            down_ref[...] = forward[supers - 1]
            up_ref[...] = entering if nodes > 1 else forward[0]

    span = supers * size
    leaving = (2, size, columns) if nodes == 2 else (size, width)
    out = pl.pallas_call(
        kernel,
        out_shape=shapes([(span, columns)] + [(span, size)] * extra + [leaving] * 2),
        in_specs=[SMEM, VMEM] + [ANY] * n,
        out_specs=[VMEM] * (3 + extra),
        scratch_shapes=[
            pltpu.VMEM((supers, size, 2 * size), jnp.float32),
            pltpu.VMEM((supers, size, width), jnp.float32),
            pltpu.SemaphoreType.DMA((n_copies,)),
        ],
        compiler_params=pltpu.CompilerParams(vmem_limit_bytes=VMEM_LIMIT),
        cost_estimate=pl.CostEstimate(
            flops=16 * supers * size * size * width, bytes_accessed=span * size, transcendentals=0
        ),
        name="solve",
    )(pattern, right_side, *[array for array, *_ in pieces])
    return out[0], out[1 : 1 + extra], out[1 + extra], out[2 + extra]


def finish(sol, part, own_mail, mail, beside_mail, supers):
    span, columns = sol.shape
    size = span // supers

    def kernel(sol_ref, part_ref, own_ref, mail_ref, beside_ref, out_ref, high_ref, low_ref):
        lower_one = lax.axis_index("node") == 0
        down = jnp.where(lower_one, own_ref[0], mail_ref[0])
        offset = jnp.where(lower_one, mail_ref[0], own_ref[0])
        matrix = jnp.where(lower_one, mail_ref[1], own_ref[1])
        up = offset + product(split(matrix), split(down))
        mine = split(jnp.where(lower_one, up, down))
        other = split(jnp.where(lower_one, down, up))

        def window(at, value):
            high_ref[at : at + size, :], low_ref[at : at + size, :] = split(value)

        for at in range(0, span, size):
            value = sol_ref[at : at + size, :] + product(split(part_ref[at : at + size, :]), mine)
            out_ref[at : at + size, :] = value
            window(at + size, value)
        beside = beside_ref[0] + product(split(beside_ref[1]), other)
        window(0, jnp.where(lower_one, 0.0, beside))
        window(size + span, jnp.where(lower_one, beside, 0.0))

    windows = jax.ShapeDtypeStruct((span + 2 * size, columns), jnp.bfloat16)
    return pl.pallas_call(
        kernel,
        out_shape=shapes([(span, columns)]) + [windows, windows],
        in_specs=[VMEM] * 5,
        out_specs=[VMEM] * 3,
        compiler_params=pltpu.CompilerParams(vmem_limit_bytes=VMEM_LIMIT),
        cost_estimate=pl.CostEstimate(
            flops=(span + 2 * size) * size * columns, bytes_accessed=span * columns, transcendentals=0
        ),
        name="finish",
    )(sol, part, own_mail, mail, beside_mail)


def split_windows(sol, before, after):
    span, columns = sol.shape
    size = before.shape[0]

    def kernel(sol_ref, before_ref, after_ref, high_ref, low_ref):
        for at, value in ((0, before_ref[...]), (size, sol_ref[...]), (size + span, after_ref[...])):
            high, low = split(value)
            high_ref[at : at + value.shape[0], :], low_ref[at : at + value.shape[0], :] = high, low

    windows = jax.ShapeDtypeStruct((span + 2 * size, columns), jnp.bfloat16)
    return pl.pallas_call(kernel, out_shape=[windows, windows], name="windows")(sol, before, after)


def subtract_product(pieces, relative, right_side, high, low, pattern, supers, size):
    span, columns = right_side.shape
    wide = 3 * size
    n = len(pieces)
    n_copies = sum(len(owners) for _, owners, _, _ in pieces)

    def kernel(*refs):
        pattern_ref, rhs_ref, high_ref, low_ref = refs[:4]
        piece_refs = refs[4 : 4 + n]
        out_ref, panels, sem = refs[4 + n :]
        for copy in place_rows(pieces, piece_refs, relative, "rhs", panels, sem):
            copy.wait()
        for s in range(supers):
            panel = masked(panels[s], pattern_ref, s, size // pattern_ref.shape[1])
            window = pl.ds(s * size, wide)
            out_ref[s * size : (s + 1) * size, :] = rhs_ref[s * size : (s + 1) * size, :] - product(
                split(panel), (high_ref[window, :], low_ref[window, :])
            )

    return pl.pallas_call(
        kernel,
        out_shape=shapes([(span, columns)])[0],
        in_specs=[SMEM] + [VMEM] * 3 + [ANY] * n,
        out_specs=VMEM,
        scratch_shapes=[
            pltpu.VMEM((supers, size, wide), jnp.float32),
            pltpu.SemaphoreType.DMA((n_copies,)),
        ],
        compiler_params=pltpu.CompilerParams(vmem_limit_bytes=VMEM_LIMIT),
        cost_estimate=pl.CostEstimate(
            flops=6 * span * wide * columns, bytes_accessed=4 * span * (wide + 3 * columns), transcendentals=0
        ),
        name="residual",
    )(pattern, right_side, high, low, *[array for array, *_ in pieces])


def dot(left, right):
    return jnp.dot(left, right, precision=lax.Precision.HIGHEST)


def on_device(right_side, diag_inv, lower, factor_pattern, jacobian, jacobian_pattern):
    supers, rows, size = diag_inv.shape
    columns = right_side.shape[1]
    span = supers * size
    nodes = lax.axis_size("node")

    factor_part = jnp.concatenate([diag_inv, lower], axis=2)
    count = lax.axis_size("rhs")
    relative = count >= 8 and not count & (count - 1)
    late = right_side
    if relative:
        factor, jacobians, late = gather_panels(factor_part, jacobian, right_side, "rhs")
    else:
        factor = gather_whole(factor_part, "rhs")
        jacobians = gather_whole(jacobian, "rhs")

    sol, parts, down, up = solve(factor, relative, late, factor_pattern, nodes, supers, size)
    if nodes == 2:
        mail = [lax.ppermute(letter, "node", [(0, 1), (1, 0)]) for letter in (down, up)]
        sol, high, low = finish(sol, parts[0], down, *mail, supers)
    else:
        before = after = jnp.zeros((size, columns), jnp.float32)
        if nodes > 1:
            upwards = [(i, i + 1) for i in range(nodes - 1)]
            downwards = [(i + 1, i) for i in range(nodes - 1)]
            below = above = before
            for _ in range(nodes - 1):
                below = lax.ppermute(
                    down[:, :columns] + dot(down[:, columns : columns + size], below), "node", upwards
                )
            for _ in range(nodes - 1):
                leaving = up[:, :columns] + dot(up[:, columns : columns + size], below)
                above = lax.ppermute(leaving + dot(up[:, columns + size :], above), "node", downwards)
            sol = sol + dot(parts[0], below) + dot(parts[1], above)
            before = lax.ppermute(sol[span - size :], "node", upwards)
            after = lax.ppermute(sol[:size], "node", downwards)
        high, low = split_windows(sol, before, after)
    residual = subtract_product(jacobians, relative, right_side, high, low, jacobian_pattern, supers, size)
    return sol, residual


def solution(mesh):
    in_specs = (
        P("node", "rhs"),
        P("node", "rhs", None),
        P("node", "rhs", None),
        P("node", None, None),
        P("node", "rhs", None),
        P("node", None, None),
    )
    out_specs = (P("node", "rhs"), P("node", "rhs"))
    return jax.shard_map(on_device, mesh=mesh, in_specs=in_specs, out_specs=out_specs, check_vma=False)
```

```python
import functools

import jax
import jax.numpy as jnp
from jax import lax
from jax.experimental import pallas as pl
from jax.experimental.pallas import tpu as pltpu
from jax.sharding import PartitionSpec as P

VMEM = pl.BlockSpec(memory_space=pltpu.VMEM)
SMEM = pl.BlockSpec(memory_space=pltpu.SMEM)
ANY = pl.BlockSpec(memory_space=pl.ANY)
VMEM_LIMIT = 20 * 2**20
PLAIN = (((1,), (0,)), ((), ()))


def split(value):
    high = value.astype(jnp.bfloat16)
    return high, (value - high.astype(jnp.float32)).astype(jnp.bfloat16)


def product(left, right, dims=PLAIN):
    dot = functools.partial(lax.dot_general, dimension_numbers=dims, preferred_element_type=jnp.float32)
    return dot(left[0], right[1]) + dot(left[1], right[0]) + dot(left[0], right[0])


def after(held, *others):
    return lax.optimization_barrier((held[0], [array for array, _ in others]))[0], held[1]


def joined(*parts):
    if len(parts) == 1:
        return parts[0]
    return jnp.concatenate([array for array, _ in parts]), [name for _, names in parts for name in names]


def cut(held, begin, end):
    return held[0][begin:end], held[1][begin:end]


def sent(held, axis, mask):
    array, names = held
    swapped = lax.ppermute(array, axis, [(i, i ^ mask) for i in range(lax.axis_size(axis))])
    return swapped, [(owner ^ mask, block) for owner, block in names]


def around(held, axis):
    return sent(held, axis, 1), sent(held, axis, 2)


def onward(pair, axis, *more):
    half = len(pair[0][1]) // 2
    first, second = cut(pair[0], 0, half), cut(pair[1], half, 2 * half)
    return joined(*more, second), joined(*more, first)


def gather_panels(own, factor_blocks, right_side, axis):
    steps = lax.axis_size(axis) // 4
    masks = []
    while steps > 1:
        masks.append(4 * (steps - 1))
        steps //= 2
    count = len(own[1])
    factor, jacobian = cut(own, 0, factor_blocks), cut(own, factor_blocks, count)

    factor_line = [factor, sent(factor, axis, masks[0])]
    jacobian_line = [jacobian, sent(jacobian, axis, masks[0])]
    own_round = around(own, axis)
    own_across = [sent(part, axis, mask) for part, mask in zip(onward(own_round, axis), (1, 2))]
    for mask in masks[1:]:
        factor_line.append(sent(joined(*factor_line), axis, mask))
    factor_rest = after(joined(*factor_line[1:]), *own_across)
    factor_round = around(factor_rest, axis)
    for mask in masks[1:]:
        jacobian_line.append(sent(joined(*jacobian_line), axis, mask))
    early_round = around(joined(*jacobian_line[1:-1]), axis)
    factor_across = [sent(part, axis, mask) for part, mask in zip(onward(factor_round, axis), (1, 2))]
    late_parts = onward(early_round, axis, jacobian_line[-1])
    late_round = [sent(part, axis, mask) for part, mask in zip(late_parts, (1, 2))]
    size = len(jacobian_line[-1][1])
    late_across = [
        sent(part, axis, mask)
        for part, mask in zip(onward([cut(part, 0, size) for part in late_round], axis), (1, 2))
    ]
    right_side, _ = after((right_side, None), *late_parts)
    arrived = [own, *factor_line[1:], *jacobian_line[1:], *own_round, *own_across, *factor_round, *factor_across]
    return arrived + [*early_round, *late_round, *late_across], right_side


def gather_whole(own, axis):
    everything = lax.all_gather(own[0], axis, tiled=True)
    return [(everything, [(owner, block) for owner in range(lax.axis_size(axis)) for _, block in own[1]])]


def runs_of(pieces, begin, end):
    chosen = []
    for array, names in pieces:
        runs = []
        for at, (owner, block) in enumerate(names):
            if not begin <= block < end:
                continue
            if runs and runs[-1][0] + runs[-1][1] == at and names[at - 1] == (owner, block - 1):
                runs[-1][1] += 1
            else:
                runs.append([at, 1, owner, block - begin])
        if runs:
            chosen.append((array, runs))
    return chosen


def place_rows(pieces, refs, relative, axis, panels, sem):
    me = lax.axis_index(axis)
    copies = []
    for (array, runs), ref in zip(pieces, refs):
        rows = array.shape[1]
        for at, length, owner, block in runs:
            row = pl.multiple_of((me ^ owner) * rows, rows) if relative else owner * rows
            copies.append(
                pltpu.make_async_copy(
                    ref.at[pl.ds(at, length)],
                    panels.at[pl.ds(block, length), pl.ds(row, rows), :],
                    sem.at[len(copies)],
                )
            )
    for copy in copies:
        copy.start()
    return copies


def shapes(arrays):
    return [jax.ShapeDtypeStruct(shape, jnp.float32) for shape in arrays]


def masked(rows, pattern_ref, s, block_rows):
    wide = rows.shape[1]
    blocks = wide // pattern_ref.shape[2]
    together = max(1, 128 // blocks)
    lane = lax.broadcasted_iota(jnp.int32, (1, together * blocks), 1)
    bands = []
    for a in range(pattern_ref.shape[1]):
        weights = []
        for first in range(0, pattern_ref.shape[2], together):
            chosen = pattern_ref[s, a, first]
            weight = jnp.full(lane.shape, chosen.astype(jnp.float32))
            for c in range(1, min(together, pattern_ref.shape[2] - first)):
                weight = jnp.where(lane >= c * blocks, pattern_ref[s, a, first + c].astype(jnp.float32), weight)
            weights.append(weight)
        weights = jnp.concatenate(weights, axis=1)[:, :wide]
        bands.append(rows[a * block_rows : (a + 1) * block_rows] * weights)
    return jnp.concatenate(bands, axis=0)


def solve(pieces, relative, right_side, pattern, nodes, supers, size):
    columns = right_side.shape[1]
    extra = 0 if nodes == 1 else 1 if nodes == 2 else 2
    width = columns + extra * size
    n = len(pieces)
    n_copies = sum(len(runs) for _, runs in pieces)

    def kernel(*refs):
        pattern_ref, rhs_ref = refs[:2]
        piece_refs = refs[2 : 2 + n]
        sol_ref = refs[2 + n]
        extra_refs = refs[3 + n : 3 + n + extra]
        down_ref, up_ref, panels, forward, sem = refs[3 + n + extra :]
        copies = place_rows(pieces, piece_refs, relative, "rhs", panels, sem)
        index = lax.axis_index("node")
        below = jnp.where(index > 0, 1.0, 0.0)
        above = jnp.where(index < nodes - 1, 1.0, 0.0)
        on_diagonal = lax.broadcasted_iota(jnp.int32, (size, size), 0) == lax.broadcasted_iota(
            jnp.int32, (size, size), 1
        )
        zeros = jnp.zeros((size, size), jnp.float32)
        for copy in copies:
            copy.wait()

        previous = None
        for s in range(supers):
            own = rhs_ref[s * size : (s + 1) * size, :]
            low = masked(panels[supers + s], pattern_ref, s, size // pattern_ref.shape[1])
            panels[supers + s] = low
            if s == 0:
                parts = [own]
                if extra:
                    parts.append(low * -below)
                if extra == 2:
                    parts.append(zeros)
                target = jnp.concatenate(parts, axis=1)
            else:
                target = jnp.concatenate([own] + [zeros] * extra, axis=1) - product(split(low), split(previous))
            previous = product(split(panels[s]), split(target))
            forward[s] = previous

        entering = None
        for s in reversed(range(supers)):
            target = forward[s]
            if s == supers - 1:
                if extra:
                    unit = jnp.where(on_diagonal, above, 0.0)
                    shift = [jnp.zeros((size, columns), jnp.float32)] + [zeros] * (extra - 1) + [unit]
                    target = target - jnp.concatenate(shift, axis=1)
            else:
                target = target - entering
            solved = product(split(panels[s].T), split(target))
            sol_ref[s * size : (s + 1) * size, :] = solved[:, :columns]
            for e, ref in enumerate(extra_refs):
                ref[s * size : (s + 1) * size, :] = solved[:, columns + e * size : columns + (e + 1) * size]
            if s > 0 or nodes > 1:
                entering = product(split(panels[supers + s].T), split(solved))

        if nodes == 2:
            upper = index == 1
            span = supers * size
            down_ref[0] = jnp.where(upper, entering[:, :columns], forward[supers - 1, :, :columns])
            down_ref[1] = entering[:, columns:]
            up_ref[0] = jnp.where(upper, sol_ref[:size, :], sol_ref[span - size :, :])
            up_ref[1] = jnp.where(upper, extra_refs[0][:size, :], extra_refs[0][span - size :, :])
        else:
            down_ref[...] = forward[supers - 1]
            up_ref[...] = entering if nodes > 1 else forward[0]

    span = supers * size
    leaving = (2, size, columns) if nodes == 2 else (size, width)
    out = pl.pallas_call(
        kernel,
        out_shape=shapes([(span, columns)] + [(span, size)] * extra + [leaving] * 2),
        in_specs=[SMEM, VMEM] + [ANY] * n,
        out_specs=[VMEM] * (3 + extra),
        scratch_shapes=[
            pltpu.VMEM((2 * supers, size, size), jnp.float32),
            pltpu.VMEM((supers, size, width), jnp.float32),
            pltpu.SemaphoreType.DMA((n_copies,)),
        ],
        compiler_params=pltpu.CompilerParams(vmem_limit_bytes=VMEM_LIMIT),
        cost_estimate=pl.CostEstimate(
            flops=16 * supers * size * size * width, bytes_accessed=span * size, transcendentals=0
        ),
        name="solve",
    )(pattern, right_side, *[array for array, _ in pieces])
    return out[0], out[1 : 1 + extra], out[1 + extra], out[2 + extra]


def finish(sol, part, own_mail, mail, beside_mail, supers):
    span, columns = sol.shape
    size = span // supers

    def kernel(sol_ref, part_ref, own_ref, mail_ref, beside_ref, out_ref, high_ref, low_ref):
        lower_one = lax.axis_index("node") == 0
        down = jnp.where(lower_one, own_ref[0], mail_ref[0])
        offset = jnp.where(lower_one, mail_ref[0], own_ref[0])
        matrix = jnp.where(lower_one, mail_ref[1], own_ref[1])
        up = offset + product(split(matrix), split(down))
        mine = split(jnp.where(lower_one, up, down))
        other = split(jnp.where(lower_one, down, up))

        def window(at, value):
            high_ref[at : at + size, :], low_ref[at : at + size, :] = split(value)

        for at in range(0, span, size):
            value = sol_ref[at : at + size, :] + product(split(part_ref[at : at + size, :]), mine)
            out_ref[at : at + size, :] = value
            window(at + size, value)
        beside = beside_ref[0] + product(split(beside_ref[1]), other)
        window(0, jnp.where(lower_one, 0.0, beside))
        window(size + span, jnp.where(lower_one, beside, 0.0))

    windows = jax.ShapeDtypeStruct((span + 2 * size, columns), jnp.bfloat16)
    return pl.pallas_call(
        kernel,
        out_shape=shapes([(span, columns)]) + [windows, windows],
        in_specs=[VMEM] * 5,
        out_specs=[VMEM] * 3,
        compiler_params=pltpu.CompilerParams(vmem_limit_bytes=VMEM_LIMIT),
        cost_estimate=pl.CostEstimate(
            flops=(span + 2 * size) * size * columns, bytes_accessed=span * columns, transcendentals=0
        ),
        name="finish",
    )(sol, part, own_mail, mail, beside_mail)


def split_windows(sol, before, after):
    span, columns = sol.shape
    size = before.shape[0]

    def kernel(sol_ref, before_ref, after_ref, high_ref, low_ref):
        for at, value in ((0, before_ref[...]), (size, sol_ref[...]), (size + span, after_ref[...])):
            high, low = split(value)
            high_ref[at : at + value.shape[0], :], low_ref[at : at + value.shape[0], :] = high, low

    windows = jax.ShapeDtypeStruct((span + 2 * size, columns), jnp.bfloat16)
    return pl.pallas_call(kernel, out_shape=[windows, windows], name="windows")(sol, before, after)


def subtract_product(pieces, relative, right_side, high, low, pattern, supers, size):
    span, columns = right_side.shape
    wide = 3 * size
    n = len(pieces)
    n_copies = sum(len(runs) for _, runs in pieces)

    def kernel(*refs):
        pattern_ref, rhs_ref, high_ref, low_ref = refs[:4]
        piece_refs = refs[4 : 4 + n]
        out_ref, panels, sem = refs[4 + n :]
        for copy in place_rows(pieces, piece_refs, relative, "rhs", panels, sem):
            copy.wait()
        for s in range(supers):
            rows = jnp.concatenate([panels[3 * s + c] for c in range(3)], axis=1)
            panel = masked(rows, pattern_ref, s, size // pattern_ref.shape[1])
            window = pl.ds(s * size, wide)
            out_ref[s * size : (s + 1) * size, :] = rhs_ref[s * size : (s + 1) * size, :] - product(
                split(panel), (high_ref[window, :], low_ref[window, :])
            )

    return pl.pallas_call(
        kernel,
        out_shape=shapes([(span, columns)])[0],
        in_specs=[SMEM] + [VMEM] * 3 + [ANY] * n,
        out_specs=VMEM,
        scratch_shapes=[
            pltpu.VMEM((3 * supers, size, size), jnp.float32),
            pltpu.SemaphoreType.DMA((n_copies,)),
        ],
        compiler_params=pltpu.CompilerParams(vmem_limit_bytes=VMEM_LIMIT),
        cost_estimate=pl.CostEstimate(
            flops=6 * span * wide * columns, bytes_accessed=4 * span * (wide + 3 * columns), transcendentals=0
        ),
        name="residual",
    )(pattern, right_side, high, low, *[array for array, _ in pieces])


def dot(left, right):
    return jnp.dot(left, right, precision=lax.Precision.HIGHEST)


def on_device(right_side, diag_inv, lower, factor_pattern, jacobian, jacobian_pattern):
    supers, rows, size = diag_inv.shape
    columns = right_side.shape[1]
    span = supers * size
    nodes = lax.axis_size("node")

    own = jnp.concatenate(
        [diag_inv, lower, jacobian.reshape(supers, rows, 3, size).swapaxes(1, 2).reshape(3 * supers, rows, size)]
    )
    own = own, [(0, block) for block in range(own.shape[0])]
    count = lax.axis_size("rhs")
    relative = count >= 16 and not count & (count - 1)
    if relative:
        arrived, late = gather_panels(own, 2 * supers, right_side, "rhs")
    else:
        arrived, late = gather_whole(own, "rhs"), right_side
    factor = runs_of(arrived, 0, 2 * supers)
    jacobians = runs_of(arrived, 2 * supers, len(own[1]))

    sol, parts, down, up = solve(factor, relative, late, factor_pattern, nodes, supers, size)
    if nodes == 2:
        mail = [lax.ppermute(letter, "node", [(0, 1), (1, 0)]) for letter in (down, up)]
        sol, high, low = finish(sol, parts[0], down, *mail, supers)
    else:
        before = after = jnp.zeros((size, columns), jnp.float32)
        if nodes > 1:
            upwards = [(i, i + 1) for i in range(nodes - 1)]
            downwards = [(i + 1, i) for i in range(nodes - 1)]
            below = above = before
            for _ in range(nodes - 1):
                below = lax.ppermute(
                    down[:, :columns] + dot(down[:, columns : columns + size], below), "node", upwards
                )
            for _ in range(nodes - 1):
                leaving = up[:, :columns] + dot(up[:, columns : columns + size], below)
                above = lax.ppermute(leaving + dot(up[:, columns + size :], above), "node", downwards)
            sol = sol + dot(parts[0], below) + dot(parts[1], above)
            before = lax.ppermute(sol[span - size :], "node", upwards)
            after = lax.ppermute(sol[:size], "node", downwards)
        high, low = split_windows(sol, before, after)
    residual = subtract_product(jacobians, relative, right_side, high, low, jacobian_pattern, supers, size)
    return sol, residual


def solution(mesh):
    in_specs = (
        P("node", "rhs"),
        P("node", "rhs", None),
        P("node", "rhs", None),
        P("node", None, None),
        P("node", "rhs", None),
        P("node", None, None),
    )
    out_specs = (P("node", "rhs"), P("node", "rhs"))
    return jax.shard_map(on_device, mesh=mesh, in_specs=in_specs, out_specs=out_specs, check_vma=False)
```

```python
import functools

import jax
import jax.numpy as jnp
from jax import lax
from jax.experimental import pallas as pl
from jax.experimental.pallas import tpu as pltpu
from jax.sharding import PartitionSpec as P

VMEM = pl.BlockSpec(memory_space=pltpu.VMEM)
SMEM = pl.BlockSpec(memory_space=pltpu.SMEM)
ANY = pl.BlockSpec(memory_space=pl.ANY)
VMEM_LIMIT = 20 * 2**20
PLAIN = (((1,), (0,)), ((), ()))


def split(value):
    high = value.astype(jnp.bfloat16)
    return high, (value - high.astype(jnp.float32)).astype(jnp.bfloat16)


def product(left, right, dims=PLAIN):
    dot = functools.partial(lax.dot_general, dimension_numbers=dims, preferred_element_type=jnp.float32)
    return dot(left[0], right[1]) + dot(left[1], right[0]) + dot(left[0], right[0])


def after(held, *others):
    return lax.optimization_barrier((held[0], [array for array, _ in others]))[0], held[1]


def joined(*parts):
    if len(parts) == 1:
        return parts[0]
    return jnp.concatenate([array for array, _ in parts]), [name for _, names in parts for name in names]


def cut(held, begin, end):
    return held[0][begin:end], held[1][begin:end]


def sent(held, axis, mask):
    array, names = held
    swapped = lax.ppermute(array, axis, [(i, i ^ mask) for i in range(lax.axis_size(axis))])
    return swapped, [(owner ^ mask, block) for owner, block in names]


def around(held, axis):
    return sent(held, axis, 1), sent(held, axis, 2)


def onward(pair, axis, *more):
    half = len(pair[0][1]) // 2
    first, second = cut(pair[0], 0, half), cut(pair[1], half, 2 * half)
    return joined(*more, second), joined(*more, first)


def gather_panels(own, factor_blocks, right_side, axis):
    steps = lax.axis_size(axis) // 4
    masks = []
    while steps > 1:
        masks.append(4 * (steps - 1))
        steps //= 2
    count = len(own[1])
    factor, jacobian = cut(own, 0, factor_blocks), cut(own, factor_blocks, count)

    factor_line = [factor] + [sent(factor, axis, 4 * high) for high in reversed(range(1, lax.axis_size(axis) // 4))]
    jacobian_line = [jacobian, sent(jacobian, axis, masks[0])]
    own_round = around(own, axis)
    own_across = [sent(part, axis, mask) for part, mask in zip(onward(own_round, axis), (1, 2))]
    factor_rest = after(joined(*factor_line[1:]), *own_across)
    factor_round = around(factor_rest, axis)
    for mask in masks[1:]:
        jacobian_line.append(sent(joined(*jacobian_line), axis, mask))
    early_round = around(joined(*jacobian_line[1:-1]), axis)
    factor_across = [sent(part, axis, mask) for part, mask in zip(onward(factor_round, axis), (1, 2))]
    late_parts = onward(early_round, axis, jacobian_line[-1])
    late_round = [sent(part, axis, mask) for part, mask in zip(late_parts, (1, 2))]
    size = len(jacobian_line[-1][1])
    late_across = [
        sent(part, axis, mask)
        for part, mask in zip(onward([cut(part, 0, size) for part in late_round], axis), (1, 2))
    ]
    right_side, _ = after((right_side, None), *late_parts)
    arrived = [own, *factor_line[1:], *jacobian_line[1:], *own_round, *own_across, *factor_round, *factor_across]
    return arrived + [*early_round, *late_round, *late_across], right_side


def gather_whole(own, axis):
    everything = lax.all_gather(own[0], axis, tiled=True)
    return [(everything, [(owner, block) for owner in range(lax.axis_size(axis)) for _, block in own[1]])]


def runs_of(pieces, begin, end):
    chosen = []
    for array, names in pieces:
        runs = []
        for at, (owner, block) in enumerate(names):
            if not begin <= block < end:
                continue
            if runs and runs[-1][0] + runs[-1][1] == at and names[at - 1] == (owner, block - 1):
                runs[-1][1] += 1
            else:
                runs.append([at, 1, owner, block - begin])
        if runs:
            chosen.append((array, runs))
    return chosen


def place_rows(pieces, refs, relative, axis, panels, sem):
    me = lax.axis_index(axis)
    copies = []
    for (array, runs), ref in zip(pieces, refs):
        rows = array.shape[1]
        for at, length, owner, block in runs:
            row = pl.multiple_of((me ^ owner) * rows, rows) if relative else owner * rows
            copies.append(
                pltpu.make_async_copy(
                    ref.at[pl.ds(at, length)],
                    panels.at[pl.ds(block, length), pl.ds(row, rows), :],
                    sem.at[len(copies)],
                )
            )
    for copy in copies:
        copy.start()
    return copies


def shapes(arrays):
    return [jax.ShapeDtypeStruct(shape, jnp.float32) for shape in arrays]


def masked(rows, pattern_ref, s, block_rows):
    wide = rows.shape[1]
    blocks = wide // pattern_ref.shape[2]
    together = max(1, 128 // blocks)
    lane = lax.broadcasted_iota(jnp.int32, (1, together * blocks), 1)
    bands = []
    for a in range(pattern_ref.shape[1]):
        weights = []
        for first in range(0, pattern_ref.shape[2], together):
            chosen = pattern_ref[s, a, first]
            weight = jnp.full(lane.shape, chosen.astype(jnp.float32))
            for c in range(1, min(together, pattern_ref.shape[2] - first)):
                weight = jnp.where(lane >= c * blocks, pattern_ref[s, a, first + c].astype(jnp.float32), weight)
            weights.append(weight)
        weights = jnp.concatenate(weights, axis=1)[:, :wide]
        bands.append(rows[a * block_rows : (a + 1) * block_rows] * weights)
    return jnp.concatenate(bands, axis=0)


def solve(pieces, relative, right_side, pattern, nodes, supers, size):
    columns = right_side.shape[1]
    extra = 0 if nodes == 1 else 1 if nodes == 2 else 2
    width = columns + extra * size
    n = len(pieces)
    n_copies = sum(len(runs) for _, runs in pieces)

    def kernel(*refs):
        pattern_ref, rhs_ref = refs[:2]
        piece_refs = refs[2 : 2 + n]
        sol_ref = refs[2 + n]
        extra_refs = refs[3 + n : 3 + n + extra]
        down_ref, up_ref, panels, forward, sem = refs[3 + n + extra :]
        copies = place_rows(pieces, piece_refs, relative, "rhs", panels, sem)
        index = lax.axis_index("node")
        below = jnp.where(index > 0, 1.0, 0.0)
        above = jnp.where(index < nodes - 1, 1.0, 0.0)
        on_diagonal = lax.broadcasted_iota(jnp.int32, (size, size), 0) == lax.broadcasted_iota(
            jnp.int32, (size, size), 1
        )
        zeros = jnp.zeros((size, size), jnp.float32)
        for copy in copies:
            copy.wait()

        previous = None
        for s in range(supers):
            own = rhs_ref[s * size : (s + 1) * size, :]
            low = masked(panels[supers + s], pattern_ref, s, size // pattern_ref.shape[1])
            panels[supers + s] = low
            if s == 0:
                parts = [own]
                if extra:
                    parts.append(low * -below)
                if extra == 2:
                    parts.append(zeros)
                target = jnp.concatenate(parts, axis=1)
            else:
                target = jnp.concatenate([own] + [zeros] * extra, axis=1) - product(split(low), split(previous))
            previous = product(split(panels[s]), split(target))
            forward[s] = previous

        entering = None
        for s in reversed(range(supers)):
            target = forward[s]
            if s == supers - 1:
                if extra:
                    unit = jnp.where(on_diagonal, above, 0.0)
                    shift = [jnp.zeros((size, columns), jnp.float32)] + [zeros] * (extra - 1) + [unit]
                    target = target - jnp.concatenate(shift, axis=1)
            else:
                target = target - entering
            solved = product(split(panels[s].T), split(target))
            sol_ref[s * size : (s + 1) * size, :] = solved[:, :columns]
            for e, ref in enumerate(extra_refs):
                ref[s * size : (s + 1) * size, :] = solved[:, columns + e * size : columns + (e + 1) * size]
            if s > 0 or nodes > 1:
                entering = product(split(panels[supers + s].T), split(solved))

        if nodes == 2:
            upper = index == 1
            span = supers * size
            down_ref[0] = jnp.where(upper, entering[:, :columns], forward[supers - 1, :, :columns])
            down_ref[1] = entering[:, columns:]
            up_ref[0] = jnp.where(upper, sol_ref[:size, :], sol_ref[span - size :, :])
            up_ref[1] = jnp.where(upper, extra_refs[0][:size, :], extra_refs[0][span - size :, :])
        else:
            down_ref[...] = forward[supers - 1]
            up_ref[...] = entering if nodes > 1 else forward[0]

    span = supers * size
    leaving = (2, size, columns) if nodes == 2 else (size, width)
    out = pl.pallas_call(
        kernel,
        out_shape=shapes([(span, columns)] + [(span, size)] * extra + [leaving] * 2),
        in_specs=[SMEM, VMEM] + [ANY] * n,
        out_specs=[VMEM] * (3 + extra),
        scratch_shapes=[
            pltpu.VMEM((2 * supers, size, size), jnp.float32),
            pltpu.VMEM((supers, size, width), jnp.float32),
            pltpu.SemaphoreType.DMA((n_copies,)),
        ],
        compiler_params=pltpu.CompilerParams(vmem_limit_bytes=VMEM_LIMIT),
        cost_estimate=pl.CostEstimate(
            flops=16 * supers * size * size * width, bytes_accessed=span * size, transcendentals=0
        ),
        name="solve",
    )(pattern, right_side, *[array for array, _ in pieces])
    return out[0], out[1 : 1 + extra], out[1 + extra], out[2 + extra]


def finish(sol, part, own_mail, mail, beside_mail, supers):
    span, columns = sol.shape
    size = span // supers

    def kernel(sol_ref, part_ref, own_ref, mail_ref, beside_ref, out_ref, high_ref, low_ref):
        lower_one = lax.axis_index("node") == 0
        down = jnp.where(lower_one, own_ref[0], mail_ref[0])
        offset = jnp.where(lower_one, mail_ref[0], own_ref[0])
        matrix = jnp.where(lower_one, mail_ref[1], own_ref[1])
        up = offset + product(split(matrix), split(down))
        mine = split(jnp.where(lower_one, up, down))
        other = split(jnp.where(lower_one, down, up))

        def window(at, value):
            high_ref[at : at + size, :], low_ref[at : at + size, :] = split(value)

        for at in range(0, span, size):
            value = sol_ref[at : at + size, :] + product(split(part_ref[at : at + size, :]), mine)
            out_ref[at : at + size, :] = value
            window(at + size, value)
        beside = beside_ref[0] + product(split(beside_ref[1]), other)
        window(0, jnp.where(lower_one, 0.0, beside))
        window(size + span, jnp.where(lower_one, beside, 0.0))

    windows = jax.ShapeDtypeStruct((span + 2 * size, columns), jnp.bfloat16)
    return pl.pallas_call(
        kernel,
        out_shape=shapes([(span, columns)]) + [windows, windows],
        in_specs=[VMEM] * 5,
        out_specs=[VMEM] * 3,
        compiler_params=pltpu.CompilerParams(vmem_limit_bytes=VMEM_LIMIT),
        cost_estimate=pl.CostEstimate(
            flops=(span + 2 * size) * size * columns, bytes_accessed=span * columns, transcendentals=0
        ),
        name="finish",
    )(sol, part, own_mail, mail, beside_mail)


def split_windows(sol, before, after):
    span, columns = sol.shape
    size = before.shape[0]

    def kernel(sol_ref, before_ref, after_ref, high_ref, low_ref):
        for at, value in ((0, before_ref[...]), (size, sol_ref[...]), (size + span, after_ref[...])):
            high, low = split(value)
            high_ref[at : at + value.shape[0], :], low_ref[at : at + value.shape[0], :] = high, low

    windows = jax.ShapeDtypeStruct((span + 2 * size, columns), jnp.bfloat16)
    return pl.pallas_call(kernel, out_shape=[windows, windows], name="windows")(sol, before, after)


def subtract_product(pieces, relative, right_side, high, low, pattern, supers, size):
    span, columns = right_side.shape
    wide = 3 * size
    n = len(pieces)
    n_copies = sum(len(runs) for _, runs in pieces)

    def kernel(*refs):
        pattern_ref, rhs_ref, high_ref, low_ref = refs[:4]
        piece_refs = refs[4 : 4 + n]
        out_ref, panels, sem = refs[4 + n :]
        for copy in place_rows(pieces, piece_refs, relative, "rhs", panels, sem):
            copy.wait()
        for s in range(supers):
            rows = jnp.concatenate([panels[3 * s + c] for c in range(3)], axis=1)
            panel = masked(rows, pattern_ref, s, size // pattern_ref.shape[1])
            window = pl.ds(s * size, wide)
            out_ref[s * size : (s + 1) * size, :] = rhs_ref[s * size : (s + 1) * size, :] - product(
                split(panel), (high_ref[window, :], low_ref[window, :])
            )

    return pl.pallas_call(
        kernel,
        out_shape=shapes([(span, columns)])[0],
        in_specs=[SMEM] + [VMEM] * 3 + [ANY] * n,
        out_specs=VMEM,
        scratch_shapes=[
            pltpu.VMEM((3 * supers, size, size), jnp.float32),
            pltpu.SemaphoreType.DMA((n_copies,)),
        ],
        compiler_params=pltpu.CompilerParams(vmem_limit_bytes=VMEM_LIMIT),
        cost_estimate=pl.CostEstimate(
            flops=6 * span * wide * columns, bytes_accessed=4 * span * (wide + 3 * columns), transcendentals=0
        ),
        name="residual",
    )(pattern, right_side, high, low, *[array for array, _ in pieces])


def dot(left, right):
    return jnp.dot(left, right, precision=lax.Precision.HIGHEST)


def on_device(right_side, diag_inv, lower, factor_pattern, jacobian, jacobian_pattern):
    supers, rows, size = diag_inv.shape
    columns = right_side.shape[1]
    span = supers * size
    nodes = lax.axis_size("node")

    own = jnp.concatenate(
        [diag_inv, lower, jacobian.reshape(supers, rows, 3, size).swapaxes(1, 2).reshape(3 * supers, rows, size)]
    )
    own = own, [(0, block) for block in range(own.shape[0])]
    count = lax.axis_size("rhs")
    relative = count >= 16 and not count & (count - 1)
    if relative:
        arrived, late = gather_panels(own, 2 * supers, right_side, "rhs")
    else:
        arrived, late = gather_whole(own, "rhs"), right_side
    factor = runs_of(arrived, 0, 2 * supers)
    jacobians = runs_of(arrived, 2 * supers, len(own[1]))

    sol, parts, down, up = solve(factor, relative, late, factor_pattern, nodes, supers, size)
    if nodes == 2:
        mail = [lax.ppermute(letter, "node", [(0, 1), (1, 0)]) for letter in (down, up)]
        sol, high, low = finish(sol, parts[0], down, *mail, supers)
    else:
        before = after = jnp.zeros((size, columns), jnp.float32)
        if nodes > 1:
            upwards = [(i, i + 1) for i in range(nodes - 1)]
            downwards = [(i + 1, i) for i in range(nodes - 1)]
            below = above = before
            for _ in range(nodes - 1):
                below = lax.ppermute(
                    down[:, :columns] + dot(down[:, columns : columns + size], below), "node", upwards
                )
            for _ in range(nodes - 1):
                leaving = up[:, :columns] + dot(up[:, columns : columns + size], below)
                above = lax.ppermute(leaving + dot(up[:, columns + size :], above), "node", downwards)
            sol = sol + dot(parts[0], below) + dot(parts[1], above)
            before = lax.ppermute(sol[span - size :], "node", upwards)
            after = lax.ppermute(sol[:size], "node", downwards)
        high, low = split_windows(sol, before, after)
    residual = subtract_product(jacobians, relative, right_side, high, low, jacobian_pattern, supers, size)
    return sol, residual


def solution(mesh):
    in_specs = (
        P("node", "rhs"),
        P("node", "rhs", None),
        P("node", "rhs", None),
        P("node", None, None),
        P("node", "rhs", None),
        P("node", None, None),
    )
    out_specs = (P("node", "rhs"), P("node", "rhs"))
    return jax.shard_map(on_device, mesh=mesh, in_specs=in_specs, out_specs=out_specs, check_vma=False)
```

```python
import functools

import jax
import jax.numpy as jnp
from jax import lax
from jax.experimental import pallas as pl
from jax.experimental.pallas import tpu as pltpu
from jax.sharding import PartitionSpec as P

VMEM = pl.BlockSpec(memory_space=pltpu.VMEM)
SMEM = pl.BlockSpec(memory_space=pltpu.SMEM)
ANY = pl.BlockSpec(memory_space=pl.ANY)
VMEM_LIMIT = 20 * 2**20
PLAIN = (((1,), (0,)), ((), ()))


def split(value):
    high = value.astype(jnp.bfloat16)
    return high, (value - high.astype(jnp.float32)).astype(jnp.bfloat16)


def product(left, right, dims=PLAIN):
    dot = functools.partial(lax.dot_general, dimension_numbers=dims, preferred_element_type=jnp.float32)
    return dot(left[0], right[1]) + dot(left[1], right[0]) + dot(left[0], right[0])


def after(held, *others):
    return lax.optimization_barrier((held[0], [array for array, _ in others]))[0], held[1]


def joined(*parts):
    if len(parts) == 1:
        return parts[0]
    return jnp.concatenate([array for array, _ in parts]), [name for _, names in parts for name in names]


def cut(held, begin, end):
    return held[0][begin:end], held[1][begin:end]


def sent(held, axis, mask):
    array, names = held
    swapped = lax.ppermute(array, axis, [(i, i ^ mask) for i in range(lax.axis_size(axis))])
    return swapped, [(owner ^ mask, block) for owner, block in names]


def around(held, axis):
    return sent(held, axis, 1), sent(held, axis, 2)


def onward(pair, size, more, axis):
    half = size // 2
    second = joined(*more, cut(pair[1], half, size))
    first = joined(*more, cut(pair[0], 0, half))
    return second, first


def send_both(parts, axis):
    return sent(parts[0], axis, 1), sent(parts[1], axis, 2)


def gather_panels(factor, jacobian, right_side, axis):
    steps = lax.axis_size(axis) // 4
    masks = []
    while steps > 1:
        masks.append(4 * (steps - 1))
        steps //= 2
    own = joined(factor, jacobian)
    factor_blocks = len(factor[1])

    factor_line = [factor, sent(factor, axis, masks[0])]
    jacobian_line = [jacobian, sent(after(jacobian, factor_line[1]), axis, masks[0])]
    own_round = around(own, axis)
    second_round = send_both(onward(own_round, len(own[1]), factor_line[1:], axis), axis)
    for mask in masks[1:]:
        factor_line.append(sent(joined(*factor_line), axis, mask))
    rest = joined(*factor_line[2:])
    second_last = [after(part, rest) for part in second_round]
    third_round = send_both(onward(second_last, factor_blocks, [rest], axis), axis)
    for mask in masks[1:]:
        jacobian_line.append(sent(joined(*jacobian_line), axis, mask))
    early = joined(*jacobian_line[1:-1])
    early_round = around(early, axis)
    factor_parts = onward(third_round, len(rest[1]), [], axis)
    factor_across = send_both(factor_parts, axis)
    early_last = [after(part, *factor_parts) for part in early_round]
    late_parts = onward(early_last, len(early[1]), jacobian_line[-1:], axis)
    late_round = send_both(late_parts, axis)
    late_across = send_both(onward(late_round, len(jacobian_line[-1][1]), [], axis), axis)
    right_side, _ = after((right_side, None), *late_parts)
    arrived = [own, *factor_line[1:], *jacobian_line[1:], *own_round, *second_round, *third_round, *factor_across]
    return arrived + [*early_round, *late_round, *late_across], right_side


def gather_whole(own, axis):
    everything = lax.all_gather(own[0], axis, tiled=True)
    return [(everything, [(owner, block) for owner in range(lax.axis_size(axis)) for _, block in own[1]])]


def runs_of(pieces, begin, end):
    chosen = []
    for array, names in pieces:
        runs = []
        for at, (owner, block) in enumerate(names):
            if not begin <= block < end:
                continue
            if runs and runs[-1][0] + runs[-1][1] == at and names[at - 1] == (owner, block - 1):
                runs[-1][1] += 1
            else:
                runs.append([at, 1, owner, block - begin])
        if runs:
            chosen.append((array, runs))
    return chosen


def place_rows(pieces, refs, relative, axis, panels, sem):
    me = lax.axis_index(axis)
    copies = []
    for (array, runs), ref in zip(pieces, refs):
        rows = array.shape[1]
        for at, length, owner, block in runs:
            row = pl.multiple_of((me ^ owner) * rows, rows) if relative else owner * rows
            copies.append(
                pltpu.make_async_copy(
                    ref.at[pl.ds(at, length)],
                    panels.at[pl.ds(block, length), pl.ds(row, rows), :],
                    sem.at[len(copies)],
                )
            )
    for copy in copies:
        copy.start()
    return copies


def shapes(arrays):
    return [jax.ShapeDtypeStruct(shape, jnp.float32) for shape in arrays]


def masked(rows, pattern_ref, s, block_rows):
    wide = rows.shape[1]
    blocks = wide // pattern_ref.shape[2]
    together = max(1, 128 // blocks)
    lane = lax.broadcasted_iota(jnp.int32, (1, together * blocks), 1)
    bands = []
    for a in range(pattern_ref.shape[1]):
        weights = []
        for first in range(0, pattern_ref.shape[2], together):
            chosen = pattern_ref[s, a, first]
            weight = jnp.full(lane.shape, chosen.astype(jnp.float32))
            for c in range(1, min(together, pattern_ref.shape[2] - first)):
                weight = jnp.where(lane >= c * blocks, pattern_ref[s, a, first + c].astype(jnp.float32), weight)
            weights.append(weight)
        weights = jnp.concatenate(weights, axis=1)[:, :wide]
        bands.append(rows[a * block_rows : (a + 1) * block_rows] * weights)
    return jnp.concatenate(bands, axis=0)


def solve(pieces, relative, right_side, pattern, nodes, supers, size):
    columns = right_side.shape[1]
    extra = 0 if nodes == 1 else 1 if nodes == 2 else 2
    width = columns + extra * size
    n = len(pieces)
    n_copies = sum(len(runs) for _, runs in pieces)

    def kernel(*refs):
        pattern_ref, rhs_ref = refs[:2]
        piece_refs = refs[2 : 2 + n]
        sol_ref = refs[2 + n]
        extra_refs = refs[3 + n : 3 + n + extra]
        down_ref, up_ref, panels, forward, sem = refs[3 + n + extra :]
        copies = place_rows(pieces, piece_refs, relative, "rhs", panels, sem)
        index = lax.axis_index("node")
        below = jnp.where(index > 0, 1.0, 0.0)
        above = jnp.where(index < nodes - 1, 1.0, 0.0)
        on_diagonal = lax.broadcasted_iota(jnp.int32, (size, size), 0) == lax.broadcasted_iota(
            jnp.int32, (size, size), 1
        )
        zeros = jnp.zeros((size, size), jnp.float32)
        for copy in copies:
            copy.wait()

        previous = None
        for s in range(supers):
            own = rhs_ref[s * size : (s + 1) * size, :]
            low = masked(panels[supers + s], pattern_ref, s, size // pattern_ref.shape[1])
            panels[supers + s] = low
            if s == 0:
                parts = [own]
                if extra:
                    parts.append(low * -below)
                if extra == 2:
                    parts.append(zeros)
                target = jnp.concatenate(parts, axis=1)
            else:
                target = jnp.concatenate([own] + [zeros] * extra, axis=1) - product(split(low), split(previous))
            previous = product(split(panels[s]), split(target))
            forward[s] = previous

        entering = None
        for s in reversed(range(supers)):
            target = forward[s]
            if s == supers - 1:
                if extra:
                    unit = jnp.where(on_diagonal, above, 0.0)
                    shift = [jnp.zeros((size, columns), jnp.float32)] + [zeros] * (extra - 1) + [unit]
                    target = target - jnp.concatenate(shift, axis=1)
            else:
                target = target - entering
            solved = product(split(panels[s].T), split(target))
            sol_ref[s * size : (s + 1) * size, :] = solved[:, :columns]
            for e, ref in enumerate(extra_refs):
                ref[s * size : (s + 1) * size, :] = solved[:, columns + e * size : columns + (e + 1) * size]
            if s > 0 or nodes > 1:
                entering = product(split(panels[supers + s].T), split(solved))

        if nodes == 2:
            upper = index == 1
            span = supers * size
            down_ref[0] = jnp.where(upper, entering[:, :columns], forward[supers - 1, :, :columns])
            down_ref[1] = entering[:, columns:]
            up_ref[0] = jnp.where(upper, sol_ref[:size, :], sol_ref[span - size :, :])
            up_ref[1] = jnp.where(upper, extra_refs[0][:size, :], extra_refs[0][span - size :, :])
        else:
            down_ref[...] = forward[supers - 1]
            up_ref[...] = entering if nodes > 1 else forward[0]

    span = supers * size
    leaving = (2, size, columns) if nodes == 2 else (size, width)
    out = pl.pallas_call(
        kernel,
        out_shape=shapes([(span, columns)] + [(span, size)] * extra + [leaving] * 2),
        in_specs=[SMEM, VMEM] + [ANY] * n,
        out_specs=[VMEM] * (3 + extra),
        scratch_shapes=[
            pltpu.VMEM((2 * supers, size, size), jnp.float32),
            pltpu.VMEM((supers, size, width), jnp.float32),
            pltpu.SemaphoreType.DMA((n_copies,)),
        ],
        compiler_params=pltpu.CompilerParams(vmem_limit_bytes=VMEM_LIMIT),
        cost_estimate=pl.CostEstimate(
            flops=16 * supers * size * size * width, bytes_accessed=span * size, transcendentals=0
        ),
        name="solve",
    )(pattern, right_side, *[array for array, _ in pieces])
    return out[0], out[1 : 1 + extra], out[1 + extra], out[2 + extra]


def finish(sol, part, own_mail, mail, beside_mail, supers):
    span, columns = sol.shape
    size = span // supers

    def kernel(sol_ref, part_ref, own_ref, mail_ref, beside_ref, out_ref, high_ref, low_ref):
        lower_one = lax.axis_index("node") == 0
        down = jnp.where(lower_one, own_ref[0], mail_ref[0])
        offset = jnp.where(lower_one, mail_ref[0], own_ref[0])
        matrix = jnp.where(lower_one, mail_ref[1], own_ref[1])
        up = offset + product(split(matrix), split(down))
        mine = split(jnp.where(lower_one, up, down))
        other = split(jnp.where(lower_one, down, up))

        def window(at, value):
            high_ref[at : at + size, :], low_ref[at : at + size, :] = split(value)

        for at in range(0, span, size):
            value = sol_ref[at : at + size, :] + product(split(part_ref[at : at + size, :]), mine)
            out_ref[at : at + size, :] = value
            window(at + size, value)
        beside = beside_ref[0] + product(split(beside_ref[1]), other)
        window(0, jnp.where(lower_one, 0.0, beside))
        window(size + span, jnp.where(lower_one, beside, 0.0))

    windows = jax.ShapeDtypeStruct((span + 2 * size, columns), jnp.bfloat16)
    return pl.pallas_call(
        kernel,
        out_shape=shapes([(span, columns)]) + [windows, windows],
        in_specs=[VMEM] * 5,
        out_specs=[VMEM] * 3,
        compiler_params=pltpu.CompilerParams(vmem_limit_bytes=VMEM_LIMIT),
        cost_estimate=pl.CostEstimate(
            flops=(span + 2 * size) * size * columns, bytes_accessed=span * columns, transcendentals=0
        ),
        name="finish",
    )(sol, part, own_mail, mail, beside_mail)


def split_windows(sol, before, after):
    span, columns = sol.shape
    size = before.shape[0]

    def kernel(sol_ref, before_ref, after_ref, high_ref, low_ref):
        for at, value in ((0, before_ref[...]), (size, sol_ref[...]), (size + span, after_ref[...])):
            high, low = split(value)
            high_ref[at : at + value.shape[0], :], low_ref[at : at + value.shape[0], :] = high, low

    windows = jax.ShapeDtypeStruct((span + 2 * size, columns), jnp.bfloat16)
    return pl.pallas_call(kernel, out_shape=[windows, windows], name="windows")(sol, before, after)


def subtract_product(pieces, relative, right_side, high, low, pattern, supers, size):
    span, columns = right_side.shape
    wide = 3 * size
    n = len(pieces)
    n_copies = sum(len(runs) for _, runs in pieces)

    def kernel(*refs):
        pattern_ref, rhs_ref, high_ref, low_ref = refs[:4]
        piece_refs = refs[4 : 4 + n]
        out_ref, panels, sem = refs[4 + n :]
        for copy in place_rows(pieces, piece_refs, relative, "rhs", panels, sem):
            copy.wait()
        for s in range(supers):
            rows = jnp.concatenate([panels[3 * s + c] for c in range(3)], axis=1)
            panel = masked(rows, pattern_ref, s, size // pattern_ref.shape[1])
            window = pl.ds(s * size, wide)
            out_ref[s * size : (s + 1) * size, :] = rhs_ref[s * size : (s + 1) * size, :] - product(
                split(panel), (high_ref[window, :], low_ref[window, :])
            )

    return pl.pallas_call(
        kernel,
        out_shape=shapes([(span, columns)])[0],
        in_specs=[SMEM] + [VMEM] * 3 + [ANY] * n,
        out_specs=VMEM,
        scratch_shapes=[
            pltpu.VMEM((3 * supers, size, size), jnp.float32),
            pltpu.SemaphoreType.DMA((n_copies,)),
        ],
        compiler_params=pltpu.CompilerParams(vmem_limit_bytes=VMEM_LIMIT),
        cost_estimate=pl.CostEstimate(
            flops=6 * span * wide * columns, bytes_accessed=4 * span * (wide + 3 * columns), transcendentals=0
        ),
        name="residual",
    )(pattern, right_side, high, low, *[array for array, _ in pieces])


def dot(left, right):
    return jnp.dot(left, right, precision=lax.Precision.HIGHEST)


def on_device(right_side, diag_inv, lower, factor_pattern, jacobian, jacobian_pattern):
    supers, rows, size = diag_inv.shape
    columns = right_side.shape[1]
    span = supers * size
    nodes = lax.axis_size("node")

    def blocks_of(array, begin):
        return array, [(0, begin + block) for block in range(array.shape[0])]

    factor_own = blocks_of(jnp.concatenate([diag_inv, lower]), 0)
    shaped = jacobian.reshape(supers, rows, 3, size).swapaxes(1, 2).reshape(3 * supers, rows, size)
    jacobian_own = blocks_of(shaped, 2 * supers)
    own = joined(factor_own, jacobian_own)
    count = lax.axis_size("rhs")
    relative = count >= 16 and not count & (count - 1)
    if relative:
        arrived, late = gather_panels(factor_own, jacobian_own, right_side, "rhs")
    else:
        arrived, late = gather_whole(own, "rhs"), right_side
    factor = runs_of(arrived, 0, 2 * supers)
    jacobians = runs_of(arrived, 2 * supers, len(own[1]))

    sol, parts, down, up = solve(factor, relative, late, factor_pattern, nodes, supers, size)
    if nodes == 2:
        mail = [lax.ppermute(letter, "node", [(0, 1), (1, 0)]) for letter in (down, up)]
        sol, high, low = finish(sol, parts[0], down, *mail, supers)
    else:
        beneath = beyond = jnp.zeros((size, columns), jnp.float32)
        if nodes > 1:
            upwards = [(i, i + 1) for i in range(nodes - 1)]
            downwards = [(i + 1, i) for i in range(nodes - 1)]
            below = above = beneath
            for _ in range(nodes - 1):
                below = lax.ppermute(
                    down[:, :columns] + dot(down[:, columns : columns + size], below), "node", upwards
                )
            for _ in range(nodes - 1):
                leaving = up[:, :columns] + dot(up[:, columns : columns + size], below)
                above = lax.ppermute(leaving + dot(up[:, columns + size :], above), "node", downwards)
            sol = sol + dot(parts[0], below) + dot(parts[1], above)
            beneath = lax.ppermute(sol[span - size :], "node", upwards)
            beyond = lax.ppermute(sol[:size], "node", downwards)
        high, low = split_windows(sol, beneath, beyond)
    residual = subtract_product(jacobians, relative, right_side, high, low, jacobian_pattern, supers, size)
    return sol, residual


def solution(mesh):
    in_specs = (
        P("node", "rhs"),
        P("node", "rhs", None),
        P("node", "rhs", None),
        P("node", None, None),
        P("node", "rhs", None),
        P("node", None, None),
    )
    out_specs = (P("node", "rhs"), P("node", "rhs"))
    return jax.shard_map(on_device, mesh=mesh, in_specs=in_specs, out_specs=out_specs, check_vma=False)
```

```python
import functools

import jax
import jax.numpy as jnp
from jax import lax
from jax.experimental import pallas as pl
from jax.experimental.pallas import tpu as pltpu
from jax.sharding import PartitionSpec as P

VMEM = pl.BlockSpec(memory_space=pltpu.VMEM)
SMEM = pl.BlockSpec(memory_space=pltpu.SMEM)
ANY = pl.BlockSpec(memory_space=pl.ANY)
VMEM_LIMIT = 20 * 2**20
PLAIN = (((1,), (0,)), ((), ()))


def split(value):
    high = value.astype(jnp.bfloat16)
    return high, (value - high.astype(jnp.float32)).astype(jnp.bfloat16)


def product(left, right, dims=PLAIN):
    dot = functools.partial(lax.dot_general, dimension_numbers=dims, preferred_element_type=jnp.float32)
    return dot(left[0], right[1]) + dot(left[1], right[0]) + dot(left[0], right[0])


def after(held, *others):
    return lax.optimization_barrier((held[0], [array for array, _ in others]))[0], held[1]


def joined(*parts):
    if len(parts) == 1:
        return parts[0]
    return jnp.concatenate([array for array, _ in parts]), [name for _, names in parts for name in names]


def cut(held, begin, end):
    return held[0][begin:end], held[1][begin:end]


def sent(held, axis, mask):
    array, names = held
    swapped = lax.ppermute(array, axis, [(i, i ^ mask) for i in range(lax.axis_size(axis))])
    return swapped, [(owner ^ mask, block) for owner, block in names]


def around(held, axis):
    return sent(held, axis, 1), sent(held, axis, 2)


def onward(pair, size, more, axis):
    half = size // 2
    second = joined(*more, cut(pair[1], half, size))
    first = joined(*more, cut(pair[0], 0, half))
    return second, first


def send_both(parts, axis):
    return sent(parts[0], axis, 1), sent(parts[1], axis, 2)


def gather_panels(factor, jacobian, right_side, axis):
    steps = lax.axis_size(axis) // 4
    masks = []
    while steps > 1:
        masks.append(4 * (steps - 1))
        steps //= 2
    own = joined(factor, jacobian)
    factor_blocks = len(factor[1])

    factor_line = [factor, sent(factor, axis, masks[0])]
    jacobian_line = [jacobian, sent(after(jacobian, factor_line[1]), axis, masks[0])]
    own_round = around(own, axis)
    second_round = send_both(onward(own_round, len(own[1]), factor_line[1:], axis), axis)
    for mask in masks[1:]:
        factor_line.append(sent(joined(*factor_line), axis, mask))
    rest = joined(*factor_line[2:])
    second_last = [after(part, rest) for part in second_round]
    third_round = send_both(onward(second_last, factor_blocks, [rest], axis), axis)
    for mask in masks[1:]:
        jacobian_line.append(sent(joined(*jacobian_line), axis, mask))
    early = joined(*jacobian_line[1:-1])
    early_round = around(early, axis)
    factor_parts = onward(third_round, len(rest[1]), [], axis)
    factor_across = send_both(factor_parts, axis)
    early_last = [after(part, *factor_parts) for part in early_round]
    late_parts = onward(early_last, len(early[1]), jacobian_line[-1:], axis)
    late_round = send_both(late_parts, axis)
    late_across = send_both(onward(late_round, len(jacobian_line[-1][1]), [], axis), axis)
    right_side, _ = after((right_side, None), *late_parts)
    arrived = [own, *factor_line[1:], *jacobian_line[1:], *own_round, *second_round, *third_round, *factor_across]
    return arrived + [*early_round, *late_round], list(late_across), right_side


def gather_whole(own, axis):
    everything = lax.all_gather(own[0], axis, tiled=True)
    return [(everything, [(owner, block) for owner in range(lax.axis_size(axis)) for _, block in own[1]])]


def runs_of(pieces, begin, end, group):
    chosen = []
    for array, names in pieces:
        runs = []
        for at, (owner, block) in enumerate(names):
            if not begin <= block < end:
                continue
            follows = runs and runs[-1][0] + runs[-1][1] == at and names[at - 1] == (owner, block - 1)
            if follows and (block - begin) % group:
                runs[-1][1] += 1
            else:
                runs.append([at, 1, owner, block - begin])
        if runs:
            chosen.append((array, runs))
    return chosen


def place_rows(pieces, refs, relative, axis, panels, sem):
    me = lax.axis_index(axis)
    placed = []
    for (array, runs), ref in zip(pieces, refs):
        rows = array.shape[1]
        for at, length, owner, block in runs:
            row = pl.multiple_of((me ^ owner) * rows, rows) if relative else owner * rows
            source = ref.at[pl.ds(at, length)]
            placed.append((block, source, panels.at[pl.ds(block, length), pl.ds(row, rows), :]))
    placed.sort(key=lambda item: item[0])
    copies = []
    for block, source, target in placed:
        copies.append((block, pltpu.make_async_copy(source, target, sem.at[len(copies)])))
        copies[-1][1].start()
    return copies


def shapes(arrays):
    return [jax.ShapeDtypeStruct(shape, jnp.float32) for shape in arrays]


def weights_of(pattern_ref, s, a, wide):
    count = pattern_ref.shape[2]
    step = wide // count
    together = max(1, 128 // step)
    lane = lax.broadcasted_iota(jnp.int32, (1, together * step), 1)
    weights = []
    for first in range(0, count, together):
        weight = jnp.full(lane.shape, pattern_ref[s, a, first].astype(jnp.float32))
        for c in range(1, min(together, count - first)):
            weight = jnp.where(lane >= c * step, pattern_ref[s, a, first + c].astype(jnp.float32), weight)
        weights.append(weight)
    return jnp.concatenate(weights, axis=1)[:, :wide]


def masked(rows, pattern_ref, s, block_rows):
    return jnp.concatenate(
        [
            rows[a * block_rows : (a + 1) * block_rows] * weights_of(pattern_ref, s, a, rows.shape[1])
            for a in range(pattern_ref.shape[1])
        ],
        axis=0,
    )


def solve(pieces, relative, right_side, pattern, nodes, supers, size):
    columns = right_side.shape[1]
    extra = 0 if nodes == 1 else 1 if nodes == 2 else 2
    width = columns + extra * size
    n = len(pieces)
    n_copies = sum(len(runs) for _, runs in pieces)

    def kernel(*refs):
        pattern_ref, rhs_ref = refs[:2]
        piece_refs = refs[2 : 2 + n]
        sol_ref = refs[2 + n]
        extra_refs = refs[3 + n : 3 + n + extra]
        down_ref, up_ref, panels, forward, sem = refs[3 + n + extra :]
        copies = place_rows(pieces, piece_refs, relative, "rhs", panels, sem)
        index = lax.axis_index("node")
        below = jnp.where(index > 0, 1.0, 0.0)
        above = jnp.where(index < nodes - 1, 1.0, 0.0)
        on_diagonal = lax.broadcasted_iota(jnp.int32, (size, size), 0) == lax.broadcasted_iota(
            jnp.int32, (size, size), 1
        )
        zeros = jnp.zeros((size, size), jnp.float32)
        for _, copy in copies:
            copy.wait()

        previous = None
        for s in range(supers):
            own = rhs_ref[s * size : (s + 1) * size, :]
            low = masked(panels[supers + s], pattern_ref, s, size // pattern_ref.shape[1])
            panels[supers + s] = low
            if s == 0:
                parts = [own]
                if extra:
                    parts.append(low * -below)
                if extra == 2:
                    parts.append(zeros)
                target = jnp.concatenate(parts, axis=1)
            else:
                target = jnp.concatenate([own] + [zeros] * extra, axis=1) - product(split(low), split(previous))
            previous = product(split(panels[s]), split(target))
            forward[s] = previous

        entering = None
        for s in reversed(range(supers)):
            target = forward[s]
            if s == supers - 1:
                if extra:
                    unit = jnp.where(on_diagonal, above, 0.0)
                    shift = [jnp.zeros((size, columns), jnp.float32)] + [zeros] * (extra - 1) + [unit]
                    target = target - jnp.concatenate(shift, axis=1)
            else:
                target = target - entering
            solved = product(split(panels[s].T), split(target))
            sol_ref[s * size : (s + 1) * size, :] = solved[:, :columns]
            for e, ref in enumerate(extra_refs):
                ref[s * size : (s + 1) * size, :] = solved[:, columns + e * size : columns + (e + 1) * size]
            if s > 0 or nodes > 1:
                entering = product(split(panels[supers + s].T), split(solved))

        if nodes == 2:
            upper = index == 1
            span = supers * size
            down_ref[0] = jnp.where(upper, entering[:, :columns], forward[supers - 1, :, :columns])
            down_ref[1] = entering[:, columns:]
            up_ref[0] = jnp.where(upper, sol_ref[:size, :], sol_ref[span - size :, :])
            up_ref[1] = jnp.where(upper, extra_refs[0][:size, :], extra_refs[0][span - size :, :])
        else:
            down_ref[...] = forward[supers - 1]
            up_ref[...] = entering if nodes > 1 else forward[0]

    span = supers * size
    leaving = (2, size, columns) if nodes == 2 else (size, width)
    out = pl.pallas_call(
        kernel,
        out_shape=shapes([(span, columns)] + [(span, size)] * extra + [leaving] * 2),
        in_specs=[SMEM, VMEM] + [ANY] * n,
        out_specs=[VMEM] * (3 + extra),
        scratch_shapes=[
            pltpu.VMEM((2 * supers, size, size), jnp.float32),
            pltpu.VMEM((supers, size, width), jnp.float32),
            pltpu.SemaphoreType.DMA((n_copies,)),
        ],
        compiler_params=pltpu.CompilerParams(vmem_limit_bytes=VMEM_LIMIT),
        cost_estimate=pl.CostEstimate(
            flops=16 * supers * size * size * width, bytes_accessed=span * size, transcendentals=0
        ),
        name="solve",
    )(pattern, right_side, *[array for array, _ in pieces])
    return out[0], out[1 : 1 + extra], out[1 + extra], out[2 + extra]


def finish(sol, part, own_mail, mail, beside_mail, supers):
    span, columns = sol.shape
    size = span // supers

    def kernel(sol_ref, part_ref, own_ref, mail_ref, beside_ref, out_ref, high_ref, low_ref):
        lower_one = lax.axis_index("node") == 0
        down = jnp.where(lower_one, own_ref[0], mail_ref[0])
        offset = jnp.where(lower_one, mail_ref[0], own_ref[0])
        matrix = jnp.where(lower_one, mail_ref[1], own_ref[1])
        up = offset + product(split(matrix), split(down))
        mine = split(jnp.where(lower_one, up, down))
        other = split(jnp.where(lower_one, down, up))

        def window(at, value):
            high_ref[at : at + size, :], low_ref[at : at + size, :] = split(value)

        for at in range(0, span, size):
            value = sol_ref[at : at + size, :] + product(split(part_ref[at : at + size, :]), mine)
            out_ref[at : at + size, :] = value
            window(at + size, value)
        beside = beside_ref[0] + product(split(beside_ref[1]), other)
        window(0, jnp.where(lower_one, 0.0, beside))
        window(size + span, jnp.where(lower_one, beside, 0.0))

    windows = jax.ShapeDtypeStruct((span + 2 * size, columns), jnp.bfloat16)
    return pl.pallas_call(
        kernel,
        out_shape=shapes([(span, columns)]) + [windows, windows],
        in_specs=[VMEM] * 5,
        out_specs=[VMEM] * 3,
        compiler_params=pltpu.CompilerParams(vmem_limit_bytes=VMEM_LIMIT),
        cost_estimate=pl.CostEstimate(
            flops=(span + 2 * size) * size * columns, bytes_accessed=span * columns, transcendentals=0
        ),
        name="finish",
    )(sol, part, own_mail, mail, beside_mail)


def split_windows(sol, before, after):
    span, columns = sol.shape
    size = before.shape[0]

    def kernel(sol_ref, before_ref, after_ref, high_ref, low_ref):
        for at, value in ((0, before_ref[...]), (size, sol_ref[...]), (size + span, after_ref[...])):
            high, low = split(value)
            high_ref[at : at + value.shape[0], :], low_ref[at : at + value.shape[0], :] = high, low

    windows = jax.ShapeDtypeStruct((span + 2 * size, columns), jnp.bfloat16)
    return pl.pallas_call(kernel, out_shape=[windows, windows], name="windows")(sol, before, after)


def subtract_product(pieces, relative, right_side, high, low, pattern, supers, size):
    span, columns = right_side.shape
    wide = 3 * size
    n = len(pieces)
    n_copies = sum(len(runs) for _, runs in pieces)

    def kernel(*refs):
        pattern_ref, rhs_ref, high_ref, low_ref = refs[:4]
        piece_refs = refs[4 : 4 + n]
        out_ref, panels, sem = refs[4 + n :]
        copies = place_rows(pieces, piece_refs, relative, "rhs", panels, sem)
        for s in range(supers):
            for block, copy in copies:
                if block // 3 == s:
                    copy.wait()
            rows = jnp.concatenate([panels[3 * s + c] for c in range(3)], axis=1)
            panel = masked(rows, pattern_ref, s, size // pattern_ref.shape[1])
            window = pl.ds(s * size, wide)
            out_ref[s * size : (s + 1) * size, :] = rhs_ref[s * size : (s + 1) * size, :] - product(
                split(panel), (high_ref[window, :], low_ref[window, :])
            )

    return pl.pallas_call(
        kernel,
        out_shape=shapes([(span, columns)])[0],
        in_specs=[SMEM] + [VMEM] * 3 + [ANY] * n,
        out_specs=VMEM,
        scratch_shapes=[
            pltpu.VMEM((3 * supers, size, size), jnp.float32),
            pltpu.SemaphoreType.DMA((n_copies,)),
        ],
        compiler_params=pltpu.CompilerParams(vmem_limit_bytes=VMEM_LIMIT),
        cost_estimate=pl.CostEstimate(
            flops=6 * span * wide * columns, bytes_accessed=4 * span * (wide + 3 * columns), transcendentals=0
        ),
        name="residual",
    )(pattern, right_side, high, low, *[array for array, _ in pieces])


def subtract_rest(pieces, residual, right_side, high, low, pattern, supers, size):
    span, columns = right_side.shape
    wide = 3 * size
    n = len(pieces)
    places = {}
    for i, (array, runs) in enumerate(pieces):
        for at, length, owner, block in runs:
            for step in range(length):
                places.setdefault(owner, {})[block + step] = (i, at + step)
    rows = pieces[0][0].shape[1]

    def kernel(*refs):
        pattern_ref, rhs_ref, high_ref, low_ref, _ = refs[:5]
        piece_refs = refs[5 : 5 + n]
        out_ref, held, sem = refs[5 + n :]
        me = lax.axis_index("rhs")
        copies = []
        for s in range(supers):
            bands, starts = [], []
            for owner, blocks in places.items():
                row = pl.multiple_of((me ^ owner) * rows, rows)
                band = [piece_refs[i][at] for i, at in (blocks[3 * s + c] for c in range(3))]
                a = row // (size // pattern_ref.shape[1])
                bands.append(jnp.concatenate(band, axis=1) * weights_of(pattern_ref, s, a, wide))
                starts.append(pl.multiple_of(s * size + row, rows))
            window = pl.ds(s * size, wide)
            result = product(split(jnp.concatenate(bands, axis=0)), (high_ref[window, :], low_ref[window, :]))
            for i, start in enumerate(starts):
                at = len(copies)
                held[at] = rhs_ref[pl.ds(start, rows), :] - result[i * rows : (i + 1) * rows]
                copies.append(pltpu.make_async_copy(held.at[at], out_ref.at[pl.ds(start, rows), :], sem.at[at]))
                copies[-1].start()
        for copy in copies:
            copy.wait()

    return pl.pallas_call(
        kernel,
        out_shape=shapes([(span, columns)])[0],
        in_specs=[SMEM] + [VMEM] * 3 + [ANY] + [VMEM] * n,
        out_specs=ANY,
        input_output_aliases={4: 0},
        scratch_shapes=[
            pltpu.VMEM((supers * len(places), rows, columns), jnp.float32),
            pltpu.SemaphoreType.DMA((supers * len(places),)),
        ],
        compiler_params=pltpu.CompilerParams(vmem_limit_bytes=VMEM_LIMIT),
        cost_estimate=pl.CostEstimate(
            flops=6 * supers * rows * len(places) * wide * columns, bytes_accessed=8 * span * size, transcendentals=0
        ),
        name="residual_rest",
    )(pattern, right_side, high, low, residual, *[array for array, _ in pieces])


def dot(left, right):
    return jnp.dot(left, right, precision=lax.Precision.HIGHEST)


def on_device(right_side, diag_inv, lower, factor_pattern, jacobian, jacobian_pattern):
    supers, rows, size = diag_inv.shape
    columns = right_side.shape[1]
    span = supers * size
    nodes = lax.axis_size("node")

    def blocks_of(array, begin):
        return array, [(0, begin + block) for block in range(array.shape[0])]

    factor_own = blocks_of(jnp.concatenate([diag_inv, lower]), 0)
    shaped = jacobian.reshape(supers, rows, 3, size).swapaxes(1, 2).reshape(3 * supers, rows, size)
    jacobian_own = blocks_of(shaped, 2 * supers)
    own = joined(factor_own, jacobian_own)
    count = lax.axis_size("rhs")
    relative = count >= 16 and not count & (count - 1)
    if relative:
        arrived, last, late = gather_panels(factor_own, jacobian_own, right_side, "rhs")
    else:
        arrived, last, late = gather_whole(own, "rhs"), [], right_side
    factor = runs_of(arrived, 0, 2 * supers, 2 * supers)
    jacobians = runs_of(arrived, 2 * supers, len(own[1]), 3)
    last = runs_of(last, 2 * supers, len(own[1]), 3)

    sol, parts, down, up = solve(factor, relative, late, factor_pattern, nodes, supers, size)
    if nodes == 2:
        mail = [lax.ppermute(letter, "node", [(0, 1), (1, 0)]) for letter in (down, up)]
        sol, high, low = finish(sol, parts[0], down, *mail, supers)
    else:
        beneath = beyond = jnp.zeros((size, columns), jnp.float32)
        if nodes > 1:
            upwards = [(i, i + 1) for i in range(nodes - 1)]
            downwards = [(i + 1, i) for i in range(nodes - 1)]
            below = above = beneath
            for _ in range(nodes - 1):
                below = lax.ppermute(
                    down[:, :columns] + dot(down[:, columns : columns + size], below), "node", upwards
                )
            for _ in range(nodes - 1):
                leaving = up[:, :columns] + dot(up[:, columns : columns + size], below)
                above = lax.ppermute(leaving + dot(up[:, columns + size :], above), "node", downwards)
            sol = sol + dot(parts[0], below) + dot(parts[1], above)
            beneath = lax.ppermute(sol[span - size :], "node", upwards)
            beyond = lax.ppermute(sol[:size], "node", downwards)
        high, low = split_windows(sol, beneath, beyond)
    residual = subtract_product(jacobians, relative, right_side, high, low, jacobian_pattern, supers, size)
    if last:
        residual = subtract_rest(last, residual, right_side, high, low, jacobian_pattern, supers, size)
    return sol, residual


def solution(mesh):
    in_specs = (
        P("node", "rhs"),
        P("node", "rhs", None),
        P("node", "rhs", None),
        P("node", None, None),
        P("node", "rhs", None),
        P("node", None, None),
    )
    out_specs = (P("node", "rhs"), P("node", "rhs"))
    return jax.shard_map(on_device, mesh=mesh, in_specs=in_specs, out_specs=out_specs, check_vma=False)
```

```python
import functools

import jax
import jax.numpy as jnp
from jax import lax
from jax.experimental import pallas as pl
from jax.experimental.pallas import tpu as pltpu
from jax.sharding import PartitionSpec as P

VMEM = pl.BlockSpec(memory_space=pltpu.VMEM)
SMEM = pl.BlockSpec(memory_space=pltpu.SMEM)
ANY = pl.BlockSpec(memory_space=pl.ANY)
VMEM_LIMIT = 20 * 2**20
PLAIN = (((1,), (0,)), ((), ()))


def split(value):
    high = value.astype(jnp.bfloat16)
    return high, (value - high.astype(jnp.float32)).astype(jnp.bfloat16)


def product(left, right, dims=PLAIN):
    dot = functools.partial(lax.dot_general, dimension_numbers=dims, preferred_element_type=jnp.float32)
    return dot(left[0], right[1]) + dot(left[1], right[0]) + dot(left[0], right[0])


def after(held, *others):
    return lax.optimization_barrier((held[0], [array for array, _ in others]))[0], held[1]


def joined(*parts):
    if len(parts) == 1:
        return parts[0]
    return jnp.concatenate([array for array, _ in parts]), [name for _, names in parts for name in names]


def cut(held, begin, end):
    return held[0][begin:end], held[1][begin:end]


def sent(held, axis, mask):
    array, names = held
    swapped = lax.ppermute(array, axis, [(i, i ^ mask) for i in range(lax.axis_size(axis))])
    return swapped, [(owner ^ mask, block) for owner, block in names]


def around(held, axis):
    return sent(held, axis, 1), sent(held, axis, 2)


def onward(pair, size, more, axis):
    half = size // 2
    second = joined(*more, cut(pair[1], half, size))
    first = joined(*more, cut(pair[0], 0, half))
    return second, first


def send_both(parts, axis):
    return sent(parts[0], axis, 1), sent(parts[1], axis, 2)


def gather_panels(factor, jacobian, right_side, axis):
    steps = lax.axis_size(axis) // 4
    masks = []
    while steps > 1:
        masks.append(4 * (steps - 1))
        steps //= 2
    own = joined(factor, jacobian)
    factor_blocks = len(factor[1])

    factor_line = [factor, sent(factor, axis, masks[0])]
    jacobian_line = [jacobian, sent(after(jacobian, factor_line[1]), axis, masks[0])]
    own_round = around(own, axis)
    second_round = send_both(onward(own_round, len(own[1]), factor_line[1:], axis), axis)
    for mask in masks[1:]:
        factor_line.append(sent(joined(*factor_line), axis, mask))
    rest = joined(*factor_line[2:])
    second_last = [after(part, rest) for part in second_round]
    third_round = send_both(onward(second_last, factor_blocks, [rest], axis), axis)
    for mask in masks[1:]:
        jacobian_line.append(sent(joined(*jacobian_line), axis, mask))
    early = joined(*jacobian_line[1:-1])
    early_round = around(early, axis)
    factor_parts = onward(third_round, len(rest[1]), [], axis)
    factor_across = send_both(factor_parts, axis)
    early_last = [after(part, *factor_parts) for part in early_round]
    late_parts = onward(early_last, len(early[1]), jacobian_line[-1:], axis)
    late_round = send_both(late_parts, axis)
    late_across = send_both(onward(late_round, len(jacobian_line[-1][1]), [], axis), axis)
    right_side, _ = after((right_side, None), *late_parts)
    arrived = [own, *factor_line[1:], *jacobian_line[1:], *own_round, *second_round, *third_round, *factor_across]
    return arrived + [*early_round, *late_round], list(late_across), right_side


def gather_whole(own, axis):
    everything = lax.all_gather(own[0], axis, tiled=True)
    return [(everything, [(owner, block) for owner in range(lax.axis_size(axis)) for _, block in own[1]])]


def places_of(pieces, begin, end):
    arrays, places = [], {}
    for array, names in pieces:
        if not any(begin <= block < end for _, block in names):
            continue
        for at, (owner, block) in enumerate(names):
            if begin <= block < end:
                places.setdefault(owner, {})[block - begin] = (len(arrays), at)
        arrays.append(array)
    return arrays, places


def row_of(owner, rows, relative):
    return pl.multiple_of((lax.axis_index("rhs") ^ owner) * rows, rows) if relative else owner * rows


def shapes(arrays):
    return [jax.ShapeDtypeStruct(shape, jnp.float32) for shape in arrays]


def weights_of(pattern_ref, s, a, wide):
    count = pattern_ref.shape[2]
    step = wide // count
    together = max(1, 128 // step)
    lane = lax.broadcasted_iota(jnp.int32, (1, together * step), 1)
    weights = []
    for first in range(0, count, together):
        weight = jnp.full(lane.shape, pattern_ref[s, a, first].astype(jnp.float32))
        for c in range(1, min(together, count - first)):
            weight = jnp.where(lane >= c * step, pattern_ref[s, a, first + c].astype(jnp.float32), weight)
        weights.append(weight)
    return jnp.concatenate(weights, axis=1)[:, :wide]


def solve(arrays, places, relative, right_side, pattern, nodes, supers, size):
    columns = right_side.shape[1]
    extra = 0 if nodes == 1 else 1 if nodes == 2 else 2
    width = columns + extra * size
    n = len(arrays)
    rows = arrays[0].shape[1]

    def kernel(*refs):
        pattern_ref, rhs_ref = refs[:2]
        piece_refs = refs[2 : 2 + n]
        sol_ref = refs[2 + n]
        extra_refs = refs[3 + n : 3 + n + extra]
        down_ref, up_ref, panels, forward = refs[3 + n + extra :]
        for owner, blocks in places.items():
            row = row_of(owner, rows, relative)
            for block, (i, at) in blocks.items():
                band = piece_refs[i][at]
                if block >= supers:
                    a = row // (size // pattern_ref.shape[1])
                    band = band * weights_of(pattern_ref, block - supers, a, size)
                panels[block, pl.ds(row, rows), :] = band
        index = lax.axis_index("node")
        below = jnp.where(index > 0, 1.0, 0.0)
        above = jnp.where(index < nodes - 1, 1.0, 0.0)
        on_diagonal = lax.broadcasted_iota(jnp.int32, (size, size), 0) == lax.broadcasted_iota(
            jnp.int32, (size, size), 1
        )
        zeros = jnp.zeros((size, size), jnp.float32)

        previous = None
        for s in range(supers):
            own = rhs_ref[s * size : (s + 1) * size, :]
            low = panels[supers + s]
            if s == 0:
                parts = [own]
                if extra:
                    parts.append(low * -below)
                if extra == 2:
                    parts.append(zeros)
                target = jnp.concatenate(parts, axis=1)
            else:
                target = jnp.concatenate([own] + [zeros] * extra, axis=1) - product(split(low), split(previous))
            previous = product(split(panels[s]), split(target))
            forward[s] = previous

        entering = None
        for s in reversed(range(supers)):
            target = forward[s]
            if s == supers - 1:
                if extra:
                    unit = jnp.where(on_diagonal, above, 0.0)
                    shift = [jnp.zeros((size, columns), jnp.float32)] + [zeros] * (extra - 1) + [unit]
                    target = target - jnp.concatenate(shift, axis=1)
            else:
                target = target - entering
            solved = product(split(panels[s].T), split(target))
            sol_ref[s * size : (s + 1) * size, :] = solved[:, :columns]
            for e, ref in enumerate(extra_refs):
                ref[s * size : (s + 1) * size, :] = solved[:, columns + e * size : columns + (e + 1) * size]
            if s > 0 or nodes > 1:
                entering = product(split(panels[supers + s].T), split(solved))

        if nodes == 2:
            upper = index == 1
            span = supers * size
            down_ref[0] = jnp.where(upper, entering[:, :columns], forward[supers - 1, :, :columns])
            down_ref[1] = entering[:, columns:]
            up_ref[0] = jnp.where(upper, sol_ref[:size, :], sol_ref[span - size :, :])
            up_ref[1] = jnp.where(upper, extra_refs[0][:size, :], extra_refs[0][span - size :, :])
        else:
            down_ref[...] = forward[supers - 1]
            up_ref[...] = entering if nodes > 1 else forward[0]

    span = supers * size
    leaving = (2, size, columns) if nodes == 2 else (size, width)
    out = pl.pallas_call(
        kernel,
        out_shape=shapes([(span, columns)] + [(span, size)] * extra + [leaving] * 2),
        in_specs=[SMEM, VMEM] + [VMEM] * n,
        out_specs=[VMEM] * (3 + extra),
        scratch_shapes=[
            pltpu.VMEM((2 * supers, size, size), jnp.float32),
            pltpu.VMEM((supers, size, width), jnp.float32),
        ],
        compiler_params=pltpu.CompilerParams(vmem_limit_bytes=VMEM_LIMIT),
        cost_estimate=pl.CostEstimate(
            flops=16 * supers * size * size * width, bytes_accessed=span * size, transcendentals=0
        ),
        name="solve",
    )(pattern, right_side, *arrays)
    return out[0], out[1 : 1 + extra], out[1 + extra], out[2 + extra]


def finish(sol, part, own_mail, mail, beside_mail, supers):
    span, columns = sol.shape
    size = span // supers

    def kernel(sol_ref, part_ref, own_ref, mail_ref, beside_ref, out_ref, high_ref, low_ref):
        lower_one = lax.axis_index("node") == 0
        down = jnp.where(lower_one, own_ref[0], mail_ref[0])
        offset = jnp.where(lower_one, mail_ref[0], own_ref[0])
        matrix = jnp.where(lower_one, mail_ref[1], own_ref[1])
        up = offset + product(split(matrix), split(down))
        mine = split(jnp.where(lower_one, up, down))
        other = split(jnp.where(lower_one, down, up))

        def window(at, value):
            high_ref[at : at + size, :], low_ref[at : at + size, :] = split(value)

        for at in range(0, span, size):
            value = sol_ref[at : at + size, :] + product(split(part_ref[at : at + size, :]), mine)
            out_ref[at : at + size, :] = value
            window(at + size, value)
        beside = beside_ref[0] + product(split(beside_ref[1]), other)
        window(0, jnp.where(lower_one, 0.0, beside))
        window(size + span, jnp.where(lower_one, beside, 0.0))

    windows = jax.ShapeDtypeStruct((span + 2 * size, columns), jnp.bfloat16)
    return pl.pallas_call(
        kernel,
        out_shape=shapes([(span, columns)]) + [windows, windows],
        in_specs=[VMEM] * 5,
        out_specs=[VMEM] * 3,
        compiler_params=pltpu.CompilerParams(vmem_limit_bytes=VMEM_LIMIT),
        cost_estimate=pl.CostEstimate(
            flops=(span + 2 * size) * size * columns, bytes_accessed=span * columns, transcendentals=0
        ),
        name="finish",
    )(sol, part, own_mail, mail, beside_mail)


def split_windows(sol, before, after):
    span, columns = sol.shape
    size = before.shape[0]

    def kernel(sol_ref, before_ref, after_ref, high_ref, low_ref):
        for at, value in ((0, before_ref[...]), (size, sol_ref[...]), (size + span, after_ref[...])):
            high, low = split(value)
            high_ref[at : at + value.shape[0], :], low_ref[at : at + value.shape[0], :] = high, low

    windows = jax.ShapeDtypeStruct((span + 2 * size, columns), jnp.bfloat16)
    return pl.pallas_call(kernel, out_shape=[windows, windows], name="windows")(sol, before, after)


def subtract_product(arrays, places, relative, right_side, high, low, pattern, supers, size, base=None):
    span, columns = right_side.shape
    wide = 3 * size
    n = len(arrays)
    rows = arrays[0].shape[1]
    extra = 0 if base is None else 1

    def kernel(*refs):
        pattern_ref, rhs_ref, high_ref, low_ref = refs[:4]
        piece_refs = refs[4 + extra : 4 + extra + n]
        out_ref = refs[4 + extra + n]
        copies = []
        for s in range(supers):
            bands, starts = [], []
            for owner, blocks in places.items():
                row = row_of(owner, rows, relative)
                band = [piece_refs[i][at] for i, at in (blocks[3 * s + c] for c in range(3))]
                a = row // (size // pattern_ref.shape[1])
                bands.append(jnp.concatenate(band, axis=1) * weights_of(pattern_ref, s, a, wide))
                starts.append(s * size + row if not relative else pl.multiple_of(s * size + row, rows))
            window = pl.ds(s * size, wide)
            result = product(split(jnp.concatenate(bands, axis=0)), (high_ref[window, :], low_ref[window, :]))
            for i, start in enumerate(starts):
                value = rhs_ref[pl.ds(start, rows), :] - result[i * rows : (i + 1) * rows]
                if base is None:
                    out_ref[pl.ds(start, rows), :] = value
                else:
                    held, sem = refs[5 + extra + n :]
                    at = len(copies)
                    held[at] = value
                    copies.append(pltpu.make_async_copy(held.at[at], out_ref.at[pl.ds(start, rows), :], sem.at[at]))
                    copies[-1].start()
        for copy in copies:
            copy.wait()

    bands = supers * len(places)
    scratch = [pltpu.VMEM((bands, rows, columns), jnp.float32), pltpu.SemaphoreType.DMA((bands,))]
    return pl.pallas_call(
        kernel,
        out_shape=shapes([(span, columns)])[0],
        in_specs=[SMEM] + [VMEM] * 3 + [ANY] * extra + [VMEM] * n,
        out_specs=ANY if extra else VMEM,
        input_output_aliases={4: 0} if extra else {},
        scratch_shapes=scratch if extra else [],
        compiler_params=pltpu.CompilerParams(vmem_limit_bytes=VMEM_LIMIT),
        cost_estimate=pl.CostEstimate(
            flops=6 * bands * rows * wide * columns, bytes_accessed=8 * bands * rows * wide, transcendentals=0
        ),
        name="residual_rest" if extra else "residual",
    )(pattern, right_side, high, low, *([base] if extra else []), *arrays)


def dot(left, right):
    return jnp.dot(left, right, precision=lax.Precision.HIGHEST)


def on_device(right_side, diag_inv, lower, factor_pattern, jacobian, jacobian_pattern):
    supers, rows, size = diag_inv.shape
    columns = right_side.shape[1]
    span = supers * size
    nodes = lax.axis_size("node")

    def blocks_of(array, begin):
        return array, [(0, begin + block) for block in range(array.shape[0])]

    factor_own = blocks_of(jnp.concatenate([diag_inv, lower]), 0)
    shaped = jacobian.reshape(supers, rows, 3, size).swapaxes(1, 2).reshape(3 * supers, rows, size)
    jacobian_own = blocks_of(shaped, 2 * supers)
    own = joined(factor_own, jacobian_own)
    count = lax.axis_size("rhs")
    relative = count >= 16 and not count & (count - 1)
    if relative:
        arrived, last, late = gather_panels(factor_own, jacobian_own, right_side, "rhs")
    else:
        arrived, last, late = gather_whole(own, "rhs"), [], right_side
    factor = places_of(arrived, 0, 2 * supers)
    jacobians, places = places_of(arrived, 2 * supers, len(own[1]))
    whole = {owner: blocks for owner, blocks in places.items() if len(blocks) == 3 * supers}
    partial = set(places) - set(whole)

    sol, parts, down, up = solve(*factor, relative, late, factor_pattern, nodes, supers, size)
    if nodes == 2:
        mail = [lax.ppermute(letter, "node", [(0, 1), (1, 0)]) for letter in (down, up)]
        sol, high, low = finish(sol, parts[0], down, *mail, supers)
    else:
        beneath = beyond = jnp.zeros((size, columns), jnp.float32)
        if nodes > 1:
            upwards = [(i, i + 1) for i in range(nodes - 1)]
            downwards = [(i + 1, i) for i in range(nodes - 1)]
            below = above = beneath
            for _ in range(nodes - 1):
                below = lax.ppermute(
                    down[:, :columns] + dot(down[:, columns : columns + size], below), "node", upwards
                )
            for _ in range(nodes - 1):
                leaving = up[:, :columns] + dot(up[:, columns : columns + size], below)
                above = lax.ppermute(leaving + dot(up[:, columns + size :], above), "node", downwards)
            sol = sol + dot(parts[0], below) + dot(parts[1], above)
            beneath = lax.ppermute(sol[span - size :], "node", upwards)
            beyond = lax.ppermute(sol[:size], "node", downwards)
        high, low = split_windows(sol, beneath, beyond)
    subtract = functools.partial(
        subtract_product,
        relative=relative,
        right_side=right_side,
        high=high,
        low=low,
        pattern=jacobian_pattern,
        supers=supers,
        size=size,
    )
    residual = subtract(jacobians, whole)
    if last:
        arrays, rest = places_of([*arrived, *last] if partial else last, 2 * supers, len(own[1]))
        rest = {owner: blocks for owner, blocks in rest.items() if owner not in whole}
        residual = subtract(arrays, rest, base=residual)
    return sol, residual


def solution(mesh):
    in_specs = (
        P("node", "rhs"),
        P("node", "rhs", None),
        P("node", "rhs", None),
        P("node", None, None),
        P("node", "rhs", None),
        P("node", None, None),
    )
    out_specs = (P("node", "rhs"), P("node", "rhs"))
    return jax.shard_map(on_device, mesh=mesh, in_specs=in_specs, out_specs=out_specs, check_vma=False)
```

```python
import functools

import jax
import jax.numpy as jnp
from jax import lax
from jax.experimental import pallas as pl
from jax.experimental.pallas import tpu as pltpu
from jax.sharding import PartitionSpec as P

VMEM = pl.BlockSpec(memory_space=pltpu.VMEM)
SMEM = pl.BlockSpec(memory_space=pltpu.SMEM)
ANY = pl.BlockSpec(memory_space=pl.ANY)
VMEM_LIMIT = 20 * 2**20
PLAIN = (((1,), (0,)), ((), ()))


def split(value):
    high = value.astype(jnp.bfloat16)
    return high, (value - high.astype(jnp.float32)).astype(jnp.bfloat16)


def product(left, right, dims=PLAIN):
    dot = functools.partial(lax.dot_general, dimension_numbers=dims, preferred_element_type=jnp.float32)
    return dot(left[0], right[1]) + dot(left[1], right[0]) + dot(left[0], right[0])


def after(held, *others):
    return lax.optimization_barrier((held[0], [array for array, _ in others]))[0], held[1]


def joined(*parts):
    if len(parts) == 1:
        return parts[0]
    return jnp.concatenate([array for array, _ in parts]), [name for _, names in parts for name in names]


def cut(held, begin, end):
    return held[0][begin:end], held[1][begin:end]


def sent(held, axis, mask):
    array, names = held
    swapped = lax.ppermute(array, axis, [(i, i ^ mask) for i in range(lax.axis_size(axis))])
    return swapped, [(owner ^ mask, block) for owner, block in names]


def around(held, axis):
    return sent(held, axis, 1), sent(held, axis, 2)


def onward(pair, size, more, axis):
    half = size // 2
    second = joined(*more, cut(pair[1], half, size))
    first = joined(*more, cut(pair[0], 0, half))
    return second, first


def send_both(parts, axis):
    return sent(parts[0], axis, 1), sent(parts[1], axis, 2)


def line_of(held, axis):
    line, step = [held], lax.axis_size(axis) // 4
    while step > 1:
        line += [sent(part, axis, 4 * (step - 1)) for part in line]
        step //= 2
    return line


def gather_panels(factor, jacobian, right_side, axis):
    own = joined(factor, jacobian)
    factor_line = line_of(factor, axis)
    own_round = around(own, axis)
    near, far = joined(*factor_line[1:-1]), factor_line[-1]
    second_parts = onward(own_round, len(own[1]), [near], axis)
    second_round = send_both(second_parts, axis)
    third_parts = onward(second_round, len(near[1]), [far], axis)
    third_round = send_both(third_parts, axis)
    factor_parts = onward(third_round, len(far[1]), [], axis)
    factor_across = send_both(factor_parts, axis)

    jacobian_line = [after(jacobian, *second_parts)]
    while len(jacobian_line) < len(factor_line).bit_length():
        passed = joined(*jacobian_line)
        jacobian_line.append(sent(passed, axis, factor_line[len(passed[1]) // len(jacobian[1])][1][0][0]))
    near, far = joined(*jacobian_line[1:-1]), jacobian_line[-1]
    near_round = around(near, axis)
    near_last = [after(part, *factor_parts) for part in near_round]
    far_parts = onward(near_last, len(near[1]), [far], axis)
    far_round = send_both(far_parts, axis)
    far_across = send_both(onward(far_round, len(far[1]), [], axis), axis)
    right_side, _ = after((right_side, None), *far_parts)
    arrived = [own, *factor_line[1:], *jacobian_line[1:], *own_round, *second_round, *third_round, *factor_across]
    return arrived + [*near_round, *far_round], list(far_across), right_side


def gather_whole(own, axis):
    everything = lax.all_gather(own[0], axis, tiled=True)
    return [(everything, [(owner, block) for owner in range(lax.axis_size(axis)) for _, block in own[1]])]


def places_of(pieces, begin, end):
    arrays, places = [], {}
    for array, names in pieces:
        if not any(begin <= block < end for _, block in names):
            continue
        for at, (owner, block) in enumerate(names):
            if begin <= block < end:
                places.setdefault(owner, {})[block - begin] = (len(arrays), at)
        arrays.append(array)
    return arrays, places


def row_of(owner, rows, relative):
    return pl.multiple_of((lax.axis_index("rhs") ^ owner) * rows, rows) if relative else owner * rows


def shapes(arrays):
    return [jax.ShapeDtypeStruct(shape, jnp.float32) for shape in arrays]


def weights_of(pattern_ref, s, a, wide):
    count = pattern_ref.shape[2]
    step = wide // count
    together = max(1, 128 // step)
    lane = lax.broadcasted_iota(jnp.int32, (1, together * step), 1)
    weights = []
    for first in range(0, count, together):
        weight = jnp.full(lane.shape, pattern_ref[s, a, first].astype(jnp.float32))
        for c in range(1, min(together, count - first)):
            weight = jnp.where(lane >= c * step, pattern_ref[s, a, first + c].astype(jnp.float32), weight)
        weights.append(weight)
    return jnp.concatenate(weights, axis=1)[:, :wide]


def solve(arrays, places, relative, right_side, pattern, nodes, supers, size):
    columns = right_side.shape[1]
    extra = 0 if nodes == 1 else 1 if nodes == 2 else 2
    width = columns + extra * size
    n = len(arrays)
    rows = arrays[0].shape[1]

    def kernel(*refs):
        pattern_ref, rhs_ref = refs[:2]
        piece_refs = refs[2 : 2 + n]
        sol_ref = refs[2 + n]
        extra_refs = refs[3 + n : 3 + n + extra]
        down_ref, up_ref, panels, forward = refs[3 + n + extra :]
        for owner, blocks in places.items():
            row = row_of(owner, rows, relative)
            for block, (i, at) in blocks.items():
                band = piece_refs[i][at]
                if block >= supers:
                    a = row // (size // pattern_ref.shape[1])
                    band = band * weights_of(pattern_ref, block - supers, a, size)
                panels[block, pl.ds(row, rows), :] = band
        index = lax.axis_index("node")
        below = jnp.where(index > 0, 1.0, 0.0)
        above = jnp.where(index < nodes - 1, 1.0, 0.0)
        zeros = jnp.zeros((size, size), jnp.float32)

        inverse = [split(panels[s]) for s in range(supers)]
        low = [split(panels[supers + s]) for s in range(supers)]
        down = [product(inverse[s], low[s]) for s in range(supers)]
        previous = None
        for s in range(supers):
            alone = product(inverse[s], split(rhs_ref[s * size : (s + 1) * size, :]))
            if s == 0:
                parts = [alone] + ([down[0] * -below] if extra else []) + [zeros] * (extra - 1)
                previous = jnp.concatenate(parts, axis=1)
            else:
                alone = jnp.concatenate([alone] + [zeros] * extra, axis=1)
                previous = alone - product(split(down[s]), split(previous))
            forward[s] = previous

        solved = None
        for s in reversed(range(supers)):
            turned = panels[s].T
            alone = product(split(turned), split(forward[s]))
            if s < supers - 1:
                up = product(low[s + 1], inverse[s])
                solved = alone - product(split(up.T), split(solved))
            elif extra:
                shift = [jnp.zeros((size, columns), jnp.float32)] + [zeros] * (extra - 1) + [turned * above]
                solved = alone - jnp.concatenate(shift, axis=1)
            else:
                solved = alone
            sol_ref[s * size : (s + 1) * size, :] = solved[:, :columns]
            for e, ref in enumerate(extra_refs):
                ref[s * size : (s + 1) * size, :] = solved[:, columns + e * size : columns + (e + 1) * size]
        entering = product(split(panels[supers].T), split(solved)) if nodes > 1 else None

        if nodes == 2:
            upper = index == 1
            span = supers * size
            down_ref[0] = jnp.where(upper, entering[:, :columns], forward[supers - 1, :, :columns])
            down_ref[1] = entering[:, columns:]
            up_ref[0] = jnp.where(upper, sol_ref[:size, :], sol_ref[span - size :, :])
            up_ref[1] = jnp.where(upper, extra_refs[0][:size, :], extra_refs[0][span - size :, :])
        else:
            down_ref[...] = forward[supers - 1]
            up_ref[...] = entering if nodes > 1 else forward[0]

    span = supers * size
    leaving = (2, size, columns) if nodes == 2 else (size, width)
    out = pl.pallas_call(
        kernel,
        out_shape=shapes([(span, columns)] + [(span, size)] * extra + [leaving] * 2),
        in_specs=[SMEM, VMEM] + [VMEM] * n,
        out_specs=[VMEM] * (3 + extra),
        scratch_shapes=[
            pltpu.VMEM((2 * supers, size, size), jnp.float32),
            pltpu.VMEM((supers, size, width), jnp.float32),
        ],
        compiler_params=pltpu.CompilerParams(vmem_limit_bytes=VMEM_LIMIT),
        cost_estimate=pl.CostEstimate(
            flops=16 * supers * size * size * width, bytes_accessed=span * size, transcendentals=0
        ),
        name="solve",
    )(pattern, right_side, *arrays)
    return out[0], out[1 : 1 + extra], out[1 + extra], out[2 + extra]


def finish(sol, part, own_mail, mail, beside_mail, supers):
    span, columns = sol.shape
    size = span // supers

    def kernel(sol_ref, part_ref, own_ref, mail_ref, beside_ref, out_ref, high_ref, low_ref):
        lower_one = lax.axis_index("node") == 0
        down = jnp.where(lower_one, own_ref[0], mail_ref[0])
        offset = jnp.where(lower_one, mail_ref[0], own_ref[0])
        matrix = jnp.where(lower_one, mail_ref[1], own_ref[1])
        up = offset + product(split(matrix), split(down))
        mine = split(jnp.where(lower_one, up, down))
        other = split(jnp.where(lower_one, down, up))

        def window(at, value):
            high_ref[at : at + size, :], low_ref[at : at + size, :] = split(value)

        for at in range(0, span, size):
            value = sol_ref[at : at + size, :] + product(split(part_ref[at : at + size, :]), mine)
            out_ref[at : at + size, :] = value
            window(at + size, value)
        beside = beside_ref[0] + product(split(beside_ref[1]), other)
        window(0, jnp.where(lower_one, 0.0, beside))
        window(size + span, jnp.where(lower_one, beside, 0.0))

    windows = jax.ShapeDtypeStruct((span + 2 * size, columns), jnp.bfloat16)
    return pl.pallas_call(
        kernel,
        out_shape=shapes([(span, columns)]) + [windows, windows],
        in_specs=[VMEM] * 5,
        out_specs=[VMEM] * 3,
        compiler_params=pltpu.CompilerParams(vmem_limit_bytes=VMEM_LIMIT),
        cost_estimate=pl.CostEstimate(
            flops=(span + 2 * size) * size * columns, bytes_accessed=span * columns, transcendentals=0
        ),
        name="finish",
    )(sol, part, own_mail, mail, beside_mail)


def split_windows(sol, before, after):
    span, columns = sol.shape
    size = before.shape[0]

    def kernel(sol_ref, before_ref, after_ref, high_ref, low_ref):
        for at, value in ((0, before_ref[...]), (size, sol_ref[...]), (size + span, after_ref[...])):
            high, low = split(value)
            high_ref[at : at + value.shape[0], :], low_ref[at : at + value.shape[0], :] = high, low

    windows = jax.ShapeDtypeStruct((span + 2 * size, columns), jnp.bfloat16)
    return pl.pallas_call(kernel, out_shape=[windows, windows], name="windows")(sol, before, after)


def subtract_product(arrays, places, relative, right_side, high, low, pattern, supers, size, base=None):
    span, columns = right_side.shape
    wide = 3 * size
    n = len(arrays)
    rows = arrays[0].shape[1]
    extra = 0 if base is None else 1

    def kernel(*refs):
        pattern_ref, rhs_ref, high_ref, low_ref = refs[:4]
        piece_refs = refs[4 + extra : 4 + extra + n]
        out_ref = refs[4 + extra + n]
        copies = []
        for s in range(supers):
            bands, starts = [], []
            for owner, blocks in places.items():
                row = row_of(owner, rows, relative)
                band = [piece_refs[i][at] for i, at in (blocks[3 * s + c] for c in range(3))]
                a = row // (size // pattern_ref.shape[1])
                bands.append(jnp.concatenate(band, axis=1) * weights_of(pattern_ref, s, a, wide))
                starts.append(s * size + row if not relative else pl.multiple_of(s * size + row, rows))
            window = pl.ds(s * size, wide)
            result = product(split(jnp.concatenate(bands, axis=0)), (high_ref[window, :], low_ref[window, :]))
            for i, start in enumerate(starts):
                value = rhs_ref[pl.ds(start, rows), :] - result[i * rows : (i + 1) * rows]
                if base is None:
                    out_ref[pl.ds(start, rows), :] = value
                else:
                    held, sem = refs[5 + extra + n :]
                    at = len(copies)
                    held[at] = value
                    copies.append(pltpu.make_async_copy(held.at[at], out_ref.at[pl.ds(start, rows), :], sem.at[at]))
                    copies[-1].start()
        for copy in copies:
            copy.wait()

    bands = supers * len(places)
    scratch = [pltpu.VMEM((bands, rows, columns), jnp.float32), pltpu.SemaphoreType.DMA((bands,))]
    return pl.pallas_call(
        kernel,
        out_shape=shapes([(span, columns)])[0],
        in_specs=[SMEM] + [VMEM] * 3 + [ANY] * extra + [VMEM] * n,
        out_specs=ANY if extra else VMEM,
        input_output_aliases={4: 0} if extra else {},
        scratch_shapes=scratch if extra else [],
        compiler_params=pltpu.CompilerParams(vmem_limit_bytes=VMEM_LIMIT),
        cost_estimate=pl.CostEstimate(
            flops=6 * bands * rows * wide * columns, bytes_accessed=8 * bands * rows * wide, transcendentals=0
        ),
        name="residual_rest" if extra else "residual",
    )(pattern, right_side, high, low, *([base] if extra else []), *arrays)


def dot(left, right):
    return jnp.dot(left, right, precision=lax.Precision.HIGHEST)


def on_device(right_side, diag_inv, lower, factor_pattern, jacobian, jacobian_pattern):
    supers, rows, size = diag_inv.shape
    columns = right_side.shape[1]
    span = supers * size
    nodes = lax.axis_size("node")

    def blocks_of(array, begin):
        return array, [(0, begin + block) for block in range(array.shape[0])]

    factor_own = blocks_of(jnp.concatenate([diag_inv, lower]), 0)
    shaped = jacobian.reshape(supers, rows, 3, size).swapaxes(1, 2).reshape(3 * supers, rows, size)
    jacobian_own = blocks_of(shaped, 2 * supers)
    own = joined(factor_own, jacobian_own)
    count = lax.axis_size("rhs")
    relative = count >= 16 and not count & (count - 1)
    if relative:
        arrived, last, late = gather_panels(factor_own, jacobian_own, right_side, "rhs")
    else:
        arrived, last, late = gather_whole(own, "rhs"), [], right_side
    factor = places_of(arrived, 0, 2 * supers)
    jacobians, places = places_of(arrived, 2 * supers, len(own[1]))
    whole = {owner: blocks for owner, blocks in places.items() if len(blocks) == 3 * supers}
    partial = set(places) - set(whole)

    sol, parts, down, up = solve(*factor, relative, late, factor_pattern, nodes, supers, size)
    if nodes == 2:
        mail = [lax.ppermute(letter, "node", [(0, 1), (1, 0)]) for letter in (down, up)]
        sol, high, low = finish(sol, parts[0], down, *mail, supers)
    else:
        beneath = beyond = jnp.zeros((size, columns), jnp.float32)
        if nodes > 1:
            upwards = [(i, i + 1) for i in range(nodes - 1)]
            downwards = [(i + 1, i) for i in range(nodes - 1)]
            below = above = beneath
            for _ in range(nodes - 1):
                below = lax.ppermute(
                    down[:, :columns] + dot(down[:, columns : columns + size], below), "node", upwards
                )
            for _ in range(nodes - 1):
                leaving = up[:, :columns] + dot(up[:, columns : columns + size], below)
                above = lax.ppermute(leaving + dot(up[:, columns + size :], above), "node", downwards)
            sol = sol + dot(parts[0], below) + dot(parts[1], above)
            beneath = lax.ppermute(sol[span - size :], "node", upwards)
            beyond = lax.ppermute(sol[:size], "node", downwards)
        high, low = split_windows(sol, beneath, beyond)
    subtract = functools.partial(
        subtract_product,
        relative=relative,
        right_side=right_side,
        high=high,
        low=low,
        pattern=jacobian_pattern,
        supers=supers,
        size=size,
    )
    residual = subtract(jacobians, whole)
    if last:
        arrays, rest = places_of([*arrived, *last] if partial else last, 2 * supers, len(own[1]))
        rest = {owner: blocks for owner, blocks in rest.items() if owner not in whole}
        residual = subtract(arrays, rest, base=residual)
    return sol, residual


def solution(mesh):
    in_specs = (
        P("node", "rhs"),
        P("node", "rhs", None),
        P("node", "rhs", None),
        P("node", None, None),
        P("node", "rhs", None),
        P("node", None, None),
    )
    out_specs = (P("node", "rhs"), P("node", "rhs"))
    return jax.shard_map(on_device, mesh=mesh, in_specs=in_specs, out_specs=out_specs, check_vma=False)
```

```python
import functools

import jax
import jax.numpy as jnp
from jax import lax
from jax.experimental import pallas as pl
from jax.experimental.pallas import tpu as pltpu
from jax.sharding import PartitionSpec as P

VMEM = pl.BlockSpec(memory_space=pltpu.VMEM)
SMEM = pl.BlockSpec(memory_space=pltpu.SMEM)
ANY = pl.BlockSpec(memory_space=pl.ANY)
VMEM_LIMIT = 20 * 2**20


def split(value):
    high = value.astype(jnp.bfloat16)
    return high, (value - high.astype(jnp.float32)).astype(jnp.bfloat16)


def product(left, right):
    return jnp.dot(
        jnp.concatenate([left[1], left[0], left[0]], axis=1),
        jnp.concatenate([right[0], right[1], right[0]], axis=0),
        preferred_element_type=jnp.float32,
    )


def after(held, *others):
    return lax.optimization_barrier((held[0], [array for array, _ in others]))[0], held[1]


def joined(*parts):
    if len(parts) == 1:
        return parts[0]
    return jnp.concatenate([array for array, _ in parts]), [name for _, names in parts for name in names]


def cut(held, begin, end):
    return held[0][begin:end], held[1][begin:end]


def sent(held, axis, mask):
    array, names = held
    swapped = lax.ppermute(array, axis, [(i, i ^ mask) for i in range(lax.axis_size(axis))])
    return swapped, [(owner ^ mask, block) for owner, block in names]


def around(held, axis):
    return sent(held, axis, 1), sent(held, axis, 2)


def onward(pair, size, more, axis):
    half = size // 2
    second = joined(*more, cut(pair[1], half, size))
    first = joined(*more, cut(pair[0], 0, half))
    return second, first


def send_both(parts, axis):
    return sent(parts[0], axis, 1), sent(parts[1], axis, 2)


def line_of(held, axis):
    line, step = [held], lax.axis_size(axis) // 4
    while step > 1:
        line += [sent(part, axis, 4 * (step - 1)) for part in line]
        step //= 2
    return line


def gather_panels(own, factor, jacobian, right_side, axis):
    factor_line = line_of(factor, axis)
    own_round = around(own, axis)
    near, far = joined(*factor_line[1:-1]), factor_line[-1]
    second_parts = onward(own_round, len(own[1]), [near], axis)
    second_round = send_both(second_parts, axis)
    third_parts = onward(second_round, len(near[1]), [far], axis)
    third_round = send_both(third_parts, axis)
    factor_parts = onward(third_round, len(far[1]), [], axis)
    factor_across = send_both(factor_parts, axis)

    jacobian_line = [after(jacobian, *second_parts)]
    while len(jacobian_line) < len(factor_line).bit_length():
        passed = joined(*jacobian_line)
        jacobian_line.append(sent(passed, axis, factor_line[len(passed[1]) // len(jacobian[1])][1][0][0]))
    near, far = joined(*jacobian_line[1:-1]), jacobian_line[-1]
    near_round = around(near, axis)
    near_last = [after(part, *factor_parts) for part in near_round]
    far_parts = onward(near_last, len(near[1]), [far], axis)
    far_round = send_both(far_parts, axis)
    far_across = send_both(onward(far_round, len(far[1]), [], axis), axis)
    right_side, _ = after((right_side, None), *far_parts)
    arrived = [own, *factor_line[1:], *jacobian_line[1:], *own_round, *second_round, *third_round, *factor_across]
    return arrived + [*near_round, *far_round], list(far_across), right_side


def pack(diag_inv, lower, jacobian):
    supers, rows, size = diag_inv.shape

    def kernel(diag_ref, lower_ref, jacobian_ref, factor_ref, blocks_ref, own_ref):
        for s in range(supers):
            factor_ref[s] = own_ref[s] = diag_ref[s]
            factor_ref[supers + s] = own_ref[supers + s] = lower_ref[s]
            for c in range(3):
                block = jacobian_ref[s, :, c * size : (c + 1) * size]
                blocks_ref[3 * s + c] = own_ref[2 * supers + 3 * s + c] = block

    return pl.pallas_call(
        kernel,
        out_shape=shapes([(count * supers, rows, size) for count in (2, 3, 5)]),
        in_specs=[VMEM] * 3,
        out_specs=[VMEM] * 3,
        name="pack",
    )(diag_inv, lower, jacobian)


def gather_whole(own, axis):
    everything = lax.all_gather(own[0], axis, tiled=True)
    return [(everything, [(owner, block) for owner in range(lax.axis_size(axis)) for _, block in own[1]])]


def places_of(pieces, begin, end):
    arrays, places = [], {}
    for array, names in pieces:
        if not any(begin <= block < end for _, block in names):
            continue
        for at, (owner, block) in enumerate(names):
            if begin <= block < end:
                places.setdefault(owner, {})[block - begin] = (len(arrays), at)
        arrays.append(array)
    return arrays, places


def row_of(owner, rows, relative):
    return pl.multiple_of((lax.axis_index("rhs") ^ owner) * rows, rows) if relative else owner * rows


def shapes(arrays):
    return [jax.ShapeDtypeStruct(shape, jnp.float32) for shape in arrays]


def weights_of(pattern_ref, s, a, wide):
    count = pattern_ref.shape[2]
    step = wide // count
    together = max(1, 128 // step)
    lane = lax.broadcasted_iota(jnp.int32, (1, together * step), 1)
    weights = []
    for first in range(0, count, together):
        weight = jnp.full(lane.shape, pattern_ref[s, a, first].astype(jnp.float32))
        for c in range(1, min(together, count - first)):
            weight = jnp.where(lane >= c * step, pattern_ref[s, a, first + c].astype(jnp.float32), weight)
        weights.append(weight)
    return jnp.concatenate(weights, axis=1)[:, :wide]


def solve(arrays, places, relative, right_side, pattern, nodes, supers, size):
    columns = right_side.shape[1]
    extra = 0 if nodes == 1 else 1 if nodes == 2 else 2
    width = columns + extra * size
    n = len(arrays)
    rows = arrays[0].shape[1]

    def kernel(*refs):
        pattern_ref, rhs_ref = refs[:2]
        piece_refs = refs[2 : 2 + n]
        sol_ref = refs[2 + n]
        extra_refs = refs[3 + n : 3 + n + extra]
        down_ref, up_ref, panels, forward = refs[3 + n + extra :]
        for owner, blocks in places.items():
            row = row_of(owner, rows, relative)
            for block, (i, at) in blocks.items():
                band = piece_refs[i][at]
                if block >= supers:
                    a = row // (size // pattern_ref.shape[1])
                    band = band * weights_of(pattern_ref, block - supers, a, size)
                panels[block, pl.ds(row, rows), :] = band
        index = lax.axis_index("node")
        below = jnp.where(index > 0, 1.0, 0.0)
        above = jnp.where(index < nodes - 1, 1.0, 0.0)
        zeros = jnp.zeros((size, size), jnp.float32)

        inverse = [split(panels[s]) for s in range(supers)]
        low = [split(panels[supers + s]) for s in range(supers)]
        down = [product(inverse[s], low[s]) for s in range(supers)]
        previous = None
        for s in range(supers):
            alone = product(inverse[s], split(rhs_ref[s * size : (s + 1) * size, :]))
            if s == 0:
                parts = [alone] + ([down[0] * -below] if extra else []) + [zeros] * (extra - 1)
                previous = jnp.concatenate(parts, axis=1)
            else:
                alone = jnp.concatenate([alone] + [zeros] * extra, axis=1)
                previous = alone - product(split(down[s]), split(previous))
            forward[s] = previous

        solved = None
        for s in reversed(range(supers)):
            turned = panels[s].T
            alone = product(split(turned), split(forward[s]))
            if s < supers - 1:
                up = product(low[s + 1], inverse[s])
                solved = alone - product(split(up.T), split(solved))
            elif extra:
                shift = [jnp.zeros((size, columns), jnp.float32)] + [zeros] * (extra - 1) + [turned * above]
                solved = alone - jnp.concatenate(shift, axis=1)
            else:
                solved = alone
            sol_ref[s * size : (s + 1) * size, :] = solved[:, :columns]
            for e, ref in enumerate(extra_refs):
                ref[s * size : (s + 1) * size, :] = solved[:, columns + e * size : columns + (e + 1) * size]
        entering = product(split(panels[supers].T), split(solved)) if nodes > 1 else None

        if nodes == 2:
            upper = index == 1
            span = supers * size
            down_ref[0] = jnp.where(upper, entering[:, :columns], forward[supers - 1, :, :columns])
            down_ref[1] = entering[:, columns:]
            up_ref[0] = jnp.where(upper, sol_ref[:size, :], sol_ref[span - size :, :])
            up_ref[1] = jnp.where(upper, extra_refs[0][:size, :], extra_refs[0][span - size :, :])
        else:
            down_ref[...] = forward[supers - 1]
            up_ref[...] = entering if nodes > 1 else forward[0]

    span = supers * size
    leaving = (2, size, columns) if nodes == 2 else (size, width)
    out = pl.pallas_call(
        kernel,
        out_shape=shapes([(span, columns)] + [(span, size)] * extra + [leaving] * 2),
        in_specs=[SMEM, VMEM] + [VMEM] * n,
        out_specs=[VMEM] * (3 + extra),
        scratch_shapes=[
            pltpu.VMEM((2 * supers, size, size), jnp.float32),
            pltpu.VMEM((supers, size, width), jnp.float32),
        ],
        compiler_params=pltpu.CompilerParams(vmem_limit_bytes=VMEM_LIMIT),
        cost_estimate=pl.CostEstimate(
            flops=16 * supers * size * size * width, bytes_accessed=span * size, transcendentals=0
        ),
        name="solve",
    )(pattern, right_side, *arrays)
    return out[0], out[1 : 1 + extra], out[1 + extra], out[2 + extra]


def finish(sol, part, own_mail, mail, beside_mail, supers):
    span, columns = sol.shape
    size = span // supers

    def kernel(sol_ref, part_ref, own_ref, mail_ref, beside_ref, out_ref, high_ref, low_ref):
        lower_one = lax.axis_index("node") == 0
        down = jnp.where(lower_one, own_ref[0], mail_ref[0])
        offset = jnp.where(lower_one, mail_ref[0], own_ref[0])
        matrix = jnp.where(lower_one, mail_ref[1], own_ref[1])
        up = offset + product(split(matrix), split(down))
        mine = split(jnp.where(lower_one, up, down))
        other = split(jnp.where(lower_one, down, up))

        def window(at, value):
            high_ref[at : at + size, :], low_ref[at : at + size, :] = split(value)

        for at in range(0, span, size):
            value = sol_ref[at : at + size, :] + product(split(part_ref[at : at + size, :]), mine)
            out_ref[at : at + size, :] = value
            window(at + size, value)
        beside = beside_ref[0] + product(split(beside_ref[1]), other)
        window(0, jnp.where(lower_one, 0.0, beside))
        window(size + span, jnp.where(lower_one, beside, 0.0))

    windows = jax.ShapeDtypeStruct((span + 2 * size, columns), jnp.bfloat16)
    return pl.pallas_call(
        kernel,
        out_shape=shapes([(span, columns)]) + [windows, windows],
        in_specs=[VMEM] * 5,
        out_specs=[VMEM] * 3,
        compiler_params=pltpu.CompilerParams(vmem_limit_bytes=VMEM_LIMIT),
        cost_estimate=pl.CostEstimate(
            flops=(span + 2 * size) * size * columns, bytes_accessed=span * columns, transcendentals=0
        ),
        name="finish",
    )(sol, part, own_mail, mail, beside_mail)


def split_windows(sol, before, after):
    span, columns = sol.shape
    size = before.shape[0]

    def kernel(sol_ref, before_ref, after_ref, high_ref, low_ref):
        for at, value in ((0, before_ref[...]), (size, sol_ref[...]), (size + span, after_ref[...])):
            high, low = split(value)
            high_ref[at : at + value.shape[0], :], low_ref[at : at + value.shape[0], :] = high, low

    windows = jax.ShapeDtypeStruct((span + 2 * size, columns), jnp.bfloat16)
    return pl.pallas_call(kernel, out_shape=[windows, windows], name="windows")(sol, before, after)


def subtract_product(arrays, places, relative, right_side, high, low, pattern, supers, size, base=None):
    span, columns = right_side.shape
    wide = 3 * size
    n = len(arrays)
    rows = arrays[0].shape[1]
    extra = 0 if base is None else 1

    def kernel(*refs):
        pattern_ref, rhs_ref, high_ref, low_ref = refs[:4]
        piece_refs = refs[4 + extra : 4 + extra + n]
        out_ref = refs[4 + extra + n]
        copies = []
        for s in range(supers):
            bands, starts = [], []
            for owner, blocks in places.items():
                row = row_of(owner, rows, relative)
                band = [piece_refs[i][at] for i, at in (blocks[3 * s + c] for c in range(3))]
                a = row // (size // pattern_ref.shape[1])
                bands.append(jnp.concatenate(band, axis=1) * weights_of(pattern_ref, s, a, wide))
                starts.append(s * size + row if not relative else pl.multiple_of(s * size + row, rows))
            window = pl.ds(s * size, wide)
            result = product(split(jnp.concatenate(bands, axis=0)), (high_ref[window, :], low_ref[window, :]))
            for i, start in enumerate(starts):
                value = rhs_ref[pl.ds(start, rows), :] - result[i * rows : (i + 1) * rows]
                if base is None:
                    out_ref[pl.ds(start, rows), :] = value
                else:
                    held, sem = refs[5 + extra + n :]
                    at = len(copies)
                    held[at] = value
                    copies.append(pltpu.make_async_copy(held.at[at], out_ref.at[pl.ds(start, rows), :], sem.at[at]))
                    copies[-1].start()
        for copy in copies:
            copy.wait()

    bands = supers * len(places)
    scratch = [pltpu.VMEM((bands, rows, columns), jnp.float32), pltpu.SemaphoreType.DMA((bands,))]
    return pl.pallas_call(
        kernel,
        out_shape=shapes([(span, columns)])[0],
        in_specs=[SMEM] + [VMEM] * 3 + [ANY] * extra + [VMEM] * n,
        out_specs=ANY if extra else VMEM,
        input_output_aliases={4: 0} if extra else {},
        scratch_shapes=scratch if extra else [],
        compiler_params=pltpu.CompilerParams(vmem_limit_bytes=VMEM_LIMIT),
        cost_estimate=pl.CostEstimate(
            flops=6 * bands * rows * wide * columns, bytes_accessed=8 * bands * rows * wide, transcendentals=0
        ),
        name="residual_rest" if extra else "residual",
    )(pattern, right_side, high, low, *([base] if extra else []), *arrays)


def dot(left, right):
    return jnp.dot(left, right, precision=lax.Precision.HIGHEST)


def on_device(right_side, diag_inv, lower, factor_pattern, jacobian, jacobian_pattern):
    supers, rows, size = diag_inv.shape
    columns = right_side.shape[1]
    span = supers * size
    nodes = lax.axis_size("node")

    def blocks_of(array, begin):
        return array, [(0, begin + block) for block in range(array.shape[0])]

    factor_own, jacobian_own, own = pack(diag_inv, lower, jacobian)
    factor_own = blocks_of(factor_own, 0)
    jacobian_own = blocks_of(jacobian_own, 2 * supers)
    own = blocks_of(own, 0)
    count = lax.axis_size("rhs")
    relative = count >= 16 and not count & (count - 1)
    if relative:
        arrived, last, late = gather_panels(own, factor_own, jacobian_own, right_side, "rhs")
    else:
        arrived, last, late = gather_whole(own, "rhs"), [], right_side
    factor = places_of(arrived, 0, 2 * supers)
    jacobians, places = places_of(arrived, 2 * supers, len(own[1]))
    whole = {owner: blocks for owner, blocks in places.items() if len(blocks) == 3 * supers}
    partial = set(places) - set(whole)

    sol, parts, down, up = solve(*factor, relative, late, factor_pattern, nodes, supers, size)
    if nodes == 2:
        mail = [lax.ppermute(letter, "node", [(0, 1), (1, 0)]) for letter in (down, up)]
        sol, high, low = finish(sol, parts[0], down, *mail, supers)
    else:
        beneath = beyond = jnp.zeros((size, columns), jnp.float32)
        if nodes > 1:
            upwards = [(i, i + 1) for i in range(nodes - 1)]
            downwards = [(i + 1, i) for i in range(nodes - 1)]
            below = above = beneath
            for _ in range(nodes - 1):
                below = lax.ppermute(
                    down[:, :columns] + dot(down[:, columns : columns + size], below), "node", upwards
                )
            for _ in range(nodes - 1):
                leaving = up[:, :columns] + dot(up[:, columns : columns + size], below)
                above = lax.ppermute(leaving + dot(up[:, columns + size :], above), "node", downwards)
            sol = sol + dot(parts[0], below) + dot(parts[1], above)
            beneath = lax.ppermute(sol[span - size :], "node", upwards)
            beyond = lax.ppermute(sol[:size], "node", downwards)
        high, low = split_windows(sol, beneath, beyond)
    subtract = functools.partial(
        subtract_product,
        relative=relative,
        right_side=right_side,
        high=high,
        low=low,
        pattern=jacobian_pattern,
        supers=supers,
        size=size,
    )
    residual = subtract(jacobians, whole)
    if last:
        arrays, rest = places_of([*arrived, *last] if partial else last, 2 * supers, len(own[1]))
        rest = {owner: blocks for owner, blocks in rest.items() if owner not in whole}
        residual = subtract(arrays, rest, base=residual)
    return sol, residual


def solution(mesh):
    in_specs = (
        P("node", "rhs"),
        P("node", "rhs", None),
        P("node", "rhs", None),
        P("node", None, None),
        P("node", "rhs", None),
        P("node", None, None),
    )
    out_specs = (P("node", "rhs"), P("node", "rhs"))
    return jax.shard_map(on_device, mesh=mesh, in_specs=in_specs, out_specs=out_specs, check_vma=False)
```

```python
import functools

import jax
import jax.numpy as jnp
from jax import lax
from jax.experimental import pallas as pl
from jax.experimental.pallas import tpu as pltpu
from jax.sharding import PartitionSpec as P

VMEM = pl.BlockSpec(memory_space=pltpu.VMEM)
SMEM = pl.BlockSpec(memory_space=pltpu.SMEM)
ANY = pl.BlockSpec(memory_space=pl.ANY)
VMEM_LIMIT = 20 * 2**20
SMALL_LIMIT = 4 * 2**20


def split(value):
    high = value.astype(jnp.bfloat16)
    return high, (value - high.astype(jnp.float32)).astype(jnp.bfloat16)


def product(left, right):
    return jnp.dot(
        jnp.concatenate([left[1], left[0], left[0]], axis=1),
        jnp.concatenate([right[0], right[1], right[0]], axis=0),
        preferred_element_type=jnp.float32,
    )


def after(held, *others):
    return lax.optimization_barrier((held[0], [array for array, _ in others]))[0], held[1]


def joined(*parts):
    if len(parts) == 1:
        return parts[0]
    return jnp.concatenate([array for array, _ in parts]), [name for _, names in parts for name in names]


def cut(held, begin, end):
    return held[0][begin:end], held[1][begin:end]


def sent(held, axis, mask):
    array, names = held
    swapped = lax.ppermute(array, axis, [(i, i ^ mask) for i in range(lax.axis_size(axis))])
    return swapped, [(owner ^ mask, block) for owner, block in names]


def around(held, axis):
    return sent(held, axis, 1), sent(held, axis, 2)


def onward(pair, size, more, axis):
    half = size // 2
    second = joined(*more, cut(pair[1], half, size))
    first = joined(*more, cut(pair[0], 0, half))
    return second, first


def send_both(parts, axis):
    return sent(parts[0], axis, 1), sent(parts[1], axis, 2)


def line_of(held, axis):
    line, step = [held], lax.axis_size(axis) // 4
    while step > 1:
        line += [sent(part, axis, 4 * (step - 1)) for part in line]
        step //= 2
    return line


def gather_panels(own, factor, jacobian, right_side, axis):
    factor_line = line_of(factor, axis)
    own_round = around(own, axis)
    near, far = joined(*factor_line[1:-1]), factor_line[-1]
    second_parts = onward(own_round, len(own[1]), [near], axis)
    second_round = send_both(second_parts, axis)
    third_parts = onward(second_round, len(near[1]), [far], axis)
    third_round = send_both(third_parts, axis)
    factor_parts = onward(third_round, len(far[1]), [], axis)
    factor_across = send_both(factor_parts, axis)

    jacobian_line = [after(jacobian, *second_parts)]
    while len(jacobian_line) < len(factor_line).bit_length():
        passed = joined(*jacobian_line)
        jacobian_line.append(sent(passed, axis, factor_line[len(passed[1]) // len(jacobian[1])][1][0][0]))
    near, far = joined(*jacobian_line[1:-1]), jacobian_line[-1]
    near_round = around(near, axis)
    near_last = [after(part, *factor_parts) for part in near_round]
    far_parts = onward(near_last, len(near[1]), [far], axis)
    far_round = send_both(far_parts, axis)
    far_across = send_both(onward(far_round, len(far[1]), [], axis), axis)
    right_side, _ = after((right_side, None), *far_parts)
    arrived = [own, *factor_line[1:], *jacobian_line[1:], *own_round, *second_round, *third_round, *factor_across]
    return arrived + [*near_round, *far_round], list(far_across), right_side


def pack(diag_inv, lower, jacobian):
    supers, rows, size = diag_inv.shape

    def kernel(diag_ref, lower_ref, jacobian_ref, factor_ref, blocks_ref, own_ref):
        for s in range(supers):
            factor_ref[s] = own_ref[s] = diag_ref[s]
            factor_ref[supers + s] = own_ref[supers + s] = lower_ref[s]
            for c in range(3):
                block = jacobian_ref[s, :, c * size : (c + 1) * size]
                blocks_ref[3 * s + c] = own_ref[2 * supers + 3 * s + c] = block

    return pl.pallas_call(
        kernel,
        out_shape=shapes([(count * supers, rows, size) for count in (2, 3, 5)]),
        in_specs=[VMEM] * 3,
        out_specs=[VMEM] * 3,
        compiler_params=pltpu.CompilerParams(vmem_limit_bytes=SMALL_LIMIT),
        name="pack",
    )(diag_inv, lower, jacobian)


def gather_whole(own, axis):
    everything = lax.all_gather(own[0], axis, tiled=True)
    return [(everything, [(owner, block) for owner in range(lax.axis_size(axis)) for _, block in own[1]])]


def places_of(pieces, begin, end):
    arrays, places = [], {}
    for array, names in pieces:
        if not any(begin <= block < end for _, block in names):
            continue
        for at, (owner, block) in enumerate(names):
            if begin <= block < end:
                places.setdefault(owner, {})[block - begin] = (len(arrays), at)
        arrays.append(array)
    return arrays, places


def row_of(owner, rows, relative):
    return pl.multiple_of((lax.axis_index("rhs") ^ owner) * rows, rows) if relative else owner * rows


def shapes(arrays):
    return [jax.ShapeDtypeStruct(shape, jnp.float32) for shape in arrays]


def widened(pattern, wide):
    supers, bands, count = pattern.shape
    step = wide // count
    together = max(1, 128 // step)

    def kernel(pattern_ref, out_ref):
        lane = lax.broadcasted_iota(jnp.int32, (1, together * step), 1)
        for s in range(supers):
            for a in range(bands):
                for first in range(0, count, together):
                    weight = jnp.full(lane.shape, pattern_ref[s, a, first].astype(jnp.float32))
                    for c in range(1, min(together, count - first)):
                        weight = jnp.where(lane >= c * step, pattern_ref[s, a, first + c].astype(jnp.float32), weight)
                    end = min(first + together, count) * step
                    row = s * bands + a
                    out_ref[row : row + 1, first * step : end] = weight[:, : end - first * step]

    return pl.pallas_call(
        kernel,
        out_shape=shapes([(supers * bands, wide)])[0],
        in_specs=[SMEM],
        out_specs=VMEM,
        compiler_params=pltpu.CompilerParams(vmem_limit_bytes=SMALL_LIMIT),
        name="widened",
    )(pattern)


def weights_of(weights_ref, s, row, supers, size):
    bands = weights_ref.shape[0] // supers
    return weights_ref[pl.ds(s * bands + row // (size // bands), 1), :]


def solve(arrays, places, relative, right_side, weights, nodes, supers, size):
    columns = right_side.shape[1]
    extra = 0 if nodes == 1 else 1 if nodes == 2 else 2
    width = columns + extra * size
    n = len(arrays)
    rows = arrays[0].shape[1]

    def kernel(*refs):
        weights_ref, rhs_ref = refs[:2]
        piece_refs = refs[2 : 2 + n]
        sol_ref = refs[2 + n]
        extra_refs = refs[3 + n : 3 + n + extra]
        down_ref, up_ref, panels, forward = refs[3 + n + extra :]
        for owner, blocks in places.items():
            row = row_of(owner, rows, relative)
            for block, (i, at) in blocks.items():
                band = piece_refs[i][at]
                if block >= supers:
                    band = band * weights_of(weights_ref, block - supers, row, supers, size)
                panels[block, pl.ds(row, rows), :] = band
        index = lax.axis_index("node")
        below = jnp.where(index > 0, 1.0, 0.0)
        above = jnp.where(index < nodes - 1, 1.0, 0.0)
        zeros = jnp.zeros((size, size), jnp.float32)

        inverse = [split(panels[s]) for s in range(supers)]
        low = [split(panels[supers + s]) for s in range(supers)]
        down = [product(inverse[s], low[s]) for s in range(supers)]
        previous = None
        for s in range(supers):
            alone = product(inverse[s], split(rhs_ref[s * size : (s + 1) * size, :]))
            if s == 0:
                parts = [alone] + ([down[0] * -below] if extra else []) + [zeros] * (extra - 1)
                previous = jnp.concatenate(parts, axis=1)
            else:
                alone = jnp.concatenate([alone] + [zeros] * extra, axis=1)
                previous = alone - product(split(down[s]), split(previous))
            forward[s] = previous

        solved = None
        for s in reversed(range(supers)):
            turned = panels[s].T
            alone = product(split(turned), split(forward[s]))
            if s < supers - 1:
                up = product(low[s + 1], inverse[s])
                solved = alone - product(split(up.T), split(solved))
            elif extra:
                shift = [jnp.zeros((size, columns), jnp.float32)] + [zeros] * (extra - 1) + [turned * above]
                solved = alone - jnp.concatenate(shift, axis=1)
            else:
                solved = alone
            sol_ref[s * size : (s + 1) * size, :] = solved[:, :columns]
            for e, ref in enumerate(extra_refs):
                ref[s * size : (s + 1) * size, :] = solved[:, columns + e * size : columns + (e + 1) * size]
        entering = product(split(panels[supers].T), split(solved)) if nodes > 1 else None

        if nodes == 2:
            upper = index == 1
            span = supers * size
            down_ref[0] = jnp.where(upper, entering[:, :columns], forward[supers - 1, :, :columns])
            down_ref[1] = entering[:, columns:]
            up_ref[0] = jnp.where(upper, sol_ref[:size, :], sol_ref[span - size :, :])
            up_ref[1] = jnp.where(upper, extra_refs[0][:size, :], extra_refs[0][span - size :, :])
        else:
            down_ref[...] = forward[supers - 1]
            up_ref[...] = entering if nodes > 1 else forward[0]

    span = supers * size
    leaving = (2, size, columns) if nodes == 2 else (size, width)
    out = pl.pallas_call(
        kernel,
        out_shape=shapes([(span, columns)] + [(span, size)] * extra + [leaving] * 2),
        in_specs=[VMEM] * (2 + n),
        out_specs=[VMEM] * (3 + extra),
        scratch_shapes=[
            pltpu.VMEM((2 * supers, size, size), jnp.float32),
            pltpu.VMEM((supers, size, width), jnp.float32),
        ],
        compiler_params=pltpu.CompilerParams(vmem_limit_bytes=VMEM_LIMIT),
        cost_estimate=pl.CostEstimate(
            flops=16 * supers * size * size * width, bytes_accessed=span * size, transcendentals=0
        ),
        name="solve",
    )(weights, right_side, *arrays)
    return out[0], out[1 : 1 + extra], out[1 + extra], out[2 + extra]


def finish(sol, part, own_mail, mail, beside_mail, supers):
    span, columns = sol.shape
    size = span // supers

    def kernel(sol_ref, part_ref, own_ref, mail_ref, beside_ref, out_ref, high_ref, low_ref, held, sem):
        lower_one = lax.axis_index("node") == 0
        down = jnp.where(lower_one, own_ref[0], mail_ref[0])
        offset = jnp.where(lower_one, mail_ref[0], own_ref[0])
        matrix = jnp.where(lower_one, mail_ref[1], own_ref[1])
        up = offset + product(split(matrix), split(down))
        mine = split(jnp.where(lower_one, up, down))
        other = split(jnp.where(lower_one, down, up))

        def window(at, value):
            high_ref[at : at + size, :], low_ref[at : at + size, :] = split(value)

        copies = []
        for at in range(0, span, size):
            value = sol_ref[at : at + size, :] + product(split(part_ref[at : at + size, :]), mine)
            held[at : at + size, :] = value
            copies.append(
                pltpu.make_async_copy(held.at[at : at + size, :], out_ref.at[at : at + size, :], sem.at[at // size])
            )
            copies[-1].start()
            window(at + size, value)
        beside = beside_ref[0] + product(split(beside_ref[1]), other)
        window(0, jnp.where(lower_one, 0.0, beside))
        window(size + span, jnp.where(lower_one, beside, 0.0))
        for copy in copies:
            copy.wait()

    windows = jax.ShapeDtypeStruct((span + 2 * size, columns), jnp.bfloat16)
    return pl.pallas_call(
        kernel,
        out_shape=shapes([(span, columns)]) + [windows, windows],
        in_specs=[VMEM] * 5,
        out_specs=[ANY, VMEM, VMEM],
        scratch_shapes=[pltpu.VMEM((span, columns), jnp.float32), pltpu.SemaphoreType.DMA((supers,))],
        compiler_params=pltpu.CompilerParams(vmem_limit_bytes=VMEM_LIMIT),
        cost_estimate=pl.CostEstimate(
            flops=(span + 2 * size) * size * columns, bytes_accessed=span * columns, transcendentals=0
        ),
        name="finish",
    )(sol, part, own_mail, mail, beside_mail)


def split_windows(sol, before, after):
    span, columns = sol.shape
    size = before.shape[0]

    def kernel(sol_ref, before_ref, after_ref, high_ref, low_ref):
        for at, value in ((0, before_ref[...]), (size, sol_ref[...]), (size + span, after_ref[...])):
            high, low = split(value)
            high_ref[at : at + value.shape[0], :], low_ref[at : at + value.shape[0], :] = high, low

    windows = jax.ShapeDtypeStruct((span + 2 * size, columns), jnp.bfloat16)
    return pl.pallas_call(kernel, out_shape=[windows, windows], name="windows")(sol, before, after)


def subtract_product(arrays, places, relative, right_side, high, low, weights, supers, size, base=None):
    span, columns = right_side.shape
    wide = 3 * size
    n = len(arrays)
    rows = arrays[0].shape[1]
    extra = 0 if base is None else 1

    def kernel(*refs):
        weights_ref, rhs_ref, high_ref, low_ref = refs[:4]
        piece_refs = refs[4 + extra : 4 + extra + n]
        out_ref, held, sem = refs[4 + extra + n :]
        copies = []

        def write(source, target):
            copies.append(pltpu.make_async_copy(source, target, sem.at[len(copies)]))
            copies[-1].start()

        for s in range(supers):
            bands, starts = [], []
            for owner, blocks in places.items():
                row = row_of(owner, rows, relative)
                band = [piece_refs[i][at] for i, at in (blocks[3 * s + c] for c in range(3))]
                bands.append(jnp.concatenate(band, axis=1) * weights_of(weights_ref, s, row, supers, size))
                starts.append(s * size + row if not relative else pl.multiple_of(s * size + row, rows))
            window = pl.ds(s * size, wide)
            result = product(split(jnp.concatenate(bands, axis=0)), (high_ref[window, :], low_ref[window, :]))
            for i, start in enumerate(starts):
                at = (s * len(places) + i) * rows if extra else start
                held[pl.ds(at, rows), :] = rhs_ref[pl.ds(start, rows), :] - result[i * rows : (i + 1) * rows]
                if extra:
                    write(held.at[pl.ds(at, rows), :], out_ref.at[pl.ds(start, rows), :])
            if not extra:
                whole = pl.ds(s * size, size)
                write(held.at[whole, :], out_ref.at[whole, :])
        for copy in copies:
            copy.wait()

    bands = supers * len(places)
    return pl.pallas_call(
        kernel,
        out_shape=shapes([(span, columns)])[0],
        in_specs=[VMEM] * 4 + [ANY] * extra + [VMEM] * n,
        out_specs=ANY,
        input_output_aliases={4: 0} if extra else {},
        scratch_shapes=[
            pltpu.VMEM((bands * rows if extra else span, columns), jnp.float32),
            pltpu.SemaphoreType.DMA((bands if extra else supers,)),
        ],
        compiler_params=pltpu.CompilerParams(vmem_limit_bytes=VMEM_LIMIT),
        cost_estimate=pl.CostEstimate(
            flops=6 * bands * rows * wide * columns, bytes_accessed=8 * bands * rows * wide, transcendentals=0
        ),
        name="residual_rest" if extra else "residual",
    )(weights, right_side, high, low, *([base] if extra else []), *arrays)


def dot(left, right):
    return jnp.dot(left, right, precision=lax.Precision.HIGHEST)


def on_device(right_side, diag_inv, lower, factor_pattern, jacobian, jacobian_pattern):
    supers, rows, size = diag_inv.shape
    columns = right_side.shape[1]
    span = supers * size
    nodes = lax.axis_size("node")

    def blocks_of(array, begin):
        return array, [(0, begin + block) for block in range(array.shape[0])]

    factor_own, jacobian_own, own = pack(diag_inv, lower, jacobian)
    factor_own = blocks_of(factor_own, 0)
    jacobian_own = blocks_of(jacobian_own, 2 * supers)
    own = blocks_of(own, 0)
    count = lax.axis_size("rhs")
    relative = count >= 16 and not count & (count - 1)
    if relative:
        arrived, last, late = gather_panels(own, factor_own, jacobian_own, right_side, "rhs")
    else:
        arrived, last, late = gather_whole(own, "rhs"), [], right_side
    factor = places_of(arrived, 0, 2 * supers)
    jacobians, places = places_of(arrived, 2 * supers, len(own[1]))
    whole = {owner: blocks for owner, blocks in places.items() if len(blocks) == 3 * supers}
    partial = set(places) - set(whole)

    sol, parts, down, up = solve(*factor, relative, late, widened(factor_pattern, size), nodes, supers, size)
    if nodes == 2:
        mail = [lax.ppermute(letter, "node", [(0, 1), (1, 0)]) for letter in (down, up)]
        sol, high, low = finish(sol, parts[0], down, *mail, supers)
    else:
        beneath = beyond = jnp.zeros((size, columns), jnp.float32)
        if nodes > 1:
            upwards = [(i, i + 1) for i in range(nodes - 1)]
            downwards = [(i + 1, i) for i in range(nodes - 1)]
            below = above = beneath
            for _ in range(nodes - 1):
                below = lax.ppermute(
                    down[:, :columns] + dot(down[:, columns : columns + size], below), "node", upwards
                )
            for _ in range(nodes - 1):
                leaving = up[:, :columns] + dot(up[:, columns : columns + size], below)
                above = lax.ppermute(leaving + dot(up[:, columns + size :], above), "node", downwards)
            sol = sol + dot(parts[0], below) + dot(parts[1], above)
            beneath = lax.ppermute(sol[span - size :], "node", upwards)
            beyond = lax.ppermute(sol[:size], "node", downwards)
        high, low = split_windows(sol, beneath, beyond)
    subtract = functools.partial(
        subtract_product,
        relative=relative,
        right_side=right_side,
        high=high,
        low=low,
        weights=widened(jacobian_pattern, 3 * size),
        supers=supers,
        size=size,
    )
    residual = subtract(jacobians, whole)
    if last:
        arrays, rest = places_of([*arrived, *last] if partial else last, 2 * supers, len(own[1]))
        rest = {owner: blocks for owner, blocks in rest.items() if owner not in whole}
        residual = subtract(arrays, rest, base=residual)
    return sol, residual


def solution(mesh):
    in_specs = (
        P("node", "rhs"),
        P("node", "rhs", None),
        P("node", "rhs", None),
        P("node", None, None),
        P("node", "rhs", None),
        P("node", None, None),
    )
    out_specs = (P("node", "rhs"), P("node", "rhs"))
    return jax.shard_map(on_device, mesh=mesh, in_specs=in_specs, out_specs=out_specs, check_vma=False)
```

```python
import functools

import jax
import jax.numpy as jnp
from jax import lax
from jax.experimental import pallas as pl
from jax.experimental.pallas import tpu as pltpu
from jax.sharding import PartitionSpec as P

VMEM = pl.BlockSpec(memory_space=pltpu.VMEM)
SMEM = pl.BlockSpec(memory_space=pltpu.SMEM)
ANY = pl.BlockSpec(memory_space=pl.ANY)
VMEM_LIMIT = 20 * 2**20
SMALL_LIMIT = 4 * 2**20


def split(value):
    high = value.astype(jnp.bfloat16)
    return high, (value - high.astype(jnp.float32)).astype(jnp.bfloat16)


def product(left, right):
    return jnp.dot(
        jnp.concatenate([left[1], left[0], left[0]], axis=1),
        jnp.concatenate([right[0], right[1], right[0]], axis=0),
        preferred_element_type=jnp.float32,
    )


def after(held, *others):
    return lax.optimization_barrier((held[0], [array for array, _ in others]))[0], held[1]


def joined(*parts):
    if len(parts) == 1:
        return parts[0]
    return jnp.concatenate([array for array, _ in parts]), [name for _, names in parts for name in names]


def cut(held, begin, end):
    return held[0][begin:end], held[1][begin:end]


def sent(held, axis, mask):
    array, names = held
    swapped = lax.ppermute(array, axis, [(i, i ^ mask) for i in range(lax.axis_size(axis))])
    return swapped, [(owner ^ mask, block) for owner, block in names]


def around(held, axis):
    return sent(held, axis, 1), sent(held, axis, 2)


def onward(pair, size, more, axis):
    half = size // 2
    second = joined(*more, cut(pair[1], half, size))
    first = joined(*more, cut(pair[0], 0, half))
    return second, first


def send_both(parts, axis):
    return sent(parts[0], axis, 1), sent(parts[1], axis, 2)


def line_of(held, axis):
    line, step = [held], lax.axis_size(axis) // 4
    while step > 1:
        line += [sent(part, axis, 4 * (step - 1)) for part in line]
        step //= 2
    return line


def gather_panels(own, factor, jacobian, right_side, axis):
    factor_line = line_of(factor, axis)
    own_round = around(own, axis)
    near, far = joined(*factor_line[1:-1]), factor_line[-1]
    second_parts = onward(own_round, len(own[1]), [near], axis)
    second_round = send_both(second_parts, axis)
    jacobian_line = line_of(after(jacobian, *second_parts), axis)
    half = len(jacobian_line) // 2
    j_near, j_far = joined(*jacobian_line[1:half]), joined(*jacobian_line[half:])
    second_last = [after(part, *jacobian_line[1:-1]) for part in second_round]
    third_parts = onward(second_last, len(near[1]), [far], axis)
    third_round = send_both(third_parts, axis)
    third_last = [after(part, jacobian_line[-1]) for part in third_round]
    factor_parts = onward(third_last, len(far[1]), [], axis)
    factor_across = send_both(factor_parts, axis)

    near, far = j_near, j_far
    near_round = around(near, axis)
    near_last = [after(part, *factor_parts) for part in near_round]
    far_parts = onward(near_last, len(near[1]), [far], axis)
    far_round = send_both(far_parts, axis)
    far_across = send_both(onward(far_round, len(far[1]), [], axis), axis)
    right_side, _ = after((right_side, None), *far_parts)
    arrived = [own, *factor_line[1:], *jacobian_line[1:], *own_round, *second_round, *third_round, *factor_across]
    return arrived + [*near_round, *far_round], list(far_across), right_side


def pack(diag_inv, lower, jacobian):
    supers, rows, size = diag_inv.shape

    def kernel(diag_ref, lower_ref, jacobian_ref, factor_ref, blocks_ref, own_ref):
        for s in range(supers):
            factor_ref[s] = own_ref[s] = diag_ref[s]
            factor_ref[supers + s] = own_ref[supers + s] = lower_ref[s]
            for c in range(3):
                block = jacobian_ref[s, :, c * size : (c + 1) * size]
                blocks_ref[3 * s + c] = own_ref[2 * supers + 3 * s + c] = block

    return pl.pallas_call(
        kernel,
        out_shape=shapes([(count * supers, rows, size) for count in (2, 3, 5)]),
        in_specs=[VMEM] * 3,
        out_specs=[VMEM] * 3,
        name="pack",
    )(diag_inv, lower, jacobian)


def gather_whole(own, axis):
    everything = lax.all_gather(own[0], axis, tiled=True)
    return [(everything, [(owner, block) for owner in range(lax.axis_size(axis)) for _, block in own[1]])]


def places_of(pieces, begin, end):
    arrays, places = [], {}
    for array, names in pieces:
        if not any(begin <= block < end for _, block in names):
            continue
        for at, (owner, block) in enumerate(names):
            if begin <= block < end:
                places.setdefault(owner, {})[block - begin] = (len(arrays), at)
        arrays.append(array)
    return arrays, places


def row_of(owner, rows, relative):
    return pl.multiple_of((lax.axis_index("rhs") ^ owner) * rows, rows) if relative else owner * rows


def shapes(arrays):
    return [jax.ShapeDtypeStruct(shape, jnp.float32) for shape in arrays]


def widened(patterns, wides):
    def widen(pattern_ref, out_ref):
        supers, bands, count = pattern_ref.shape
        step = out_ref.shape[1] // count
        together = max(1, 128 // step)
        lane = lax.broadcasted_iota(jnp.int32, (1, together * step), 1)
        for s in range(supers):
            for a in range(bands):
                for first in range(0, count, together):
                    weight = jnp.full(lane.shape, pattern_ref[s, a, first].astype(jnp.float32))
                    for c in range(1, min(together, count - first)):
                        weight = jnp.where(lane >= c * step, pattern_ref[s, a, first + c].astype(jnp.float32), weight)
                    end = min(first + together, count) * step
                    row = s * bands + a
                    out_ref[row : row + 1, first * step : end] = weight[:, : end - first * step]

    def kernel(*refs):
        for pattern_ref, out_ref in zip(refs[: len(patterns)], refs[len(patterns) :]):
            widen(pattern_ref, out_ref)

    return pl.pallas_call(
        kernel,
        out_shape=shapes([(p.shape[0] * p.shape[1], wide) for p, wide in zip(patterns, wides)]),
        in_specs=[SMEM] * len(patterns),
        out_specs=[VMEM] * len(patterns),
        compiler_params=pltpu.CompilerParams(vmem_limit_bytes=SMALL_LIMIT),
        name="widened",
    )(*patterns)


def weights_of(weights_ref, s, row, supers, size):
    bands = weights_ref.shape[0] // supers
    return weights_ref[pl.ds(s * bands + row // (size // bands), 1), :]


def solve(arrays, places, relative, right_side, weights, nodes, supers, size):
    columns = right_side.shape[1]
    extra = 0 if nodes == 1 else 1 if nodes == 2 else 2
    width = columns + extra * size
    n = len(arrays)
    rows = arrays[0].shape[1]

    def kernel(*refs):
        weights_ref, rhs_ref = refs[:2]
        piece_refs = refs[2 : 2 + n]
        sol_ref = refs[2 + n]
        extra_refs = refs[3 + n : 3 + n + extra]
        down_ref, up_ref, panels, forward = refs[3 + n + extra :]
        for owner, blocks in places.items():
            row = row_of(owner, rows, relative)
            for block, (i, at) in blocks.items():
                band = piece_refs[i][at]
                if block >= supers:
                    band = band * weights_of(weights_ref, block - supers, row, supers, size)
                panels[block, pl.ds(row, rows), :] = band
        index = lax.axis_index("node")
        below = jnp.where(index > 0, 1.0, 0.0)
        above = jnp.where(index < nodes - 1, 1.0, 0.0)
        zeros = jnp.zeros((size, size), jnp.float32)

        inverse = [split(panels[s]) for s in range(supers)]
        low = [split(panels[supers + s]) for s in range(supers)]
        down = [product(inverse[s], low[s]) for s in range(supers)]
        previous = None
        for s in range(supers):
            alone = product(inverse[s], split(rhs_ref[s * size : (s + 1) * size, :]))
            if s == 0:
                parts = [alone] + ([down[0] * -below] if extra else []) + [zeros] * (extra - 1)
                previous = jnp.concatenate(parts, axis=1)
            else:
                alone = jnp.concatenate([alone] + [zeros] * extra, axis=1)
                previous = alone - product(split(down[s]), split(previous))
            forward[s] = previous

        solved = None
        for s in reversed(range(supers)):
            turned = panels[s].T
            alone = product(split(turned), split(forward[s]))
            if s < supers - 1:
                up = product(low[s + 1], inverse[s])
                solved = alone - product(split(up.T), split(solved))
            elif extra:
                shift = [jnp.zeros((size, columns), jnp.float32)] + [zeros] * (extra - 1) + [turned * above]
                solved = alone - jnp.concatenate(shift, axis=1)
            else:
                solved = alone
            sol_ref[s * size : (s + 1) * size, :] = solved[:, :columns]
            for e, ref in enumerate(extra_refs):
                ref[s * size : (s + 1) * size, :] = solved[:, columns + e * size : columns + (e + 1) * size]
        entering = product(split(panels[supers].T), split(solved)) if nodes > 1 else None

        if nodes == 2:
            upper = index == 1
            span = supers * size
            down_ref[0] = jnp.where(upper, entering[:, :columns], forward[supers - 1, :, :columns])
            down_ref[1] = entering[:, columns:]
            up_ref[0] = jnp.where(upper, sol_ref[:size, :], sol_ref[span - size :, :])
            up_ref[1] = jnp.where(upper, extra_refs[0][:size, :], extra_refs[0][span - size :, :])
        else:
            down_ref[...] = forward[supers - 1]
            up_ref[...] = entering if nodes > 1 else forward[0]

    span = supers * size
    leaving = (2, size, columns) if nodes == 2 else (size, width)
    out = pl.pallas_call(
        kernel,
        out_shape=shapes([(span, columns)] + [(span, size)] * extra + [leaving] * 2),
        in_specs=[VMEM] * (2 + n),
        out_specs=[VMEM] * (3 + extra),
        scratch_shapes=[
            pltpu.VMEM((2 * supers, size, size), jnp.float32),
            pltpu.VMEM((supers, size, width), jnp.float32),
        ],
        compiler_params=pltpu.CompilerParams(vmem_limit_bytes=VMEM_LIMIT),
        cost_estimate=pl.CostEstimate(
            flops=16 * supers * size * size * width, bytes_accessed=span * size, transcendentals=0
        ),
        name="solve",
    )(weights, right_side, *arrays)
    return out[0], out[1 : 1 + extra], out[1 + extra], out[2 + extra]


def finish(sol, part, own_mail, mail, beside_mail, supers):
    span, columns = sol.shape
    size = span // supers

    def kernel(sol_ref, part_ref, own_ref, mail_ref, beside_ref, out_ref, high_ref, low_ref, held, sem):
        lower_one = lax.axis_index("node") == 0
        down = jnp.where(lower_one, own_ref[0], mail_ref[0])
        offset = jnp.where(lower_one, mail_ref[0], own_ref[0])
        matrix = jnp.where(lower_one, mail_ref[1], own_ref[1])
        up = offset + product(split(matrix), split(down))
        mine = split(jnp.where(lower_one, up, down))
        other = split(jnp.where(lower_one, down, up))

        def window(at, value):
            high_ref[at : at + size, :], low_ref[at : at + size, :] = split(value)

        copies = []
        for at in range(0, span, size):
            value = sol_ref[at : at + size, :] + product(split(part_ref[at : at + size, :]), mine)
            held[at : at + size, :] = value
            copies.append(
                pltpu.make_async_copy(held.at[at : at + size, :], out_ref.at[at : at + size, :], sem.at[at // size])
            )
            copies[-1].start()
            window(at + size, value)
        beside = beside_ref[0] + product(split(beside_ref[1]), other)
        window(0, jnp.where(lower_one, 0.0, beside))
        window(size + span, jnp.where(lower_one, beside, 0.0))
        for copy in copies:
            copy.wait()

    windows = jax.ShapeDtypeStruct((span + 2 * size, columns), jnp.bfloat16)
    return pl.pallas_call(
        kernel,
        out_shape=shapes([(span, columns)]) + [windows, windows],
        in_specs=[VMEM] * 5,
        out_specs=[ANY, VMEM, VMEM],
        scratch_shapes=[pltpu.VMEM((span, columns), jnp.float32), pltpu.SemaphoreType.DMA((supers,))],
        compiler_params=pltpu.CompilerParams(vmem_limit_bytes=VMEM_LIMIT),
        cost_estimate=pl.CostEstimate(
            flops=(span + 2 * size) * size * columns, bytes_accessed=span * columns, transcendentals=0
        ),
        name="finish",
    )(sol, part, own_mail, mail, beside_mail)


def split_windows(sol, before, after):
    span, columns = sol.shape
    size = before.shape[0]

    def kernel(sol_ref, before_ref, after_ref, high_ref, low_ref):
        for at, value in ((0, before_ref[...]), (size, sol_ref[...]), (size + span, after_ref[...])):
            high, low = split(value)
            high_ref[at : at + value.shape[0], :], low_ref[at : at + value.shape[0], :] = high, low

    windows = jax.ShapeDtypeStruct((span + 2 * size, columns), jnp.bfloat16)
    return pl.pallas_call(kernel, out_shape=[windows, windows], name="windows")(sol, before, after)


def subtract_product(arrays, places, relative, right_side, high, low, weights, supers, size, base=None):
    span, columns = right_side.shape
    wide = 3 * size
    n = len(arrays)
    rows = arrays[0].shape[1]
    extra = 0 if base is None else 1

    def kernel(*refs):
        weights_ref, rhs_ref, high_ref, low_ref = refs[:4]
        piece_refs = refs[4 + extra : 4 + extra + n]
        out_ref, held, sem = refs[4 + extra + n :]
        copies = []

        def write(source, target):
            copies.append(pltpu.make_async_copy(source, target, sem.at[len(copies)]))
            copies[-1].start()

        for s in range(supers):
            bands, starts = [], []
            for owner, blocks in places.items():
                row = row_of(owner, rows, relative)
                band = [piece_refs[i][at] for i, at in (blocks[3 * s + c] for c in range(3))]
                bands.append(jnp.concatenate(band, axis=1) * weights_of(weights_ref, s, row, supers, size))
                starts.append(s * size + row if not relative else pl.multiple_of(s * size + row, rows))
            window = pl.ds(s * size, wide)
            result = product(split(jnp.concatenate(bands, axis=0)), (high_ref[window, :], low_ref[window, :]))
            for i, start in enumerate(starts):
                at = (s * len(places) + i) * rows if extra else start
                held[pl.ds(at, rows), :] = rhs_ref[pl.ds(start, rows), :] - result[i * rows : (i + 1) * rows]
                if extra:
                    write(held.at[pl.ds(at, rows), :], out_ref.at[pl.ds(start, rows), :])
            if not extra:
                whole = pl.ds(s * size, size)
                write(held.at[whole, :], out_ref.at[whole, :])
        for copy in copies:
            copy.wait()

    bands = supers * len(places)
    return pl.pallas_call(
        kernel,
        out_shape=shapes([(span, columns)])[0],
        in_specs=[VMEM] * 4 + [ANY] * extra + [VMEM] * n,
        out_specs=ANY,
        input_output_aliases={4: 0} if extra else {},
        scratch_shapes=[
            pltpu.VMEM((bands * rows if extra else span, columns), jnp.float32),
            pltpu.SemaphoreType.DMA((bands if extra else supers,)),
        ],
        compiler_params=pltpu.CompilerParams(vmem_limit_bytes=VMEM_LIMIT),
        cost_estimate=pl.CostEstimate(
            flops=6 * bands * rows * wide * columns, bytes_accessed=8 * bands * rows * wide, transcendentals=0
        ),
        name="residual_rest" if extra else "residual",
    )(weights, right_side, high, low, *([base] if extra else []), *arrays)


def dot(left, right):
    return jnp.dot(left, right, precision=lax.Precision.HIGHEST)


def on_device(right_side, diag_inv, lower, factor_pattern, jacobian, jacobian_pattern):
    supers, rows, size = diag_inv.shape
    columns = right_side.shape[1]
    span = supers * size
    nodes = lax.axis_size("node")

    def blocks_of(array, begin):
        return array, [(0, begin + block) for block in range(array.shape[0])]

    factor_own, jacobian_own, own = pack(diag_inv, lower, jacobian)
    factor_own = blocks_of(factor_own, 0)
    jacobian_own = blocks_of(jacobian_own, 2 * supers)
    own = blocks_of(own, 0)
    count = lax.axis_size("rhs")
    relative = count >= 16 and not count & (count - 1)
    if relative:
        arrived, last, late = gather_panels(own, factor_own, jacobian_own, right_side, "rhs")
    else:
        arrived, last, late = gather_whole(own, "rhs"), [], right_side
    factor = places_of(arrived, 0, 2 * supers)
    jacobians, places = places_of(arrived, 2 * supers, len(own[1]))
    whole = {owner: blocks for owner, blocks in places.items() if len(blocks) == 3 * supers}
    partial = set(places) - set(whole)

    factor_weights, jacobian_weights = widened([factor_pattern, jacobian_pattern], [size, 3 * size])
    sol, parts, down, up = solve(*factor, relative, late, factor_weights, nodes, supers, size)
    if nodes == 2:
        mail = [lax.ppermute(letter, "node", [(0, 1), (1, 0)]) for letter in (down, up)]
        sol, high, low = finish(sol, parts[0], down, *mail, supers)
    else:
        beneath = beyond = jnp.zeros((size, columns), jnp.float32)
        if nodes > 1:
            upwards = [(i, i + 1) for i in range(nodes - 1)]
            downwards = [(i + 1, i) for i in range(nodes - 1)]
            below = above = beneath
            for _ in range(nodes - 1):
                below = lax.ppermute(
                    down[:, :columns] + dot(down[:, columns : columns + size], below), "node", upwards
                )
            for _ in range(nodes - 1):
                leaving = up[:, :columns] + dot(up[:, columns : columns + size], below)
                above = lax.ppermute(leaving + dot(up[:, columns + size :], above), "node", downwards)
            sol = sol + dot(parts[0], below) + dot(parts[1], above)
            beneath = lax.ppermute(sol[span - size :], "node", upwards)
            beyond = lax.ppermute(sol[:size], "node", downwards)
        high, low = split_windows(sol, beneath, beyond)
    subtract = functools.partial(
        subtract_product,
        relative=relative,
        right_side=right_side,
        high=high,
        low=low,
        weights=jacobian_weights,
        supers=supers,
        size=size,
    )
    residual = subtract(jacobians, whole)
    if last:
        arrays, rest = places_of([*arrived, *last] if partial else last, 2 * supers, len(own[1]))
        rest = {owner: blocks for owner, blocks in rest.items() if owner not in whole}
        residual = subtract(arrays, rest, base=residual)
    return sol, residual


def solution(mesh):
    in_specs = (
        P("node", "rhs"),
        P("node", "rhs", None),
        P("node", "rhs", None),
        P("node", None, None),
        P("node", "rhs", None),
        P("node", None, None),
    )
    out_specs = (P("node", "rhs"), P("node", "rhs"))
    return jax.shard_map(on_device, mesh=mesh, in_specs=in_specs, out_specs=out_specs, check_vma=False)
```

```python
import functools

import jax
import jax.numpy as jnp
from jax import lax
from jax.experimental import pallas as pl
from jax.experimental.pallas import tpu as pltpu
from jax.sharding import PartitionSpec as P

VMEM = pl.BlockSpec(memory_space=pltpu.VMEM)
SMEM = pl.BlockSpec(memory_space=pltpu.SMEM)
ANY = pl.BlockSpec(memory_space=pl.ANY)
VMEM_LIMIT = 20 * 2**20
SMALL_LIMIT = 4 * 2**20


def split(value):
    high = value.astype(jnp.bfloat16)
    return high, (value - high.astype(jnp.float32)).astype(jnp.bfloat16)


def product(left, right):
    return jnp.dot(
        jnp.concatenate([left[1], left[0], left[0]], axis=1),
        jnp.concatenate([right[0], right[1], right[0]], axis=0),
        preferred_element_type=jnp.float32,
    )


def after(held, *others):
    return lax.optimization_barrier((held[0], [array for array, _ in others]))[0], held[1]


def joined(*parts):
    if len(parts) == 1:
        return parts[0]
    return jnp.concatenate([array for array, _ in parts]), [name for _, names in parts for name in names]


def cut(held, begin, end):
    return held[0][begin:end], held[1][begin:end]


def sent(held, axis, mask):
    array, names = held
    swapped = lax.ppermute(array, axis, [(i, i ^ mask) for i in range(lax.axis_size(axis))])
    return swapped, [(owner ^ mask, block) for owner, block in names]


def around(held, axis):
    return sent(held, axis, 1), sent(held, axis, 2)


def onward(pair, size, more, axis):
    half = size // 2
    second = joined(*more, cut(pair[1], half, size))
    first = joined(*more, cut(pair[0], 0, half))
    return second, first


def send_both(parts, axis):
    return sent(parts[0], axis, 1), sent(parts[1], axis, 2)


def masks_of(axis):
    masks, step = [], lax.axis_size(axis) // 4
    while step > 1:
        masks.append(4 * (step - 1))
        step //= 2
    return masks


def line_of(held, axis):
    *masks, last = masks_of(axis)
    beside = sent(held, axis, last)
    line = [held]
    for mask in masks:
        line += [sent(part, axis, mask) for part in line]
    return line + [beside] + [sent(part, axis, last) for part in line[1:]]


def gather_panels(own, factor, jacobian, right_side, axis):
    factor_line = line_of(factor, axis)
    own_round = around(own, axis)
    near, far = joined(*factor_line[1:-1]), factor_line[-1]
    second_parts = onward(own_round, len(own[1]), [near], axis)
    second_round = send_both(second_parts, axis)
    third_parts = onward(second_round, len(near[1]), [far], axis)
    third_round = send_both(third_parts, axis)
    factor_parts = onward(third_round, len(far[1]), [], axis)
    factor_across = send_both(factor_parts, axis)

    jacobian_line = [after(jacobian, *second_parts)]
    for mask in masks_of(axis):
        jacobian_line.append(sent(joined(*jacobian_line), axis, mask))
    near, far = joined(*jacobian_line[1:-1]), jacobian_line[-1]
    near_round = around(near, axis)
    near_last = [after(part, *factor_parts) for part in near_round]
    far_parts = onward(near_last, len(near[1]), [far], axis)
    far_round = send_both(far_parts, axis)
    far_across = send_both(onward(far_round, len(far[1]), [], axis), axis)
    right_side, _ = after((right_side, None), *far_parts)
    arrived = [own, *factor_line[1:], *jacobian_line[1:], *own_round, *second_round, *third_round, *factor_across]
    return arrived + [*near_round, *far_round], list(far_across), right_side


def pack(diag_inv, lower, jacobian, spare):
    supers, rows, size = diag_inv.shape
    kept = 3 * supers - spare

    def kernel(diag_ref, lower_ref, jacobian_ref, factor_ref, blocks_ref, own_ref):
        def block(q):
            return jacobian_ref[q // 3, :, q % 3 * size : (q % 3 + 1) * size]

        for s in range(supers):
            factor_ref[s] = own_ref[s] = diag_ref[s]
            factor_ref[supers + s] = own_ref[supers + s] = lower_ref[s]
        for k in range(kept):
            value = jnp.where(lax.axis_index("node") == 0, block(k + 1), block(k)) if spare else block(k)
            blocks_ref[k] = own_ref[2 * supers + k] = value

    return pl.pallas_call(
        kernel,
        out_shape=shapes([(count, rows, size) for count in (2 * supers, kept, 2 * supers + kept)]),
        in_specs=[VMEM] * 3,
        out_specs=[VMEM] * 3,
        name="pack",
    )(diag_inv, lower, jacobian)


def gather_whole(own, axis):
    everything = lax.all_gather(own[0], axis, tiled=True)
    return [(everything, [(owner, block) for owner in range(lax.axis_size(axis)) for _, block in own[1]])]


def places_of(pieces, begin, end):
    arrays, places = [], {}
    for array, names in pieces:
        if not any(begin <= block < end for _, block in names):
            continue
        for at, (owner, block) in enumerate(names):
            if begin <= block < end:
                places.setdefault(owner, {})[block - begin] = (len(arrays), at)
        arrays.append(array)
    return arrays, places


def row_of(owner, rows, relative):
    return pl.multiple_of((lax.axis_index("rhs") ^ owner) * rows, rows) if relative else owner * rows


def shapes(arrays):
    return [jax.ShapeDtypeStruct(shape, jnp.float32) for shape in arrays]


def widened(patterns, wides):
    def widen(pattern_ref, out_ref):
        supers, bands, count = pattern_ref.shape
        step = out_ref.shape[1] // count
        together = max(1, 128 // step)
        lane = lax.broadcasted_iota(jnp.int32, (1, together * step), 1)
        for s in range(supers):
            for a in range(bands):
                for first in range(0, count, together):
                    weight = jnp.full(lane.shape, pattern_ref[s, a, first].astype(jnp.float32))
                    for c in range(1, min(together, count - first)):
                        weight = jnp.where(lane >= c * step, pattern_ref[s, a, first + c].astype(jnp.float32), weight)
                    end = min(first + together, count) * step
                    row = s * bands + a
                    out_ref[row : row + 1, first * step : end] = weight[:, : end - first * step]

    def kernel(*refs):
        for pattern_ref, out_ref in zip(refs[: len(patterns)], refs[len(patterns) :]):
            widen(pattern_ref, out_ref)

    return pl.pallas_call(
        kernel,
        out_shape=shapes([(p.shape[0] * p.shape[1], wide) for p, wide in zip(patterns, wides)]),
        in_specs=[SMEM] * len(patterns),
        out_specs=[VMEM] * len(patterns),
        compiler_params=pltpu.CompilerParams(vmem_limit_bytes=SMALL_LIMIT),
        name="widened",
    )(*patterns)


def weights_of(weights_ref, s, row, supers, size):
    bands = weights_ref.shape[0] // supers
    return weights_ref[pl.ds(s * bands + row // (size // bands), 1), :]


def cuts_of(size):
    third = -(-4 * size // 24) * 8
    return [0, third, 2 * third, 4 * size]


def parts_of(i, size):
    cuts = cuts_of(size)
    for k, (first, last) in enumerate(zip(cuts, cuts[1:])):
        begin, end = max(first, i * size), min(last, (i + 1) * size)
        if begin < end:
            yield k, begin - first, begin - i * size, end - i * size


def solve(arrays, places, relative, right_side, weights, nodes, supers, size):
    columns = right_side.shape[1]
    extra = 0 if nodes == 1 else 1 if nodes == 2 else 2
    width = columns + extra * size
    n = len(arrays)
    rows = arrays[0].shape[1]

    def kernel(*refs):
        weights_ref, rhs_ref = refs[:2]
        piece_refs = refs[2 : 2 + n]
        sol_ref = refs[2 + n]
        extra_refs = refs[3 + n : 3 + n + extra]
        *leaving_refs, panels, forward = refs[3 + n + extra :]
        for owner, blocks in places.items():
            row = row_of(owner, rows, relative)
            for block, (i, at) in blocks.items():
                band = piece_refs[i][at]
                if block >= supers:
                    band = band * weights_of(weights_ref, block - supers, row, supers, size)
                panels[block, pl.ds(row, rows), :] = band
        index = lax.axis_index("node")
        below = jnp.where(index > 0, 1.0, 0.0)
        above = jnp.where(index < nodes - 1, 1.0, 0.0)
        zeros = jnp.zeros((size, size), jnp.float32)

        inverse = [split(panels[s]) for s in range(supers)]
        low = [split(panels[supers + s]) for s in range(supers)]
        down = [product(inverse[s], low[s]) for s in range(supers)]
        previous = None
        for s in range(supers):
            alone = product(inverse[s], split(rhs_ref[s * size : (s + 1) * size, :]))
            if s == 0:
                parts = [alone] + ([down[0] * -below] if extra else []) + [zeros] * (extra - 1)
                previous = jnp.concatenate(parts, axis=1)
            else:
                alone = jnp.concatenate([alone] + [zeros] * extra, axis=1)
                previous = alone - product(split(down[s]), split(previous))
            forward[s] = previous

        solved = None
        for s in reversed(range(supers)):
            turned = panels[s].T
            alone = product(split(turned), split(forward[s]))
            if s < supers - 1:
                up = product(low[s + 1], inverse[s])
                solved = alone - product(split(up.T), split(solved))
            elif extra:
                shift = [jnp.zeros((size, columns), jnp.float32)] + [zeros] * (extra - 1) + [turned * above]
                solved = alone - jnp.concatenate(shift, axis=1)
            else:
                solved = alone
            sol_ref[s * size : (s + 1) * size, :] = solved[:, :columns]
            for e, ref in enumerate(extra_refs):
                ref[s * size : (s + 1) * size, :] = solved[:, columns + e * size : columns + (e + 1) * size]
        entering = product(split(panels[supers].T), split(solved)) if nodes > 1 else None

        if nodes == 2:
            upper = index == 1
            span = supers * size
            letters = [
                jnp.where(upper, entering[:, :columns], forward[supers - 1, :, :columns]),
                entering[:, columns:],
                jnp.where(upper, sol_ref[:size, :], sol_ref[span - size :, :]),
                jnp.where(upper, extra_refs[0][:size, :], extra_refs[0][span - size :, :]),
            ]
            for i, letter in enumerate(letters):
                for k, row, begin, end in parts_of(i, size):
                    leaving_refs[k][row : row + end - begin, :] = letter[begin:end]
        else:
            leaving_refs[0][...] = forward[supers - 1]
            leaving_refs[1][...] = entering if nodes > 1 else forward[0]

    span = supers * size
    cuts = cuts_of(size)
    leaving = [(e - b, columns) for b, e in zip(cuts, cuts[1:])] if nodes == 2 else [(size, width)] * 2
    out = pl.pallas_call(
        kernel,
        out_shape=shapes([(span, columns)] + [(span, size)] * extra + leaving),
        in_specs=[VMEM] * (2 + n),
        out_specs=[VMEM] * (1 + extra + len(leaving)),
        scratch_shapes=[
            pltpu.VMEM((2 * supers, size, size), jnp.float32),
            pltpu.VMEM((supers, size, width), jnp.float32),
        ],
        compiler_params=pltpu.CompilerParams(vmem_limit_bytes=VMEM_LIMIT),
        cost_estimate=pl.CostEstimate(
            flops=16 * supers * size * size * width, bytes_accessed=span * size, transcendentals=0
        ),
        name="solve",
    )(weights, right_side, *arrays)
    return out[0], out[1 : 1 + extra], out[1 + extra :]


def finish(sol, part, own_mail, mail, supers):
    span, columns = sol.shape
    size = span // supers
    n = len(mail)

    def kernel(sol_ref, part_ref, *refs):
        own_refs, mail_refs, (out_ref, high_ref, low_ref, held, sem) = refs[:n], refs[n : 2 * n], refs[2 * n :]

        def letter(piece_refs, i):
            parts = [piece_refs[k][row : row + end - begin, :] for k, row, begin, end in parts_of(i, size)]
            return jnp.concatenate(parts, axis=0)

        lower_one = lax.axis_index("node") == 0
        down = jnp.where(lower_one, letter(own_refs, 0), letter(mail_refs, 0))
        offset = jnp.where(lower_one, letter(mail_refs, 0), letter(own_refs, 0))
        matrix = jnp.where(lower_one, letter(mail_refs, 1), letter(own_refs, 1))
        up = offset + product(split(matrix), split(down))
        mine = split(jnp.where(lower_one, up, down))
        other = split(jnp.where(lower_one, down, up))

        def window(at, value):
            high_ref[at : at + size, :], low_ref[at : at + size, :] = split(value)

        copies = []
        for at in range(0, span, size):
            value = sol_ref[at : at + size, :] + product(split(part_ref[at : at + size, :]), mine)
            held[at : at + size, :] = value
            copies.append(
                pltpu.make_async_copy(held.at[at : at + size, :], out_ref.at[at : at + size, :], sem.at[at // size])
            )
            copies[-1].start()
            window(at + size, value)
        beside = letter(mail_refs, 2) + product(split(letter(mail_refs, 3)), other)
        window(0, jnp.where(lower_one, 0.0, beside))
        window(size + span, jnp.where(lower_one, beside, 0.0))
        for copy in copies:
            copy.wait()

    windows = jax.ShapeDtypeStruct((span + 2 * size, columns), jnp.bfloat16)
    return pl.pallas_call(
        kernel,
        out_shape=shapes([(span, columns)]) + [windows, windows],
        in_specs=[VMEM] * (2 + 2 * n),
        out_specs=[ANY, VMEM, VMEM],
        scratch_shapes=[pltpu.VMEM((span, columns), jnp.float32), pltpu.SemaphoreType.DMA((supers,))],
        compiler_params=pltpu.CompilerParams(vmem_limit_bytes=VMEM_LIMIT),
        cost_estimate=pl.CostEstimate(
            flops=(span + 2 * size) * size * columns, bytes_accessed=span * columns, transcendentals=0
        ),
        name="finish",
    )(sol, part, *own_mail, *mail)


def split_windows(sol, before, after):
    span, columns = sol.shape
    size = before.shape[0]

    def kernel(sol_ref, before_ref, after_ref, high_ref, low_ref):
        for at, value in ((0, before_ref[...]), (size, sol_ref[...]), (size + span, after_ref[...])):
            high, low = split(value)
            high_ref[at : at + value.shape[0], :], low_ref[at : at + value.shape[0], :] = high, low

    windows = jax.ShapeDtypeStruct((span + 2 * size, columns), jnp.bfloat16)
    return pl.pallas_call(kernel, out_shape=[windows, windows], name="windows")(sol, before, after)


def subtract_product(arrays, places, relative, right_side, high, low, weights, supers, size, spare, base=None):
    span, columns = right_side.shape
    wide = 3 * size
    n = len(arrays)
    rows = arrays[0].shape[1]
    extra = 0 if base is None else 1

    def kernel(*refs):
        weights_ref, rhs_ref, high_ref, low_ref = refs[:4]
        piece_refs = refs[4 + extra : 4 + extra + n]
        out_ref, held, sem = refs[4 + extra + n :]
        copies = []

        def block_of(blocks, q):
            def held_as(k):
                if not 0 <= k < 3 * supers - spare:
                    return jnp.zeros((rows, size), jnp.float32)
                i, at = blocks[k]
                return piece_refs[i][at]

            return jnp.where(lax.axis_index("node") == 0, held_as(q - 1), held_as(q)) if spare else held_as(q)

        def write(source, target):
            copies.append(pltpu.make_async_copy(source, target, sem.at[len(copies)]))
            copies[-1].start()

        for s in range(supers):
            bands, starts = [], []
            for owner, blocks in places.items():
                row = row_of(owner, rows, relative)
                band = [block_of(blocks, 3 * s + c) for c in range(3)]
                bands.append(jnp.concatenate(band, axis=1) * weights_of(weights_ref, s, row, supers, size))
                starts.append(s * size + row if not relative else pl.multiple_of(s * size + row, rows))
            window = pl.ds(s * size, wide)
            result = product(split(jnp.concatenate(bands, axis=0)), (high_ref[window, :], low_ref[window, :]))
            for i, start in enumerate(starts):
                at = (s * len(places) + i) * rows if extra else start
                held[pl.ds(at, rows), :] = rhs_ref[pl.ds(start, rows), :] - result[i * rows : (i + 1) * rows]
                if extra:
                    write(held.at[pl.ds(at, rows), :], out_ref.at[pl.ds(start, rows), :])
            if not extra:
                whole = pl.ds(s * size, size)
                write(held.at[whole, :], out_ref.at[whole, :])
        for copy in copies:
            copy.wait()

    bands = supers * len(places)
    return pl.pallas_call(
        kernel,
        out_shape=shapes([(span, columns)])[0],
        in_specs=[VMEM] * 4 + [ANY] * extra + [VMEM] * n,
        out_specs=ANY,
        input_output_aliases={4: 0} if extra else {},
        scratch_shapes=[
            pltpu.VMEM((bands * rows if extra else span, columns), jnp.float32),
            pltpu.SemaphoreType.DMA((bands if extra else supers,)),
        ],
        compiler_params=pltpu.CompilerParams(vmem_limit_bytes=VMEM_LIMIT),
        cost_estimate=pl.CostEstimate(
            flops=6 * bands * rows * wide * columns, bytes_accessed=8 * bands * rows * wide, transcendentals=0
        ),
        name="residual_rest" if extra else "residual",
    )(weights, right_side, high, low, *([base] if extra else []), *arrays)


def dot(left, right):
    return jnp.dot(left, right, precision=lax.Precision.HIGHEST)


def on_device(right_side, diag_inv, lower, factor_pattern, jacobian, jacobian_pattern):
    supers, rows, size = diag_inv.shape
    columns = right_side.shape[1]
    span = supers * size
    nodes = lax.axis_size("node")

    def blocks_of(array, begin):
        return array, [(0, begin + block) for block in range(array.shape[0])]

    spare = 1 if nodes == 2 else 0
    factor_own, jacobian_own, own = pack(diag_inv, lower, jacobian, spare)
    factor_own = blocks_of(factor_own, 0)
    jacobian_own = blocks_of(jacobian_own, 2 * supers)
    own = blocks_of(own, 0)
    count = lax.axis_size("rhs")
    relative = count >= 16 and not count & (count - 1)
    if relative:
        arrived, last, late = gather_panels(own, factor_own, jacobian_own, right_side, "rhs")
    else:
        arrived, last, late = gather_whole(own, "rhs"), [], right_side
    factor = places_of(arrived, 0, 2 * supers)
    jacobians, places = places_of(arrived, 2 * supers, len(own[1]))
    whole = {owner: blocks for owner, blocks in places.items() if len(blocks) == 3 * supers - spare}
    partial = set(places) - set(whole)

    factor_weights, jacobian_weights = widened([factor_pattern, jacobian_pattern], [size, 3 * size])
    sol, parts, leaving = solve(*factor, relative, late, factor_weights, nodes, supers, size)
    if nodes == 2:
        mail = [lax.ppermute(piece, "node", [(0, 1), (1, 0)]) for piece in leaving]
        sol, high, low = finish(sol, parts[0], leaving, mail, supers)
    else:
        beneath = beyond = jnp.zeros((size, columns), jnp.float32)
        if nodes > 1:
            upwards = [(i, i + 1) for i in range(nodes - 1)]
            downwards = [(i + 1, i) for i in range(nodes - 1)]
            below = above = beneath
            down, up = leaving
            for _ in range(nodes - 1):
                below = lax.ppermute(
                    down[:, :columns] + dot(down[:, columns : columns + size], below), "node", upwards
                )
            for _ in range(nodes - 1):
                leaving = up[:, :columns] + dot(up[:, columns : columns + size], below)
                above = lax.ppermute(leaving + dot(up[:, columns + size :], above), "node", downwards)
            sol = sol + dot(parts[0], below) + dot(parts[1], above)
            beneath = lax.ppermute(sol[span - size :], "node", upwards)
            beyond = lax.ppermute(sol[:size], "node", downwards)
        high, low = split_windows(sol, beneath, beyond)
    subtract = functools.partial(
        subtract_product,
        relative=relative,
        right_side=right_side,
        high=high,
        low=low,
        weights=jacobian_weights,
        supers=supers,
        size=size,
        spare=spare,
    )
    residual = subtract(jacobians, whole)
    if last:
        arrays, rest = places_of([*arrived, *last] if partial else last, 2 * supers, len(own[1]))
        rest = {owner: blocks for owner, blocks in rest.items() if owner not in whole}
        residual = subtract(arrays, rest, base=residual)
    return sol, residual


def solution(mesh):
    in_specs = (
        P("node", "rhs"),
        P("node", "rhs", None),
        P("node", "rhs", None),
        P("node", None, None),
        P("node", "rhs", None),
        P("node", None, None),
    )
    out_specs = (P("node", "rhs"), P("node", "rhs"))
    return jax.shard_map(on_device, mesh=mesh, in_specs=in_specs, out_specs=out_specs, check_vma=False)
```

```python
import functools

import jax
import jax.numpy as jnp
from jax import lax
from jax.experimental import pallas as pl
from jax.experimental.pallas import tpu as pltpu
from jax.sharding import PartitionSpec as P

VMEM = pl.BlockSpec(memory_space=pltpu.VMEM)
SMEM = pl.BlockSpec(memory_space=pltpu.SMEM)
ANY = pl.BlockSpec(memory_space=pl.ANY)
VMEM_LIMIT = 20 * 2**20
SMALL_LIMIT = 4 * 2**20


def split(value):
    high = value.astype(jnp.bfloat16)
    return high, (value - high.astype(jnp.float32)).astype(jnp.bfloat16)


def product(left, right):
    return jnp.dot(
        jnp.concatenate([left[1], left[0], left[0]], axis=1),
        jnp.concatenate([right[0], right[1], right[0]], axis=0),
        preferred_element_type=jnp.float32,
    )


def after(held, *others):
    return lax.optimization_barrier((held[0], [array for array, _ in others]))[0], held[1]


def joined(*parts):
    if len(parts) == 1:
        return parts[0]
    return jnp.concatenate([array for array, _ in parts]), [name for _, names in parts for name in names]


def cut(held, begin, end):
    return held[0][begin:end], held[1][begin:end]


def sent(held, axis, mask):
    array, names = held
    swapped = lax.ppermute(array, axis, [(i, i ^ mask) for i in range(lax.axis_size(axis))])
    return swapped, [(owner ^ mask, block) for owner, block in names]


def around(held, axis):
    return sent(held, axis, 1), sent(held, axis, 2)


def onward(pair, size, more, axis):
    half = size // 2
    second = joined(*more, cut(pair[1], half, size))
    first = joined(*more, cut(pair[0], 0, half))
    return second, first


def send_both(parts, axis):
    return sent(parts[0], axis, 1), sent(parts[1], axis, 2)


def masks_of(axis):
    masks, step = [], lax.axis_size(axis) // 4
    while step > 1:
        masks.append(4 * (step - 1))
        step //= 2
    return masks


def line_of(held, axis):
    *masks, last = masks_of(axis)
    beside = sent(held, axis, last)
    line = [held]
    for mask in masks:
        line += [sent(part, axis, mask) for part in line]
    return line + [beside] + [sent(part, axis, last) for part in line[1:]]


def gather_panels(own, factor, jacobian, right_side, axis):
    factor_line = line_of(factor, axis)
    own_round = around(own, axis)
    near, far = joined(*factor_line[1:-1]), factor_line[-1]
    second_parts = onward(own_round, len(own[1]), [near], axis)
    second_round = send_both(second_parts, axis)
    jacobian_line = line_of(after(jacobian, *second_parts), axis)
    second_last = [after(part, jacobian_line[1]) for part in second_round]
    third_parts = onward(second_last, len(near[1]), [far], axis)
    third_round = send_both(third_parts, axis)
    factor_parts = onward(third_round, len(far[1]), [], axis)
    factor_across = send_both(factor_parts, axis)

    half = len(jacobian_line) // 2
    near, far = joined(*jacobian_line[1:half]), joined(*jacobian_line[half:])
    near_round = around(near, axis)
    near_last = [after(part, *factor_parts) for part in near_round]
    far_parts = onward(near_last, len(near[1]), [far], axis)
    far_round = send_both(far_parts, axis)
    far_across = send_both(onward(far_round, len(far[1]), [], axis), axis)
    right_side, _ = after((right_side, None), *far_parts)
    arrived = [own, *factor_line[1:], *jacobian_line[1:], *own_round, *second_round, *third_round, *factor_across]
    return arrived + [*near_round, *far_round], list(far_across), right_side


def pack(diag_inv, lower, jacobian, spare):
    supers, rows, size = diag_inv.shape
    kept = 3 * supers - spare

    def kernel(diag_ref, lower_ref, jacobian_ref, factor_ref, blocks_ref, own_ref):
        def block(q):
            return jacobian_ref[q // 3, :, q % 3 * size : (q % 3 + 1) * size]

        for s in range(supers):
            factor_ref[s] = own_ref[s] = diag_ref[s]
            factor_ref[supers + s] = own_ref[supers + s] = lower_ref[s]
        for k in range(kept):
            value = jnp.where(lax.axis_index("node") == 0, block(k + 1), block(k)) if spare else block(k)
            blocks_ref[k] = own_ref[2 * supers + k] = value

    return pl.pallas_call(
        kernel,
        out_shape=shapes([(count, rows, size) for count in (2 * supers, kept, 2 * supers + kept)]),
        in_specs=[VMEM] * 3,
        out_specs=[VMEM] * 3,
        name="pack",
    )(diag_inv, lower, jacobian)


def gather_whole(own, axis):
    everything = lax.all_gather(own[0], axis, tiled=True)
    return [(everything, [(owner, block) for owner in range(lax.axis_size(axis)) for _, block in own[1]])]


def places_of(pieces, begin, end):
    arrays, places = [], {}
    for array, names in pieces:
        if not any(begin <= block < end for _, block in names):
            continue
        for at, (owner, block) in enumerate(names):
            if begin <= block < end:
                places.setdefault(owner, {})[block - begin] = (len(arrays), at)
        arrays.append(array)
    return arrays, places


def row_of(owner, rows, relative):
    return pl.multiple_of((lax.axis_index("rhs") ^ owner) * rows, rows) if relative else owner * rows


def shapes(arrays):
    return [jax.ShapeDtypeStruct(shape, jnp.float32) for shape in arrays]


def widened(patterns, wides):
    def widen(pattern_ref, out_ref):
        supers, bands, count = pattern_ref.shape
        step = out_ref.shape[1] // count
        together = max(1, 128 // step)
        lane = lax.broadcasted_iota(jnp.int32, (1, together * step), 1)
        for s in range(supers):
            for a in range(bands):
                for first in range(0, count, together):
                    weight = jnp.full(lane.shape, pattern_ref[s, a, first].astype(jnp.float32))
                    for c in range(1, min(together, count - first)):
                        weight = jnp.where(lane >= c * step, pattern_ref[s, a, first + c].astype(jnp.float32), weight)
                    end = min(first + together, count) * step
                    row = s * bands + a
                    out_ref[row : row + 1, first * step : end] = weight[:, : end - first * step]

    def kernel(*refs):
        for pattern_ref, out_ref in zip(refs[: len(patterns)], refs[len(patterns) :]):
            widen(pattern_ref, out_ref)

    return pl.pallas_call(
        kernel,
        out_shape=shapes([(p.shape[0] * p.shape[1], wide) for p, wide in zip(patterns, wides)]),
        in_specs=[SMEM] * len(patterns),
        out_specs=[VMEM] * len(patterns),
        compiler_params=pltpu.CompilerParams(vmem_limit_bytes=SMALL_LIMIT),
        name="widened",
    )(*patterns)


def weights_of(weights_ref, s, row, supers, size):
    bands = weights_ref.shape[0] // supers
    return weights_ref[pl.ds(s * bands + row // (size // bands), 1), :]


def cuts_of(size):
    third = -(-4 * size // 24) * 8
    return [0, third, 2 * third, 4 * size]


def parts_of(i, size):
    cuts = cuts_of(size)
    for k, (first, last) in enumerate(zip(cuts, cuts[1:])):
        begin, end = max(first, i * size), min(last, (i + 1) * size)
        if begin < end:
            yield k, begin - first, begin - i * size, end - i * size


def solve(arrays, places, relative, right_side, weights, nodes, supers, size):
    columns = right_side.shape[1]
    extra = 0 if nodes == 1 else 1 if nodes == 2 else 2
    width = columns + extra * size
    n = len(arrays)
    rows = arrays[0].shape[1]

    def kernel(*refs):
        weights_ref, rhs_ref = refs[:2]
        piece_refs = refs[2 : 2 + n]
        sol_ref = refs[2 + n]
        extra_refs = refs[3 + n : 3 + n + extra]
        *leaving_refs, panels, forward = refs[3 + n + extra :]
        for owner, blocks in places.items():
            row = row_of(owner, rows, relative)
            for block, (i, at) in blocks.items():
                band = piece_refs[i][at]
                if block >= supers:
                    band = band * weights_of(weights_ref, block - supers, row, supers, size)
                panels[block, pl.ds(row, rows), :] = band
        index = lax.axis_index("node")
        below = jnp.where(index > 0, 1.0, 0.0)
        above = jnp.where(index < nodes - 1, 1.0, 0.0)
        zeros = jnp.zeros((size, size), jnp.float32)

        inverse = [split(panels[s]) for s in range(supers)]
        low = [split(panels[supers + s]) for s in range(supers)]
        down = [product(inverse[s], low[s]) for s in range(supers)]
        previous = None
        for s in range(supers):
            alone = product(inverse[s], split(rhs_ref[s * size : (s + 1) * size, :]))
            if s == 0:
                parts = [alone] + ([down[0] * -below] if extra else []) + [zeros] * (extra - 1)
                previous = jnp.concatenate(parts, axis=1)
            else:
                alone = jnp.concatenate([alone] + [zeros] * extra, axis=1)
                previous = alone - product(split(down[s]), split(previous))
            forward[s] = previous

        solved = None
        for s in reversed(range(supers)):
            turned = panels[s].T
            alone = product(split(turned), split(forward[s]))
            if s < supers - 1:
                up = product(low[s + 1], inverse[s])
                solved = alone - product(split(up.T), split(solved))
            elif extra:
                shift = [jnp.zeros((size, columns), jnp.float32)] + [zeros] * (extra - 1) + [turned * above]
                solved = alone - jnp.concatenate(shift, axis=1)
            else:
                solved = alone
            sol_ref[s * size : (s + 1) * size, :] = solved[:, :columns]
            for e, ref in enumerate(extra_refs):
                ref[s * size : (s + 1) * size, :] = solved[:, columns + e * size : columns + (e + 1) * size]
        entering = product(split(panels[supers].T), split(solved)) if nodes > 1 else None

        if nodes == 2:
            upper = index == 1
            span = supers * size
            letters = [
                jnp.where(upper, entering[:, :columns], forward[supers - 1, :, :columns]),
                entering[:, columns:],
                jnp.where(upper, sol_ref[:size, :], sol_ref[span - size :, :]),
                jnp.where(upper, extra_refs[0][:size, :], extra_refs[0][span - size :, :]),
            ]
            for i, letter in enumerate(letters):
                for k, row, begin, end in parts_of(i, size):
                    leaving_refs[k][row : row + end - begin, :] = letter[begin:end]
        else:
            leaving_refs[0][...] = forward[supers - 1]
            leaving_refs[1][...] = entering if nodes > 1 else forward[0]

    span = supers * size
    cuts = cuts_of(size)
    leaving = [(e - b, columns) for b, e in zip(cuts, cuts[1:])] if nodes == 2 else [(size, width)] * 2
    out = pl.pallas_call(
        kernel,
        out_shape=shapes([(span, columns)] + [(span, size)] * extra + leaving),
        in_specs=[VMEM] * (2 + n),
        out_specs=[VMEM] * (1 + extra + len(leaving)),
        scratch_shapes=[
            pltpu.VMEM((2 * supers, size, size), jnp.float32),
            pltpu.VMEM((supers, size, width), jnp.float32),
        ],
        compiler_params=pltpu.CompilerParams(vmem_limit_bytes=VMEM_LIMIT),
        cost_estimate=pl.CostEstimate(
            flops=16 * supers * size * size * width, bytes_accessed=span * size, transcendentals=0
        ),
        name="solve",
    )(weights, right_side, *arrays)
    return out[0], out[1 : 1 + extra], out[1 + extra :]


def finish(sol, part, own_mail, mail, supers):
    span, columns = sol.shape
    size = span // supers
    n = len(mail)

    def kernel(sol_ref, part_ref, *refs):
        own_refs, mail_refs, (out_ref, high_ref, low_ref, held, sem) = refs[:n], refs[n : 2 * n], refs[2 * n :]

        def letter(piece_refs, i):
            parts = [piece_refs[k][row : row + end - begin, :] for k, row, begin, end in parts_of(i, size)]
            return jnp.concatenate(parts, axis=0)

        lower_one = lax.axis_index("node") == 0
        down = jnp.where(lower_one, letter(own_refs, 0), letter(mail_refs, 0))
        offset = jnp.where(lower_one, letter(mail_refs, 0), letter(own_refs, 0))
        matrix = jnp.where(lower_one, letter(mail_refs, 1), letter(own_refs, 1))
        up = offset + product(split(matrix), split(down))
        mine = split(jnp.where(lower_one, up, down))
        other = split(jnp.where(lower_one, down, up))

        def window(at, value):
            high_ref[at : at + size, :], low_ref[at : at + size, :] = split(value)

        copies = []
        for at in range(0, span, size):
            value = sol_ref[at : at + size, :] + product(split(part_ref[at : at + size, :]), mine)
            held[at : at + size, :] = value
            copies.append(
                pltpu.make_async_copy(held.at[at : at + size, :], out_ref.at[at : at + size, :], sem.at[at // size])
            )
            copies[-1].start()
            window(at + size, value)
        beside = letter(mail_refs, 2) + product(split(letter(mail_refs, 3)), other)
        window(0, jnp.where(lower_one, 0.0, beside))
        window(size + span, jnp.where(lower_one, beside, 0.0))
        for copy in copies:
            copy.wait()

    windows = jax.ShapeDtypeStruct((span + 2 * size, columns), jnp.bfloat16)
    return pl.pallas_call(
        kernel,
        out_shape=shapes([(span, columns)]) + [windows, windows],
        in_specs=[VMEM] * (2 + 2 * n),
        out_specs=[ANY, VMEM, VMEM],
        scratch_shapes=[pltpu.VMEM((span, columns), jnp.float32), pltpu.SemaphoreType.DMA((supers,))],
        compiler_params=pltpu.CompilerParams(vmem_limit_bytes=VMEM_LIMIT),
        cost_estimate=pl.CostEstimate(
            flops=(span + 2 * size) * size * columns, bytes_accessed=span * columns, transcendentals=0
        ),
        name="finish",
    )(sol, part, *own_mail, *mail)


def split_windows(sol, before, after):
    span, columns = sol.shape
    size = before.shape[0]

    def kernel(sol_ref, before_ref, after_ref, high_ref, low_ref):
        for at, value in ((0, before_ref[...]), (size, sol_ref[...]), (size + span, after_ref[...])):
            high, low = split(value)
            high_ref[at : at + value.shape[0], :], low_ref[at : at + value.shape[0], :] = high, low

    windows = jax.ShapeDtypeStruct((span + 2 * size, columns), jnp.bfloat16)
    return pl.pallas_call(kernel, out_shape=[windows, windows], name="windows")(sol, before, after)


def subtract_product(arrays, places, relative, right_side, high, low, weights, supers, size, spare, base=None):
    span, columns = right_side.shape
    wide = 3 * size
    n = len(arrays)
    rows = arrays[0].shape[1]
    extra = 0 if base is None else 1

    def kernel(*refs):
        weights_ref, rhs_ref, high_ref, low_ref = refs[:4]
        piece_refs = refs[4 + extra : 4 + extra + n]
        out_ref, held, sem = refs[4 + extra + n :]
        copies = []

        def block_of(blocks, q):
            def held_as(k):
                if not 0 <= k < 3 * supers - spare:
                    return jnp.zeros((rows, size), jnp.float32)
                i, at = blocks[k]
                return piece_refs[i][at]

            return jnp.where(lax.axis_index("node") == 0, held_as(q - 1), held_as(q)) if spare else held_as(q)

        def write(source, target):
            copies.append(pltpu.make_async_copy(source, target, sem.at[len(copies)]))
            copies[-1].start()

        for s in range(supers):
            bands, starts = [], []
            for owner, blocks in places.items():
                row = row_of(owner, rows, relative)
                band = [block_of(blocks, 3 * s + c) for c in range(3)]
                bands.append(jnp.concatenate(band, axis=1) * weights_of(weights_ref, s, row, supers, size))
                starts.append(s * size + row if not relative else pl.multiple_of(s * size + row, rows))
            window = pl.ds(s * size, wide)
            result = product(split(jnp.concatenate(bands, axis=0)), (high_ref[window, :], low_ref[window, :]))
            for i, start in enumerate(starts):
                at = (s * len(places) + i) * rows if extra else start
                held[pl.ds(at, rows), :] = rhs_ref[pl.ds(start, rows), :] - result[i * rows : (i + 1) * rows]
                if extra:
                    write(held.at[pl.ds(at, rows), :], out_ref.at[pl.ds(start, rows), :])
            if not extra:
                whole = pl.ds(s * size, size)
                write(held.at[whole, :], out_ref.at[whole, :])
        for copy in copies:
            copy.wait()

    bands = supers * len(places)
    return pl.pallas_call(
        kernel,
        out_shape=shapes([(span, columns)])[0],
        in_specs=[VMEM] * 4 + [ANY] * extra + [VMEM] * n,
        out_specs=ANY,
        input_output_aliases={4: 0} if extra else {},
        scratch_shapes=[
            pltpu.VMEM((bands * rows if extra else span, columns), jnp.float32),
            pltpu.SemaphoreType.DMA((bands if extra else supers,)),
        ],
        compiler_params=pltpu.CompilerParams(vmem_limit_bytes=VMEM_LIMIT),
        cost_estimate=pl.CostEstimate(
            flops=6 * bands * rows * wide * columns, bytes_accessed=8 * bands * rows * wide, transcendentals=0
        ),
        name="residual_rest" if extra else "residual",
    )(weights, right_side, high, low, *([base] if extra else []), *arrays)


def dot(left, right):
    return jnp.dot(left, right, precision=lax.Precision.HIGHEST)


def on_device(right_side, diag_inv, lower, factor_pattern, jacobian, jacobian_pattern):
    supers, rows, size = diag_inv.shape
    columns = right_side.shape[1]
    span = supers * size
    nodes = lax.axis_size("node")

    def blocks_of(array, begin):
        return array, [(0, begin + block) for block in range(array.shape[0])]

    spare = 1 if nodes == 2 else 0
    factor_own, jacobian_own, own = pack(diag_inv, lower, jacobian, spare)
    factor_own = blocks_of(factor_own, 0)
    jacobian_own = blocks_of(jacobian_own, 2 * supers)
    own = blocks_of(own, 0)
    count = lax.axis_size("rhs")
    relative = count >= 16 and not count & (count - 1)
    if relative:
        arrived, last, late = gather_panels(own, factor_own, jacobian_own, right_side, "rhs")
    else:
        arrived, last, late = gather_whole(own, "rhs"), [], right_side
    factor = places_of(arrived, 0, 2 * supers)
    jacobians, places = places_of(arrived, 2 * supers, len(own[1]))
    whole = {owner: blocks for owner, blocks in places.items() if len(blocks) == 3 * supers - spare}
    partial = set(places) - set(whole)

    factor_weights, jacobian_weights = widened([factor_pattern, jacobian_pattern], [size, 3 * size])
    sol, parts, leaving = solve(*factor, relative, late, factor_weights, nodes, supers, size)
    if nodes == 2:
        mail = [lax.ppermute(piece, "node", [(0, 1), (1, 0)]) for piece in leaving]
        sol, high, low = finish(sol, parts[0], leaving, mail, supers)
    else:
        beneath = beyond = jnp.zeros((size, columns), jnp.float32)
        if nodes > 1:
            upwards = [(i, i + 1) for i in range(nodes - 1)]
            downwards = [(i + 1, i) for i in range(nodes - 1)]
            below = above = beneath
            down, up = leaving
            for _ in range(nodes - 1):
                below = lax.ppermute(
                    down[:, :columns] + dot(down[:, columns : columns + size], below), "node", upwards
                )
            for _ in range(nodes - 1):
                leaving = up[:, :columns] + dot(up[:, columns : columns + size], below)
                above = lax.ppermute(leaving + dot(up[:, columns + size :], above), "node", downwards)
            sol = sol + dot(parts[0], below) + dot(parts[1], above)
            beneath = lax.ppermute(sol[span - size :], "node", upwards)
            beyond = lax.ppermute(sol[:size], "node", downwards)
        high, low = split_windows(sol, beneath, beyond)
    subtract = functools.partial(
        subtract_product,
        relative=relative,
        right_side=right_side,
        high=high,
        low=low,
        weights=jacobian_weights,
        supers=supers,
        size=size,
        spare=spare,
    )
    residual = subtract(jacobians, whole)
    if last:
        arrays, rest = places_of([*arrived, *last] if partial else last, 2 * supers, len(own[1]))
        rest = {owner: blocks for owner, blocks in rest.items() if owner not in whole}
        residual = subtract(arrays, rest, base=residual)
    return sol, residual


def solution(mesh):
    in_specs = (
        P("node", "rhs"),
        P("node", "rhs", None),
        P("node", "rhs", None),
        P("node", None, None),
        P("node", "rhs", None),
        P("node", None, None),
    )
    out_specs = (P("node", "rhs"), P("node", "rhs"))
    return jax.shard_map(on_device, mesh=mesh, in_specs=in_specs, out_specs=out_specs, check_vma=False)
```

```python
import functools

import jax
import jax.numpy as jnp
from jax import lax
from jax.experimental import pallas as pl
from jax.experimental.pallas import tpu as pltpu
from jax.sharding import PartitionSpec as P

VMEM = pl.BlockSpec(memory_space=pltpu.VMEM)
SMEM = pl.BlockSpec(memory_space=pltpu.SMEM)
ANY = pl.BlockSpec(memory_space=pl.ANY)
VMEM_LIMIT = 20 * 2**20
SMALL_LIMIT = 4 * 2**20


def split(value):
    high = value.astype(jnp.bfloat16)
    return high, (value - high.astype(jnp.float32)).astype(jnp.bfloat16)


def product(left, right):
    return jnp.dot(
        jnp.concatenate([left[1], left[0], left[0]], axis=1),
        jnp.concatenate([right[0], right[1], right[0]], axis=0),
        preferred_element_type=jnp.float32,
    )


def after(held, *others):
    return lax.optimization_barrier((held[0], [array for array, _ in others]))[0], held[1]


def joined(*parts):
    if len(parts) == 1:
        return parts[0]
    return jnp.concatenate([array for array, _ in parts]), [name for _, names in parts for name in names]


def cut(held, begin, end):
    return held[0][begin:end], held[1][begin:end]


def sent(held, axis, mask):
    array, names = held
    swapped = lax.ppermute(array, axis, [(i, i ^ mask) for i in range(lax.axis_size(axis))])
    return swapped, [(owner ^ mask, block) for owner, block in names]


def around(held, axis):
    return sent(held, axis, 1), sent(held, axis, 2)


def onward(pair, size, more, axis):
    half = size // 2
    second = joined(*more, cut(pair[1], half, size))
    first = joined(*more, cut(pair[0], 0, half))
    return second, first


def send_both(parts, axis):
    return sent(parts[0], axis, 1), sent(parts[1], axis, 2)


def masks_of(axis):
    masks, step = [], lax.axis_size(axis) // 4
    while step > 1:
        masks.append(4 * (step - 1))
        step //= 2
    return masks


def line_of(held, axis):
    *masks, last = masks_of(axis)
    beside = sent(held, axis, last)
    line = [held]
    for mask in masks:
        line += [sent(part, axis, mask) for part in line]
    return line + [beside] + [sent(part, axis, last) for part in line[1:]]


def gather_panels(own, factor, jacobian, right_side, axis):
    factor_line = line_of(factor, axis)
    own_round = around(own, axis)
    near, far = joined(*factor_line[1:-1]), factor_line[-1]
    second_parts = onward(own_round, len(own[1]), [near], axis)
    second_round = send_both(second_parts, axis)
    third_parts = onward(second_round, len(near[1]), [far], axis)
    third_round = send_both(third_parts, axis)
    factor_parts = onward(third_round, len(far[1]), [], axis)
    factor_across = send_both(factor_parts, axis)

    jacobian_line = [after(jacobian, *second_parts)]
    for mask in masks_of(axis):
        jacobian_line.append(sent(joined(*jacobian_line), axis, mask))
    near, far = joined(*jacobian_line[1:-1]), jacobian_line[-1]
    near_round = around(near, axis)
    near_last = [after(part, *factor_parts) for part in near_round]
    far_parts = onward(near_last, len(near[1]), [far], axis)
    far_round = send_both(far_parts, axis)
    far_across = send_both(onward(far_round, len(far[1]), [], axis), axis)
    right_side, _ = after((right_side, None), *far_parts)
    arrived = [own, *factor_line[1:], *jacobian_line[1:], *own_round, *second_round, *third_round, *factor_across]
    return arrived + [*near_round, *far_round], list(far_across), right_side


def pack(diag_inv, lower, jacobian, spare):
    supers, rows, size = diag_inv.shape
    kept = 3 * supers - spare

    def kernel(diag_ref, lower_ref, jacobian_ref, factor_ref, blocks_ref, own_ref, sem):
        def move(first, last):
            copies = []

            def start(source, target):
                copies.append(pltpu.make_async_copy(source, target, sem.at[len(copies)]))
                copies[-1].start()

            for ref, base in ((own_ref, 2 * supers), (blocks_ref, 0)):
                for c in range(3):
                    begin, end = max(c * supers, first), min((c + 1) * supers, last)
                    band = jacobian_ref.at[pl.ds(begin - c * supers, end - begin), :, pl.ds(c * size, size)]
                    start(band, ref.at[pl.ds(base + begin - first, end - begin)])
            for ref in (own_ref, factor_ref):
                start(diag_ref, ref.at[pl.ds(0, supers)])
                start(lower_ref, ref.at[pl.ds(supers, supers)])
            for copy in copies:
                copy.wait()

        if spare:
            pl.when(lax.axis_index("node") == 0)(lambda: move(1, 3 * supers))
            pl.when(lax.axis_index("node") != 0)(lambda: move(0, kept))
        else:
            move(0, kept)

    return pl.pallas_call(
        kernel,
        out_shape=shapes([(count, rows, size) for count in (2 * supers, kept, 2 * supers + kept)]),
        in_specs=[ANY] * 3,
        out_specs=[ANY] * 3,
        scratch_shapes=[pltpu.SemaphoreType.DMA((10,))],
        compiler_params=pltpu.CompilerParams(vmem_limit_bytes=60 * 2**20),
        name="pack",
    )(diag_inv, lower, jacobian)


def gather_whole(own, axis):
    everything = lax.all_gather(own[0], axis, tiled=True)
    return [(everything, [(owner, block) for owner in range(lax.axis_size(axis)) for _, block in own[1]])]


def places_of(pieces, begin, end):
    arrays, places = [], {}
    for array, names in pieces:
        if not any(begin <= block < end for _, block in names):
            continue
        for at, (owner, block) in enumerate(names):
            if begin <= block < end:
                places.setdefault(owner, {})[block - begin] = (len(arrays), at)
        arrays.append(array)
    return arrays, places


def row_of(owner, rows, relative):
    return pl.multiple_of((lax.axis_index("rhs") ^ owner) * rows, rows) if relative else owner * rows


def shapes(arrays):
    return [jax.ShapeDtypeStruct(shape, jnp.float32) for shape in arrays]


def widened(patterns, wides):
    def widen(pattern_ref, out_ref):
        supers, bands, count = pattern_ref.shape
        step = out_ref.shape[1] // count
        together = max(1, 128 // step)
        lane = lax.broadcasted_iota(jnp.int32, (1, together * step), 1)
        for s in range(supers):
            for a in range(bands):
                for first in range(0, count, together):
                    weight = jnp.full(lane.shape, pattern_ref[s, a, first].astype(jnp.float32))
                    for c in range(1, min(together, count - first)):
                        weight = jnp.where(lane >= c * step, pattern_ref[s, a, first + c].astype(jnp.float32), weight)
                    end = min(first + together, count) * step
                    row = s * bands + a
                    out_ref[row : row + 1, first * step : end] = weight[:, : end - first * step]

    def kernel(*refs):
        for pattern_ref, out_ref in zip(refs[: len(patterns)], refs[len(patterns) :]):
            widen(pattern_ref, out_ref)

    return pl.pallas_call(
        kernel,
        out_shape=shapes([(p.shape[0] * p.shape[1], wide) for p, wide in zip(patterns, wides)]),
        in_specs=[SMEM] * len(patterns),
        out_specs=[VMEM] * len(patterns),
        compiler_params=pltpu.CompilerParams(vmem_limit_bytes=SMALL_LIMIT),
        name="widened",
    )(*patterns)


def weights_of(weights_ref, s, row, supers, size):
    bands = weights_ref.shape[0] // supers
    return weights_ref[pl.ds(s * bands + row // (size // bands), 1), :]


def cuts_of(size):
    third = -(-4 * size // 24) * 8
    return [0, third, 2 * third, 4 * size]


def parts_of(i, size):
    cuts = cuts_of(size)
    for k, (first, last) in enumerate(zip(cuts, cuts[1:])):
        begin, end = max(first, i * size), min(last, (i + 1) * size)
        if begin < end:
            yield k, begin - first, begin - i * size, end - i * size


def solve(arrays, places, relative, right_side, weights, nodes, supers, size):
    columns = right_side.shape[1]
    extra = 0 if nodes == 1 else 1 if nodes == 2 else 2
    width = columns + extra * size
    n = len(arrays)
    rows = arrays[0].shape[1]

    def kernel(*refs):
        weights_ref, rhs_ref = refs[:2]
        piece_refs = refs[2 : 2 + n]
        sol_ref = refs[2 + n]
        extra_refs = refs[3 + n : 3 + n + extra]
        *leaving_refs, panels, forward = refs[3 + n + extra :]
        for owner, blocks in places.items():
            row = row_of(owner, rows, relative)
            for block, (i, at) in blocks.items():
                band = piece_refs[i][at]
                if block >= supers:
                    band = band * weights_of(weights_ref, block - supers, row, supers, size)
                panels[block, pl.ds(row, rows), :] = band
        index = lax.axis_index("node")
        below = jnp.where(index > 0, 1.0, 0.0)
        above = jnp.where(index < nodes - 1, 1.0, 0.0)
        zeros = jnp.zeros((size, size), jnp.float32)

        inverse = [split(panels[s]) for s in range(supers)]
        low = [split(panels[supers + s]) for s in range(supers)]
        down = [product(inverse[s], low[s]) for s in range(supers)]
        previous = None
        for s in range(supers):
            alone = product(inverse[s], split(rhs_ref[s * size : (s + 1) * size, :]))
            if s == 0:
                parts = [alone] + ([down[0] * -below] if extra else []) + [zeros] * (extra - 1)
                previous = jnp.concatenate(parts, axis=1)
            else:
                alone = jnp.concatenate([alone] + [zeros] * extra, axis=1)
                previous = alone - product(split(down[s]), split(previous))
            forward[s] = previous

        solved = None
        for s in reversed(range(supers)):
            turned = panels[s].T
            alone = product(split(turned), split(forward[s]))
            if s < supers - 1:
                up = product(low[s + 1], inverse[s])
                solved = alone - product(split(up.T), split(solved))
            elif extra:
                shift = [jnp.zeros((size, columns), jnp.float32)] + [zeros] * (extra - 1) + [turned * above]
                solved = alone - jnp.concatenate(shift, axis=1)
            else:
                solved = alone
            sol_ref[s * size : (s + 1) * size, :] = solved[:, :columns]
            for e, ref in enumerate(extra_refs):
                ref[s * size : (s + 1) * size, :] = solved[:, columns + e * size : columns + (e + 1) * size]
        entering = product(split(panels[supers].T), split(solved)) if nodes > 1 else None

        if nodes == 2:
            upper = index == 1
            span = supers * size
            letters = [
                jnp.where(upper, entering[:, :columns], forward[supers - 1, :, :columns]),
                entering[:, columns:],
                jnp.where(upper, sol_ref[:size, :], sol_ref[span - size :, :]),
                jnp.where(upper, extra_refs[0][:size, :], extra_refs[0][span - size :, :]),
            ]
            for i, letter in enumerate(letters):
                for k, row, begin, end in parts_of(i, size):
                    leaving_refs[k][row : row + end - begin, :] = letter[begin:end]
        else:
            leaving_refs[0][...] = forward[supers - 1]
            leaving_refs[1][...] = entering if nodes > 1 else forward[0]

    span = supers * size
    cuts = cuts_of(size)
    leaving = [(e - b, columns) for b, e in zip(cuts, cuts[1:])] if nodes == 2 else [(size, width)] * 2
    out = pl.pallas_call(
        kernel,
        out_shape=shapes([(span, columns)] + [(span, size)] * extra + leaving),
        in_specs=[VMEM] * (2 + n),
        out_specs=[VMEM] * (1 + extra + len(leaving)),
        scratch_shapes=[
            pltpu.VMEM((2 * supers, size, size), jnp.float32),
            pltpu.VMEM((supers, size, width), jnp.float32),
        ],
        compiler_params=pltpu.CompilerParams(vmem_limit_bytes=VMEM_LIMIT),
        cost_estimate=pl.CostEstimate(
            flops=16 * supers * size * size * width, bytes_accessed=span * size, transcendentals=0
        ),
        name="solve",
    )(weights, right_side, *arrays)
    return out[0], out[1 : 1 + extra], out[1 + extra :]


def finish(sol, part, own_mail, mail, supers):
    span, columns = sol.shape
    size = span // supers
    n = len(mail)

    def kernel(sol_ref, part_ref, *refs):
        own_refs, mail_refs, (out_ref, high_ref, low_ref, held, sem) = refs[:n], refs[n : 2 * n], refs[2 * n :]

        def letter(piece_refs, i):
            parts = [piece_refs[k][row : row + end - begin, :] for k, row, begin, end in parts_of(i, size)]
            return jnp.concatenate(parts, axis=0)

        lower_one = lax.axis_index("node") == 0
        down = jnp.where(lower_one, letter(own_refs, 0), letter(mail_refs, 0))
        offset = jnp.where(lower_one, letter(mail_refs, 0), letter(own_refs, 0))
        matrix = jnp.where(lower_one, letter(mail_refs, 1), letter(own_refs, 1))
        up = offset + product(split(matrix), split(down))
        mine = split(jnp.where(lower_one, up, down))
        other = split(jnp.where(lower_one, down, up))

        def window(at, value):
            high_ref[at : at + size, :], low_ref[at : at + size, :] = split(value)

        copies = []
        for at in range(0, span, size):
            value = sol_ref[at : at + size, :] + product(split(part_ref[at : at + size, :]), mine)
            held[at : at + size, :] = value
            copies.append(
                pltpu.make_async_copy(held.at[at : at + size, :], out_ref.at[at : at + size, :], sem.at[at // size])
            )
            copies[-1].start()
            window(at + size, value)
        beside = letter(mail_refs, 2) + product(split(letter(mail_refs, 3)), other)
        window(0, jnp.where(lower_one, 0.0, beside))
        window(size + span, jnp.where(lower_one, beside, 0.0))
        for copy in copies:
            copy.wait()

    windows = jax.ShapeDtypeStruct((span + 2 * size, columns), jnp.bfloat16)
    return pl.pallas_call(
        kernel,
        out_shape=shapes([(span, columns)]) + [windows, windows],
        in_specs=[VMEM] * (2 + 2 * n),
        out_specs=[ANY, VMEM, VMEM],
        scratch_shapes=[pltpu.VMEM((span, columns), jnp.float32), pltpu.SemaphoreType.DMA((supers,))],
        compiler_params=pltpu.CompilerParams(vmem_limit_bytes=VMEM_LIMIT),
        cost_estimate=pl.CostEstimate(
            flops=(span + 2 * size) * size * columns, bytes_accessed=span * columns, transcendentals=0
        ),
        name="finish",
    )(sol, part, *own_mail, *mail)


def split_windows(sol, before, after):
    span, columns = sol.shape
    size = before.shape[0]

    def kernel(sol_ref, before_ref, after_ref, high_ref, low_ref):
        for at, value in ((0, before_ref[...]), (size, sol_ref[...]), (size + span, after_ref[...])):
            high, low = split(value)
            high_ref[at : at + value.shape[0], :], low_ref[at : at + value.shape[0], :] = high, low

    windows = jax.ShapeDtypeStruct((span + 2 * size, columns), jnp.bfloat16)
    return pl.pallas_call(kernel, out_shape=[windows, windows], name="windows")(sol, before, after)


def subtract_product(arrays, places, relative, right_side, high, low, weights, supers, size, spare, base=None):
    span, columns = right_side.shape
    wide = 3 * size
    n = len(arrays)
    rows = arrays[0].shape[1]
    extra = 0 if base is None else 1

    def kernel(*refs):
        weights_ref, rhs_ref, high_ref, low_ref = refs[:4]
        piece_refs = refs[4 + extra : 4 + extra + n]
        out_ref, held, sem = refs[4 + extra + n :]
        copies = []

        def block_of(blocks, q):
            def held_as(k):
                if not 0 <= k < 3 * supers - spare:
                    return jnp.zeros((rows, size), jnp.float32)
                i, at = blocks[k]
                return piece_refs[i][at]

            return jnp.where(lax.axis_index("node") == 0, held_as(q - 1), held_as(q)) if spare else held_as(q)

        def write(source, target):
            copies.append(pltpu.make_async_copy(source, target, sem.at[len(copies)]))
            copies[-1].start()

        for s in range(supers):
            bands, starts = [], []
            for owner, blocks in places.items():
                row = row_of(owner, rows, relative)
                band = [block_of(blocks, c * supers + s) for c in range(3)]
                bands.append(jnp.concatenate(band, axis=1) * weights_of(weights_ref, s, row, supers, size))
                starts.append(s * size + row if not relative else pl.multiple_of(s * size + row, rows))
            window = pl.ds(s * size, wide)
            result = product(split(jnp.concatenate(bands, axis=0)), (high_ref[window, :], low_ref[window, :]))
            for i, start in enumerate(starts):
                at = (s * len(places) + i) * rows if extra else start
                held[pl.ds(at, rows), :] = rhs_ref[pl.ds(start, rows), :] - result[i * rows : (i + 1) * rows]
                if extra:
                    write(held.at[pl.ds(at, rows), :], out_ref.at[pl.ds(start, rows), :])
            if not extra:
                whole = pl.ds(s * size, size)
                write(held.at[whole, :], out_ref.at[whole, :])
        for copy in copies:
            copy.wait()

    bands = supers * len(places)
    return pl.pallas_call(
        kernel,
        out_shape=shapes([(span, columns)])[0],
        in_specs=[VMEM] * 4 + [ANY] * extra + [VMEM] * n,
        out_specs=ANY,
        input_output_aliases={4: 0} if extra else {},
        scratch_shapes=[
            pltpu.VMEM((bands * rows if extra else span, columns), jnp.float32),
            pltpu.SemaphoreType.DMA((bands if extra else supers,)),
        ],
        compiler_params=pltpu.CompilerParams(vmem_limit_bytes=VMEM_LIMIT),
        cost_estimate=pl.CostEstimate(
            flops=6 * bands * rows * wide * columns, bytes_accessed=8 * bands * rows * wide, transcendentals=0
        ),
        name="residual_rest" if extra else "residual",
    )(weights, right_side, high, low, *([base] if extra else []), *arrays)


def dot(left, right):
    return jnp.dot(left, right, precision=lax.Precision.HIGHEST)


def on_device(right_side, diag_inv, lower, factor_pattern, jacobian, jacobian_pattern):
    supers, rows, size = diag_inv.shape
    columns = right_side.shape[1]
    span = supers * size
    nodes = lax.axis_size("node")

    def blocks_of(array, begin):
        return array, [(0, begin + block) for block in range(array.shape[0])]

    spare = 1 if nodes == 2 else 0
    factor_own, jacobian_own, own = pack(diag_inv, lower, jacobian, spare)
    factor_own = blocks_of(factor_own, 0)
    jacobian_own = blocks_of(jacobian_own, 2 * supers)
    own = blocks_of(own, 0)
    count = lax.axis_size("rhs")
    relative = count >= 16 and not count & (count - 1)
    if relative:
        arrived, last, late = gather_panels(own, factor_own, jacobian_own, right_side, "rhs")
    else:
        arrived, last, late = gather_whole(own, "rhs"), [], right_side
    factor = places_of(arrived, 0, 2 * supers)
    jacobians, places = places_of(arrived, 2 * supers, len(own[1]))
    whole = {owner: blocks for owner, blocks in places.items() if len(blocks) == 3 * supers - spare}
    partial = set(places) - set(whole)

    factor_weights, jacobian_weights = widened([factor_pattern, jacobian_pattern], [size, 3 * size])
    sol, parts, leaving = solve(*factor, relative, late, factor_weights, nodes, supers, size)
    if nodes == 2:
        mail = [lax.ppermute(piece, "node", [(0, 1), (1, 0)]) for piece in leaving]
        sol, high, low = finish(sol, parts[0], leaving, mail, supers)
    else:
        beneath = beyond = jnp.zeros((size, columns), jnp.float32)
        if nodes > 1:
            upwards = [(i, i + 1) for i in range(nodes - 1)]
            downwards = [(i + 1, i) for i in range(nodes - 1)]
            below = above = beneath
            down, up = leaving
            for _ in range(nodes - 1):
                below = lax.ppermute(
                    down[:, :columns] + dot(down[:, columns : columns + size], below), "node", upwards
                )
            for _ in range(nodes - 1):
                leaving = up[:, :columns] + dot(up[:, columns : columns + size], below)
                above = lax.ppermute(leaving + dot(up[:, columns + size :], above), "node", downwards)
            sol = sol + dot(parts[0], below) + dot(parts[1], above)
            beneath = lax.ppermute(sol[span - size :], "node", upwards)
            beyond = lax.ppermute(sol[:size], "node", downwards)
        high, low = split_windows(sol, beneath, beyond)
    subtract = functools.partial(
        subtract_product,
        relative=relative,
        right_side=right_side,
        high=high,
        low=low,
        weights=jacobian_weights,
        supers=supers,
        size=size,
        spare=spare,
    )
    residual = subtract(jacobians, whole)
    if last:
        arrays, rest = places_of([*arrived, *last] if partial else last, 2 * supers, len(own[1]))
        rest = {owner: blocks for owner, blocks in rest.items() if owner not in whole}
        residual = subtract(arrays, rest, base=residual)
    return sol, residual


def solution(mesh):
    in_specs = (
        P("node", "rhs"),
        P("node", "rhs", None),
        P("node", "rhs", None),
        P("node", None, None),
        P("node", "rhs", None),
        P("node", None, None),
    )
    out_specs = (P("node", "rhs"), P("node", "rhs"))
    return jax.shard_map(on_device, mesh=mesh, in_specs=in_specs, out_specs=out_specs, check_vma=False)
```

```python
import functools

import jax
import jax.numpy as jnp
from jax import lax
from jax.experimental import pallas as pl
from jax.experimental.pallas import tpu as pltpu
from jax.sharding import PartitionSpec as P

VMEM = pl.BlockSpec(memory_space=pltpu.VMEM)
SMEM = pl.BlockSpec(memory_space=pltpu.SMEM)
ANY = pl.BlockSpec(memory_space=pl.ANY)
VMEM_LIMIT = 20 * 2**20
SMALL_LIMIT = 4 * 2**20


def split(value):
    high = value.astype(jnp.bfloat16)
    return high, (value - high.astype(jnp.float32)).astype(jnp.bfloat16)


def product(left, right):
    return jnp.dot(
        jnp.concatenate([left[1], left[0], left[0]], axis=1),
        jnp.concatenate([right[0], right[1], right[0]], axis=0),
        preferred_element_type=jnp.float32,
    )


def after(held, *others):
    return lax.optimization_barrier((held[0], [array for array, _ in others]))[0], held[1]


def joined(*parts):
    if len(parts) == 1:
        return parts[0]
    return jnp.concatenate([array for array, _ in parts]), [name for _, names in parts for name in names]


def cut(held, begin, end):
    return held[0][begin:end], held[1][begin:end]


def sent(held, axis, mask):
    array, names = held
    swapped = lax.ppermute(array, axis, [(i, i ^ mask) for i in range(lax.axis_size(axis))])
    return swapped, [(owner ^ mask, block) for owner, block in names]


def around(held, axis):
    return sent(held, axis, 1), sent(held, axis, 2)


def onward(pair, size, more, axis):
    half = size // 2
    second = joined(*more, cut(pair[1], half, size))
    first = joined(*more, cut(pair[0], 0, half))
    return second, first


def onward_joined(pair, size, more, axis):
    half = size // 2
    second, first = more[1] + pair[1][1][half:size], more[1] + pair[0][1][:half]
    length = len(more[1])

    def kernel(first_ref, second_ref, more_ref, to_first_ref, to_second_ref):
        to_first_ref[:length] = to_second_ref[:length] = more_ref[...]
        to_first_ref[length:] = second_ref[half:size]
        to_second_ref[length:] = first_ref[:half]

    out = pl.pallas_call(
        kernel,
        out_shape=shapes([(len(names), *more[0].shape[1:]) for names in (second, first)]),
        in_specs=[VMEM] * 3,
        out_specs=[VMEM] * 2,
        compiler_params=pltpu.CompilerParams(vmem_limit_bytes=SMALL_LIMIT),
        cost_estimate=pl.CostEstimate(flops=0, bytes_accessed=4 * more[0].size, transcendentals=0),
        name="onward",
    )(pair[0][0], pair[1][0], more[0])
    return (out[0], second), (out[1], first)


def send_both(parts, axis):
    return sent(parts[0], axis, 1), sent(parts[1], axis, 2)


def masks_of(axis):
    masks, step = [], lax.axis_size(axis) // 4
    while step > 1:
        masks.append(4 * (step - 1))
        step //= 2
    return masks


def line_of(held, axis):
    *masks, last = masks_of(axis)
    beside = sent(held, axis, last)
    line = [held]
    for mask in masks:
        line += [sent(part, axis, mask) for part in line]
    return line + [beside] + [sent(part, axis, last) for part in line[1:]]


def gather_panels(own, factor, jacobian, right_side, axis):
    factor_line = line_of(factor, axis)
    own_round = around(own, axis)
    near, far = joined(*factor_line[1:-1]), factor_line[-1]
    second_parts = onward(own_round, len(own[1]), [near], axis)
    second_round = send_both(second_parts, axis)
    third_parts = onward(second_round, len(near[1]), [far], axis)
    third_round = send_both(third_parts, axis)
    factor_parts = onward(third_round, len(far[1]), [], axis)
    factor_across = send_both(factor_parts, axis)

    jacobian_line = [after(jacobian, *second_parts)]
    for mask in masks_of(axis):
        jacobian_line.append(sent(joined(*jacobian_line), axis, mask))
    near, far = joined(*jacobian_line[1:-1]), jacobian_line[-1]
    near_round = around(near, axis)
    near_last = [after(part, *factor_parts) for part in near_round]
    far_parts = onward_joined(near_last, len(near[1]), far, axis)
    far_round = send_both(far_parts, axis)
    far_across = send_both(onward(far_round, len(far[1]), [], axis), axis)
    right_side, _ = after((right_side, None), *far_parts)
    arrived = [own, *factor_line[1:], *jacobian_line[1:], *own_round, *second_round, *third_round, *factor_across]
    return arrived + [*near_round, *far_round], list(far_across), right_side


def pack(diag_inv, lower, jacobian, spare):
    supers, rows, size = diag_inv.shape
    kept = 3 * supers - spare

    def kernel(diag_ref, lower_ref, jacobian_ref, factor_ref, blocks_ref, own_ref):
        def block(q):
            return jacobian_ref[q // 3, :, q % 3 * size : (q % 3 + 1) * size]

        for s in range(supers):
            factor_ref[s] = own_ref[s] = diag_ref[s]
            factor_ref[supers + s] = own_ref[supers + s] = lower_ref[s]
        for k in range(kept):
            value = jnp.where(lax.axis_index("node") == 0, block(k + 1), block(k)) if spare else block(k)
            blocks_ref[k] = own_ref[2 * supers + k] = value

    return pl.pallas_call(
        kernel,
        out_shape=shapes([(count, rows, size) for count in (2 * supers, kept, 2 * supers + kept)]),
        in_specs=[VMEM] * 3,
        out_specs=[VMEM] * 3,
        name="pack",
    )(diag_inv, lower, jacobian)


def gather_whole(own, axis):
    everything = lax.all_gather(own[0], axis, tiled=True)
    return [(everything, [(owner, block) for owner in range(lax.axis_size(axis)) for _, block in own[1]])]


def places_of(pieces, begin, end):
    arrays, places = [], {}
    for array, names in pieces:
        if not any(begin <= block < end for _, block in names):
            continue
        for at, (owner, block) in enumerate(names):
            if begin <= block < end:
                places.setdefault(owner, {})[block - begin] = (len(arrays), at)
        arrays.append(array)
    return arrays, places


def row_of(owner, rows, relative):
    return pl.multiple_of((lax.axis_index("rhs") ^ owner) * rows, rows) if relative else owner * rows


def shapes(arrays):
    return [jax.ShapeDtypeStruct(shape, jnp.float32) for shape in arrays]


def widened(patterns, wides):
    def widen(pattern_ref, out_ref):
        supers, bands, count = pattern_ref.shape
        step = out_ref.shape[1] // count
        together = max(1, 128 // step)
        lane = lax.broadcasted_iota(jnp.int32, (1, together * step), 1)
        for s in range(supers):
            for a in range(bands):
                for first in range(0, count, together):
                    weight = jnp.full(lane.shape, pattern_ref[s, a, first].astype(jnp.float32))
                    for c in range(1, min(together, count - first)):
                        weight = jnp.where(lane >= c * step, pattern_ref[s, a, first + c].astype(jnp.float32), weight)
                    end = min(first + together, count) * step
                    row = s * bands + a
                    out_ref[row : row + 1, first * step : end] = weight[:, : end - first * step]

    def kernel(*refs):
        for pattern_ref, out_ref in zip(refs[: len(patterns)], refs[len(patterns) :]):
            widen(pattern_ref, out_ref)

    return pl.pallas_call(
        kernel,
        out_shape=shapes([(p.shape[0] * p.shape[1], wide) for p, wide in zip(patterns, wides)]),
        in_specs=[SMEM] * len(patterns),
        out_specs=[VMEM] * len(patterns),
        compiler_params=pltpu.CompilerParams(vmem_limit_bytes=SMALL_LIMIT),
        name="widened",
    )(*patterns)


def weights_of(weights_ref, s, row, supers, size):
    bands = weights_ref.shape[0] // supers
    return weights_ref[pl.ds(s * bands + row // (size // bands), 1), :]


def cuts_of(size):
    third = -(-4 * size // 24) * 8
    return [0, third, 2 * third, 4 * size]


def parts_of(i, size):
    cuts = cuts_of(size)
    for k, (first, last) in enumerate(zip(cuts, cuts[1:])):
        begin, end = max(first, i * size), min(last, (i + 1) * size)
        if begin < end:
            yield k, begin - first, begin - i * size, end - i * size


def solve(arrays, places, relative, right_side, weights, nodes, supers, size):
    columns = right_side.shape[1]
    extra = 0 if nodes == 1 else 1 if nodes == 2 else 2
    width = columns + extra * size
    n = len(arrays)
    rows = arrays[0].shape[1]

    def kernel(*refs):
        weights_ref, rhs_ref = refs[:2]
        piece_refs = refs[2 : 2 + n]
        sol_ref = refs[2 + n]
        extra_refs = refs[3 + n : 3 + n + extra]
        *leaving_refs, panels, forward = refs[3 + n + extra :]
        for owner, blocks in places.items():
            row = row_of(owner, rows, relative)
            for block, (i, at) in blocks.items():
                band = piece_refs[i][at]
                if block >= supers:
                    band = band * weights_of(weights_ref, block - supers, row, supers, size)
                panels[block, pl.ds(row, rows), :] = band
        index = lax.axis_index("node")
        below = jnp.where(index > 0, 1.0, 0.0)
        above = jnp.where(index < nodes - 1, 1.0, 0.0)
        zeros = jnp.zeros((size, size), jnp.float32)

        inverse = [split(panels[s]) for s in range(supers)]
        low = [split(panels[supers + s]) for s in range(supers)]
        down = [product(inverse[s], low[s]) for s in range(supers)]
        previous = None
        for s in range(supers):
            alone = product(inverse[s], split(rhs_ref[s * size : (s + 1) * size, :]))
            if s == 0:
                parts = [alone] + ([down[0] * -below] if extra else []) + [zeros] * (extra - 1)
                previous = jnp.concatenate(parts, axis=1)
            else:
                alone = jnp.concatenate([alone] + [zeros] * extra, axis=1)
                previous = alone - product(split(down[s]), split(previous))
            forward[s] = previous

        solved = None
        for s in reversed(range(supers)):
            turned = panels[s].T
            alone = product(split(turned), split(forward[s]))
            if s < supers - 1:
                up = product(low[s + 1], inverse[s])
                solved = alone - product(split(up.T), split(solved))
            elif extra:
                shift = [jnp.zeros((size, columns), jnp.float32)] + [zeros] * (extra - 1) + [turned * above]
                solved = alone - jnp.concatenate(shift, axis=1)
            else:
                solved = alone
            sol_ref[s * size : (s + 1) * size, :] = solved[:, :columns]
            for e, ref in enumerate(extra_refs):
                ref[s * size : (s + 1) * size, :] = solved[:, columns + e * size : columns + (e + 1) * size]
        entering = product(split(panels[supers].T), split(solved)) if nodes > 1 else None

        if nodes == 2:
            upper = index == 1
            span = supers * size
            letters = [
                jnp.where(upper, entering[:, :columns], forward[supers - 1, :, :columns]),
                entering[:, columns:],
                jnp.where(upper, sol_ref[:size, :], sol_ref[span - size :, :]),
                jnp.where(upper, extra_refs[0][:size, :], extra_refs[0][span - size :, :]),
            ]
            for i, letter in enumerate(letters):
                for k, row, begin, end in parts_of(i, size):
                    leaving_refs[k][row : row + end - begin, :] = letter[begin:end]
        else:
            leaving_refs[0][...] = forward[supers - 1]
            leaving_refs[1][...] = entering if nodes > 1 else forward[0]

    span = supers * size
    cuts = cuts_of(size)
    leaving = [(e - b, columns) for b, e in zip(cuts, cuts[1:])] if nodes == 2 else [(size, width)] * 2
    out = pl.pallas_call(
        kernel,
        out_shape=shapes([(span, columns)] + [(span, size)] * extra + leaving),
        in_specs=[VMEM] * (2 + n),
        out_specs=[VMEM] * (1 + extra + len(leaving)),
        scratch_shapes=[
            pltpu.VMEM((2 * supers, size, size), jnp.float32),
            pltpu.VMEM((supers, size, width), jnp.float32),
        ],
        compiler_params=pltpu.CompilerParams(vmem_limit_bytes=VMEM_LIMIT),
        cost_estimate=pl.CostEstimate(
            flops=16 * supers * size * size * width, bytes_accessed=span * size, transcendentals=0
        ),
        name="solve",
    )(weights, right_side, *arrays)
    return out[0], out[1 : 1 + extra], out[1 + extra :]


def finish(sol, part, own_mail, mail, supers):
    span, columns = sol.shape
    size = span // supers
    n = len(mail)

    def kernel(sol_ref, part_ref, *refs):
        own_refs, mail_refs, (out_ref, high_ref, low_ref, held, sem) = refs[:n], refs[n : 2 * n], refs[2 * n :]

        def letter(piece_refs, i):
            parts = [piece_refs[k][row : row + end - begin, :] for k, row, begin, end in parts_of(i, size)]
            return jnp.concatenate(parts, axis=0)

        lower_one = lax.axis_index("node") == 0
        down = jnp.where(lower_one, letter(own_refs, 0), letter(mail_refs, 0))
        offset = jnp.where(lower_one, letter(mail_refs, 0), letter(own_refs, 0))
        matrix = jnp.where(lower_one, letter(mail_refs, 1), letter(own_refs, 1))
        up = offset + product(split(matrix), split(down))
        mine = split(jnp.where(lower_one, up, down))
        other = split(jnp.where(lower_one, down, up))

        def window(at, value):
            high_ref[at : at + size, :], low_ref[at : at + size, :] = split(value)

        copies = []
        for at in range(0, span, size):
            value = sol_ref[at : at + size, :] + product(split(part_ref[at : at + size, :]), mine)
            held[at : at + size, :] = value
            copies.append(
                pltpu.make_async_copy(held.at[at : at + size, :], out_ref.at[at : at + size, :], sem.at[at // size])
            )
            copies[-1].start()
            window(at + size, value)
        beside = letter(mail_refs, 2) + product(split(letter(mail_refs, 3)), other)
        window(0, jnp.where(lower_one, 0.0, beside))
        window(size + span, jnp.where(lower_one, beside, 0.0))
        for copy in copies:
            copy.wait()

    windows = jax.ShapeDtypeStruct((span + 2 * size, columns), jnp.bfloat16)
    return pl.pallas_call(
        kernel,
        out_shape=shapes([(span, columns)]) + [windows, windows],
        in_specs=[VMEM] * (2 + 2 * n),
        out_specs=[ANY, VMEM, VMEM],
        scratch_shapes=[pltpu.VMEM((span, columns), jnp.float32), pltpu.SemaphoreType.DMA((supers,))],
        compiler_params=pltpu.CompilerParams(vmem_limit_bytes=VMEM_LIMIT),
        cost_estimate=pl.CostEstimate(
            flops=(span + 2 * size) * size * columns, bytes_accessed=span * columns, transcendentals=0
        ),
        name="finish",
    )(sol, part, *own_mail, *mail)


def split_windows(sol, before, after):
    span, columns = sol.shape
    size = before.shape[0]

    def kernel(sol_ref, before_ref, after_ref, high_ref, low_ref):
        for at, value in ((0, before_ref[...]), (size, sol_ref[...]), (size + span, after_ref[...])):
            high, low = split(value)
            high_ref[at : at + value.shape[0], :], low_ref[at : at + value.shape[0], :] = high, low

    windows = jax.ShapeDtypeStruct((span + 2 * size, columns), jnp.bfloat16)
    return pl.pallas_call(kernel, out_shape=[windows, windows], name="windows")(sol, before, after)


def subtract_product(arrays, places, relative, right_side, high, low, weights, supers, size, spare, base=None):
    span, columns = right_side.shape
    wide = 3 * size
    n = len(arrays)
    rows = arrays[0].shape[1]
    extra = 0 if base is None else 1

    def kernel(*refs):
        weights_ref, rhs_ref, high_ref, low_ref = refs[:4]
        piece_refs = refs[4 + extra : 4 + extra + n]
        out_ref, held, sem = refs[4 + extra + n :]
        copies = []

        def block_of(blocks, q):
            def held_as(k):
                if not 0 <= k < 3 * supers - spare:
                    return jnp.zeros((rows, size), jnp.float32)
                i, at = blocks[k]
                return piece_refs[i][at]

            return jnp.where(lax.axis_index("node") == 0, held_as(q - 1), held_as(q)) if spare else held_as(q)

        def write(source, target):
            copies.append(pltpu.make_async_copy(source, target, sem.at[len(copies)]))
            copies[-1].start()

        for s in range(supers):
            bands, starts = [], []
            for owner, blocks in places.items():
                row = row_of(owner, rows, relative)
                band = [block_of(blocks, 3 * s + c) for c in range(3)]
                bands.append(jnp.concatenate(band, axis=1) * weights_of(weights_ref, s, row, supers, size))
                starts.append(s * size + row if not relative else pl.multiple_of(s * size + row, rows))
            window = pl.ds(s * size, wide)
            result = product(split(jnp.concatenate(bands, axis=0)), (high_ref[window, :], low_ref[window, :]))
            for i, start in enumerate(starts):
                at = (s * len(places) + i) * rows if extra else start
                held[pl.ds(at, rows), :] = rhs_ref[pl.ds(start, rows), :] - result[i * rows : (i + 1) * rows]
                if extra:
                    write(held.at[pl.ds(at, rows), :], out_ref.at[pl.ds(start, rows), :])
            if not extra:
                whole = pl.ds(s * size, size)
                write(held.at[whole, :], out_ref.at[whole, :])
        for copy in copies:
            copy.wait()

    bands = supers * len(places)
    return pl.pallas_call(
        kernel,
        out_shape=shapes([(span, columns)])[0],
        in_specs=[VMEM] * 4 + [ANY] * extra + [VMEM] * n,
        out_specs=ANY,
        input_output_aliases={4: 0} if extra else {},
        scratch_shapes=[
            pltpu.VMEM((bands * rows if extra else span, columns), jnp.float32),
            pltpu.SemaphoreType.DMA((bands if extra else supers,)),
        ],
        compiler_params=pltpu.CompilerParams(vmem_limit_bytes=VMEM_LIMIT),
        cost_estimate=pl.CostEstimate(
            flops=6 * bands * rows * wide * columns, bytes_accessed=8 * bands * rows * wide, transcendentals=0
        ),
        name="residual_rest" if extra else "residual",
    )(weights, right_side, high, low, *([base] if extra else []), *arrays)


def dot(left, right):
    return jnp.dot(left, right, precision=lax.Precision.HIGHEST)


def on_device(right_side, diag_inv, lower, factor_pattern, jacobian, jacobian_pattern):
    supers, rows, size = diag_inv.shape
    columns = right_side.shape[1]
    span = supers * size
    nodes = lax.axis_size("node")

    def blocks_of(array, begin):
        return array, [(0, begin + block) for block in range(array.shape[0])]

    spare = 1 if nodes == 2 else 0
    factor_own, jacobian_own, own = pack(diag_inv, lower, jacobian, spare)
    factor_own = blocks_of(factor_own, 0)
    jacobian_own = blocks_of(jacobian_own, 2 * supers)
    own = blocks_of(own, 0)
    count = lax.axis_size("rhs")
    relative = count >= 16 and not count & (count - 1)
    if relative:
        arrived, last, late = gather_panels(own, factor_own, jacobian_own, right_side, "rhs")
    else:
        arrived, last, late = gather_whole(own, "rhs"), [], right_side
    factor = places_of(arrived, 0, 2 * supers)
    jacobians, places = places_of(arrived, 2 * supers, len(own[1]))
    whole = {owner: blocks for owner, blocks in places.items() if len(blocks) == 3 * supers - spare}
    partial = set(places) - set(whole)

    factor_weights, jacobian_weights = widened([factor_pattern, jacobian_pattern], [size, 3 * size])
    sol, parts, leaving = solve(*factor, relative, late, factor_weights, nodes, supers, size)
    if nodes == 2:
        mail = [lax.ppermute(piece, "node", [(0, 1), (1, 0)]) for piece in leaving]
        sol, high, low = finish(sol, parts[0], leaving, mail, supers)
    else:
        beneath = beyond = jnp.zeros((size, columns), jnp.float32)
        if nodes > 1:
            upwards = [(i, i + 1) for i in range(nodes - 1)]
            downwards = [(i + 1, i) for i in range(nodes - 1)]
            below = above = beneath
            down, up = leaving
            for _ in range(nodes - 1):
                below = lax.ppermute(
                    down[:, :columns] + dot(down[:, columns : columns + size], below), "node", upwards
                )
            for _ in range(nodes - 1):
                leaving = up[:, :columns] + dot(up[:, columns : columns + size], below)
                above = lax.ppermute(leaving + dot(up[:, columns + size :], above), "node", downwards)
            sol = sol + dot(parts[0], below) + dot(parts[1], above)
            beneath = lax.ppermute(sol[span - size :], "node", upwards)
            beyond = lax.ppermute(sol[:size], "node", downwards)
        high, low = split_windows(sol, beneath, beyond)
    subtract = functools.partial(
        subtract_product,
        relative=relative,
        right_side=right_side,
        high=high,
        low=low,
        weights=jacobian_weights,
        supers=supers,
        size=size,
        spare=spare,
    )
    residual = subtract(jacobians, whole)
    if last:
        arrays, rest = places_of([*arrived, *last] if partial else last, 2 * supers, len(own[1]))
        rest = {owner: blocks for owner, blocks in rest.items() if owner not in whole}
        residual = subtract(arrays, rest, base=residual)
    return sol, residual


def solution(mesh):
    in_specs = (
        P("node", "rhs"),
        P("node", "rhs", None),
        P("node", "rhs", None),
        P("node", None, None),
        P("node", "rhs", None),
        P("node", None, None),
    )
    out_specs = (P("node", "rhs"), P("node", "rhs"))
    return jax.shard_map(on_device, mesh=mesh, in_specs=in_specs, out_specs=out_specs, check_vma=False)
```

```python
import functools

import jax
import jax.numpy as jnp
from jax import lax
from jax.experimental import pallas as pl
from jax.experimental.pallas import tpu as pltpu
from jax.sharding import PartitionSpec as P

VMEM = pl.BlockSpec(memory_space=pltpu.VMEM)
SMEM = pl.BlockSpec(memory_space=pltpu.SMEM)
ANY = pl.BlockSpec(memory_space=pl.ANY)
VMEM_LIMIT = 20 * 2**20
SMALL_LIMIT = 4 * 2**20


def split(value):
    high = value.astype(jnp.bfloat16)
    return high, (value - high.astype(jnp.float32)).astype(jnp.bfloat16)


def product(left, right):
    return jnp.dot(
        jnp.concatenate([left[1], left[0], left[0]], axis=1),
        jnp.concatenate([right[0], right[1], right[0]], axis=0),
        preferred_element_type=jnp.float32,
    )


def after(held, *others):
    return lax.optimization_barrier((held[0], [array for array, _ in others]))[0], held[1]


def joined(*parts):
    if len(parts) == 1:
        return parts[0]
    return jnp.concatenate([array for array, _ in parts]), [name for _, names in parts for name in names]


def cut(held, begin, end):
    return held[0][begin:end], held[1][begin:end]


def sent(held, axis, mask):
    array, names = held
    swapped = lax.ppermute(array, axis, [(i, i ^ mask) for i in range(lax.axis_size(axis))])
    return swapped, [(owner ^ mask, block) for owner, block in names]


def around(held, axis):
    return sent(held, axis, 1), sent(held, axis, 2)


def onward(pair, size, more, axis):
    half = size // 2
    second = joined(*more, cut(pair[1], half, size))
    first = joined(*more, cut(pair[0], 0, half))
    return second, first


def onward_joined(pair, size, more, axis):
    half = size // 2
    second, first = more[1] + pair[1][1][half:size], more[1] + pair[0][1][:half]
    length = len(more[1])

    def kernel(first_ref, second_ref, more_ref, to_first_ref, to_second_ref):
        to_first_ref[:length] = to_second_ref[:length] = more_ref[...]
        to_first_ref[length:] = second_ref[half:size]
        to_second_ref[length:] = first_ref[:half]

    out = pl.pallas_call(
        kernel,
        out_shape=shapes([(len(names), *more[0].shape[1:]) for names in (second, first)]),
        in_specs=[VMEM] * 3,
        out_specs=[VMEM] * 2,
        compiler_params=pltpu.CompilerParams(vmem_limit_bytes=SMALL_LIMIT),
        cost_estimate=pl.CostEstimate(flops=0, bytes_accessed=4 * more[0].size, transcendentals=0),
        name="onward",
    )(pair[0][0], pair[1][0], more[0])
    return (out[0], second), (out[1], first)


def send_both(parts, axis):
    return sent(parts[0], axis, 1), sent(parts[1], axis, 2)


def masks_of(axis):
    masks, step = [], lax.axis_size(axis) // 4
    while step > 1:
        masks.append(4 * (step - 1))
        step //= 2
    return masks


def line_of(held, axis):
    *masks, last = masks_of(axis)
    beside = sent(held, axis, last)
    line = [held]
    for mask in masks:
        line += [sent(part, axis, mask) for part in line]
    return line + [beside] + [sent(part, axis, last) for part in line[1:]]


def gather_panels(own, factor, jacobian, right_side, tables, axis):
    factor_line = line_of(factor, axis)
    own_round = around(own, axis)
    near, far = joined(*factor_line[1:-1]), factor_line[-1]
    far = after(far, *[(table, None) for table in tables])
    second_parts = onward(own_round, len(own[1]), [near], axis)
    second_round = send_both(second_parts, axis)
    third_parts = onward(second_round, len(near[1]), [far], axis)
    third_round = send_both(third_parts, axis)
    factor_parts = onward(third_round, len(far[1]), [], axis)
    factor_across = send_both(factor_parts, axis)

    jacobian_line = [after(jacobian, *second_parts)]
    for mask in masks_of(axis):
        jacobian_line.append(sent(joined(*jacobian_line), axis, mask))
    near, far = joined(*jacobian_line[1:-1]), jacobian_line[-1]
    near_round = around(near, axis)
    near_last = [after(part, *factor_parts) for part in near_round]
    far_parts = onward_joined(near_last, len(near[1]), far, axis)
    far_round = send_both(far_parts, axis)
    far_across = send_both(onward(far_round, len(far[1]), [], axis), axis)
    right_side, _ = after((right_side, None), *far_parts)
    arrived = [own, *factor_line[1:], *jacobian_line[1:], *own_round, *second_round, *third_round, *factor_across]
    return arrived + [*near_round, *far_round], list(far_across), right_side


def pack(diag_inv, lower, jacobian, spare):
    supers, rows, size = diag_inv.shape
    kept = 3 * supers - spare

    def kernel(diag_ref, lower_ref, jacobian_ref, factor_ref, blocks_ref, own_ref):
        def block(q):
            return jacobian_ref[q // 3, :, q % 3 * size : (q % 3 + 1) * size]

        for s in range(supers):
            factor_ref[s] = own_ref[s] = diag_ref[s]
            factor_ref[supers + s] = own_ref[supers + s] = lower_ref[s]
        for k in range(kept):
            value = jnp.where(lax.axis_index("node") == 0, block(k + 1), block(k)) if spare else block(k)
            blocks_ref[k] = own_ref[2 * supers + k] = value

    return pl.pallas_call(
        kernel,
        out_shape=shapes([(count, rows, size) for count in (2 * supers, kept, 2 * supers + kept)]),
        in_specs=[VMEM] * 3,
        out_specs=[VMEM] * 3,
        name="pack",
    )(diag_inv, lower, jacobian)


def gather_whole(own, axis):
    everything = lax.all_gather(own[0], axis, tiled=True)
    return [(everything, [(owner, block) for owner in range(lax.axis_size(axis)) for _, block in own[1]])]


def places_of(pieces, begin, end):
    arrays, places = [], {}
    for array, names in pieces:
        if not any(begin <= block < end for _, block in names):
            continue
        for at, (owner, block) in enumerate(names):
            if begin <= block < end:
                places.setdefault(owner, {})[block - begin] = (len(arrays), at)
        arrays.append(array)
    return arrays, places


def row_of(owner, rows, relative):
    return pl.multiple_of((lax.axis_index("rhs") ^ owner) * rows, rows) if relative else owner * rows


def shapes(arrays):
    return [jax.ShapeDtypeStruct(shape, jnp.float32) for shape in arrays]


def widened(patterns, wides):
    def widen(pattern_ref, out_ref):
        supers, bands, count = pattern_ref.shape
        step = out_ref.shape[1] // count
        together = max(1, 128 // step)
        lane = lax.broadcasted_iota(jnp.int32, (1, together * step), 1)
        for s in range(supers):
            for a in range(bands):
                for first in range(0, count, together):
                    weight = jnp.full(lane.shape, pattern_ref[s, a, first].astype(jnp.float32))
                    for c in range(1, min(together, count - first)):
                        weight = jnp.where(lane >= c * step, pattern_ref[s, a, first + c].astype(jnp.float32), weight)
                    end = min(first + together, count) * step
                    row = s * bands + a
                    out_ref[row : row + 1, first * step : end] = weight[:, : end - first * step]

    def kernel(*refs):
        for pattern_ref, out_ref in zip(refs[: len(patterns)], refs[len(patterns) :]):
            widen(pattern_ref, out_ref)

    return pl.pallas_call(
        kernel,
        out_shape=shapes([(p.shape[0] * p.shape[1], wide) for p, wide in zip(patterns, wides)]),
        in_specs=[SMEM] * len(patterns),
        out_specs=[VMEM] * len(patterns),
        compiler_params=pltpu.CompilerParams(vmem_limit_bytes=SMALL_LIMIT),
        name="widened",
    )(*patterns)


def weights_of(weights_ref, s, row, supers, size):
    bands = weights_ref.shape[0] // supers
    return weights_ref[pl.ds(s * bands + row // (size // bands), 1), :]


def cuts_of(size):
    third = -(-4 * size // 24) * 8
    return [0, third, 2 * third, 4 * size]


def parts_of(i, size):
    cuts = cuts_of(size)
    for k, (first, last) in enumerate(zip(cuts, cuts[1:])):
        begin, end = max(first, i * size), min(last, (i + 1) * size)
        if begin < end:
            yield k, begin - first, begin - i * size, end - i * size


def solve(arrays, places, relative, right_side, weights, nodes, supers, size):
    columns = right_side.shape[1]
    extra = 0 if nodes == 1 else 1 if nodes == 2 else 2
    width = columns + extra * size
    n = len(arrays)
    rows = arrays[0].shape[1]

    def kernel(*refs):
        weights_ref, rhs_ref = refs[:2]
        piece_refs = refs[2 : 2 + n]
        sol_ref = refs[2 + n]
        extra_refs = refs[3 + n : 3 + n + extra]
        *leaving_refs, panels, forward = refs[3 + n + extra :]
        for owner, blocks in places.items():
            row = row_of(owner, rows, relative)
            for block, (i, at) in blocks.items():
                band = piece_refs[i][at]
                if block >= supers:
                    band = band * weights_of(weights_ref, block - supers, row, supers, size)
                panels[block, pl.ds(row, rows), :] = band
        index = lax.axis_index("node")
        below = jnp.where(index > 0, 1.0, 0.0)
        above = jnp.where(index < nodes - 1, 1.0, 0.0)
        zeros = jnp.zeros((size, size), jnp.float32)

        inverse = [split(panels[s]) for s in range(supers)]
        low = [split(panels[supers + s]) for s in range(supers)]
        down = [product(inverse[s], low[s]) for s in range(supers)]
        previous = None
        for s in range(supers):
            alone = product(inverse[s], split(rhs_ref[s * size : (s + 1) * size, :]))
            if s == 0:
                parts = [alone] + ([down[0] * -below] if extra else []) + [zeros] * (extra - 1)
                previous = jnp.concatenate(parts, axis=1)
            else:
                alone = jnp.concatenate([alone] + [zeros] * extra, axis=1)
                previous = alone - product(split(down[s]), split(previous))
            forward[s] = previous

        solved = None
        for s in reversed(range(supers)):
            turned = panels[s].T
            alone = product(split(turned), split(forward[s]))
            if s < supers - 1:
                up = product(low[s + 1], inverse[s])
                solved = alone - product(split(up.T), split(solved))
            elif extra:
                shift = [jnp.zeros((size, columns), jnp.float32)] + [zeros] * (extra - 1) + [turned * above]
                solved = alone - jnp.concatenate(shift, axis=1)
            else:
                solved = alone
            sol_ref[s * size : (s + 1) * size, :] = solved[:, :columns]
            for e, ref in enumerate(extra_refs):
                ref[s * size : (s + 1) * size, :] = solved[:, columns + e * size : columns + (e + 1) * size]
        entering = product(split(panels[supers].T), split(solved)) if nodes > 1 else None

        if nodes == 2:
            upper = index == 1
            span = supers * size
            letters = [
                jnp.where(upper, entering[:, :columns], forward[supers - 1, :, :columns]),
                entering[:, columns:],
                jnp.where(upper, sol_ref[:size, :], sol_ref[span - size :, :]),
                jnp.where(upper, extra_refs[0][:size, :], extra_refs[0][span - size :, :]),
            ]
            for i, letter in enumerate(letters):
                for k, row, begin, end in parts_of(i, size):
                    leaving_refs[k][row : row + end - begin, :] = letter[begin:end]
        else:
            leaving_refs[0][...] = forward[supers - 1]
            leaving_refs[1][...] = entering if nodes > 1 else forward[0]

    span = supers * size
    cuts = cuts_of(size)
    leaving = [(e - b, columns) for b, e in zip(cuts, cuts[1:])] if nodes == 2 else [(size, width)] * 2
    out = pl.pallas_call(
        kernel,
        out_shape=shapes([(span, columns)] + [(span, size)] * extra + leaving),
        in_specs=[VMEM] * (2 + n),
        out_specs=[VMEM] * (1 + extra + len(leaving)),
        scratch_shapes=[
            pltpu.VMEM((2 * supers, size, size), jnp.float32),
            pltpu.VMEM((supers, size, width), jnp.float32),
        ],
        compiler_params=pltpu.CompilerParams(vmem_limit_bytes=VMEM_LIMIT),
        cost_estimate=pl.CostEstimate(
            flops=16 * supers * size * size * width, bytes_accessed=span * size, transcendentals=0
        ),
        name="solve",
    )(weights, right_side, *arrays)
    return out[0], out[1 : 1 + extra], out[1 + extra :]


def finish(sol, part, own_mail, mail, supers):
    span, columns = sol.shape
    size = span // supers
    n = len(mail)

    def kernel(sol_ref, part_ref, *refs):
        own_refs, mail_refs, (out_ref, high_ref, low_ref, held, sem) = refs[:n], refs[n : 2 * n], refs[2 * n :]

        def letter(piece_refs, i):
            parts = [piece_refs[k][row : row + end - begin, :] for k, row, begin, end in parts_of(i, size)]
            return jnp.concatenate(parts, axis=0)

        lower_one = lax.axis_index("node") == 0
        down = jnp.where(lower_one, letter(own_refs, 0), letter(mail_refs, 0))
        offset = jnp.where(lower_one, letter(mail_refs, 0), letter(own_refs, 0))
        matrix = jnp.where(lower_one, letter(mail_refs, 1), letter(own_refs, 1))
        up = offset + product(split(matrix), split(down))
        mine = split(jnp.where(lower_one, up, down))
        other = split(jnp.where(lower_one, down, up))

        def window(at, value):
            high_ref[at : at + size, :], low_ref[at : at + size, :] = split(value)

        copies = []
        for at in range(0, span, size):
            value = sol_ref[at : at + size, :] + product(split(part_ref[at : at + size, :]), mine)
            held[at : at + size, :] = value
            copies.append(
                pltpu.make_async_copy(held.at[at : at + size, :], out_ref.at[at : at + size, :], sem.at[at // size])
            )
            copies[-1].start()
            window(at + size, value)
        beside = letter(mail_refs, 2) + product(split(letter(mail_refs, 3)), other)
        window(0, jnp.where(lower_one, 0.0, beside))
        window(size + span, jnp.where(lower_one, beside, 0.0))
        for copy in copies:
            copy.wait()

    windows = jax.ShapeDtypeStruct((span + 2 * size, columns), jnp.bfloat16)
    return pl.pallas_call(
        kernel,
        out_shape=shapes([(span, columns)]) + [windows, windows],
        in_specs=[VMEM] * (2 + 2 * n),
        out_specs=[ANY, VMEM, VMEM],
        scratch_shapes=[pltpu.VMEM((span, columns), jnp.float32), pltpu.SemaphoreType.DMA((supers,))],
        compiler_params=pltpu.CompilerParams(vmem_limit_bytes=VMEM_LIMIT),
        cost_estimate=pl.CostEstimate(
            flops=(span + 2 * size) * size * columns, bytes_accessed=span * columns, transcendentals=0
        ),
        name="finish",
    )(sol, part, *own_mail, *mail)


def split_windows(sol, before, after):
    span, columns = sol.shape
    size = before.shape[0]

    def kernel(sol_ref, before_ref, after_ref, high_ref, low_ref):
        for at, value in ((0, before_ref[...]), (size, sol_ref[...]), (size + span, after_ref[...])):
            high, low = split(value)
            high_ref[at : at + value.shape[0], :], low_ref[at : at + value.shape[0], :] = high, low

    windows = jax.ShapeDtypeStruct((span + 2 * size, columns), jnp.bfloat16)
    return pl.pallas_call(kernel, out_shape=[windows, windows], name="windows")(sol, before, after)


def subtract_product(arrays, places, relative, right_side, high, low, weights, supers, size, spare, base=None):
    span, columns = right_side.shape
    wide = 3 * size
    n = len(arrays)
    rows = arrays[0].shape[1]
    extra = 0 if base is None else 1

    def kernel(*refs):
        weights_ref, rhs_ref, high_ref, low_ref = refs[:4]
        piece_refs = refs[4 + extra : 4 + extra + n]
        out_ref, held, sem = refs[4 + extra + n :]
        copies = []

        def block_of(blocks, q):
            def held_as(k):
                if not 0 <= k < 3 * supers - spare:
                    return jnp.zeros((rows, size), jnp.float32)
                i, at = blocks[k]
                return piece_refs[i][at]

            return jnp.where(lax.axis_index("node") == 0, held_as(q - 1), held_as(q)) if spare else held_as(q)

        def write(source, target):
            copies.append(pltpu.make_async_copy(source, target, sem.at[len(copies)]))
            copies[-1].start()

        for s in range(supers):
            bands, starts = [], []
            for owner, blocks in places.items():
                row = row_of(owner, rows, relative)
                band = [block_of(blocks, 3 * s + c) for c in range(3)]
                bands.append(jnp.concatenate(band, axis=1) * weights_of(weights_ref, s, row, supers, size))
                starts.append(s * size + row if not relative else pl.multiple_of(s * size + row, rows))
            window = pl.ds(s * size, wide)
            result = product(split(jnp.concatenate(bands, axis=0)), (high_ref[window, :], low_ref[window, :]))
            for i, start in enumerate(starts):
                at = (s * len(places) + i) * rows if extra else start
                held[pl.ds(at, rows), :] = rhs_ref[pl.ds(start, rows), :] - result[i * rows : (i + 1) * rows]
                if extra:
                    write(held.at[pl.ds(at, rows), :], out_ref.at[pl.ds(start, rows), :])
            if not extra:
                whole = pl.ds(s * size, size)
                write(held.at[whole, :], out_ref.at[whole, :])
        for copy in copies:
            copy.wait()

    bands = supers * len(places)
    return pl.pallas_call(
        kernel,
        out_shape=shapes([(span, columns)])[0],
        in_specs=[VMEM] * 4 + [ANY] * extra + [VMEM] * n,
        out_specs=ANY,
        input_output_aliases={4: 0} if extra else {},
        scratch_shapes=[
            pltpu.VMEM((bands * rows if extra else span, columns), jnp.float32),
            pltpu.SemaphoreType.DMA((bands if extra else supers,)),
        ],
        compiler_params=pltpu.CompilerParams(vmem_limit_bytes=VMEM_LIMIT),
        cost_estimate=pl.CostEstimate(
            flops=6 * bands * rows * wide * columns, bytes_accessed=8 * bands * rows * wide, transcendentals=0
        ),
        name="residual_rest" if extra else "residual",
    )(weights, right_side, high, low, *([base] if extra else []), *arrays)


def dot(left, right):
    return jnp.dot(left, right, precision=lax.Precision.HIGHEST)


def on_device(right_side, diag_inv, lower, factor_pattern, jacobian, jacobian_pattern):
    supers, rows, size = diag_inv.shape
    columns = right_side.shape[1]
    span = supers * size
    nodes = lax.axis_size("node")

    def blocks_of(array, begin):
        return array, [(0, begin + block) for block in range(array.shape[0])]

    spare = 1 if nodes == 2 else 0
    factor_own, jacobian_own, own = pack(diag_inv, lower, jacobian, spare)
    factor_own = blocks_of(factor_own, 0)
    jacobian_own = blocks_of(jacobian_own, 2 * supers)
    own = blocks_of(own, 0)
    tables = factor_weights, jacobian_weights = widened([factor_pattern, jacobian_pattern], [size, 3 * size])
    count = lax.axis_size("rhs")
    relative = count >= 16 and not count & (count - 1)
    if relative:
        arrived, last, late = gather_panels(own, factor_own, jacobian_own, right_side, tables, "rhs")
    else:
        arrived, last, late = gather_whole(own, "rhs"), [], right_side
    factor = places_of(arrived, 0, 2 * supers)
    jacobians, places = places_of(arrived, 2 * supers, len(own[1]))
    whole = {owner: blocks for owner, blocks in places.items() if len(blocks) == 3 * supers - spare}
    partial = set(places) - set(whole)

    sol, parts, leaving = solve(*factor, relative, late, factor_weights, nodes, supers, size)
    if nodes == 2:
        mail = [lax.ppermute(piece, "node", [(0, 1), (1, 0)]) for piece in leaving]
        sol, high, low = finish(sol, parts[0], leaving, mail, supers)
    else:
        beneath = beyond = jnp.zeros((size, columns), jnp.float32)
        if nodes > 1:
            upwards = [(i, i + 1) for i in range(nodes - 1)]
            downwards = [(i + 1, i) for i in range(nodes - 1)]
            below = above = beneath
            down, up = leaving
            for _ in range(nodes - 1):
                below = lax.ppermute(
                    down[:, :columns] + dot(down[:, columns : columns + size], below), "node", upwards
                )
            for _ in range(nodes - 1):
                leaving = up[:, :columns] + dot(up[:, columns : columns + size], below)
                above = lax.ppermute(leaving + dot(up[:, columns + size :], above), "node", downwards)
            sol = sol + dot(parts[0], below) + dot(parts[1], above)
            beneath = lax.ppermute(sol[span - size :], "node", upwards)
            beyond = lax.ppermute(sol[:size], "node", downwards)
        high, low = split_windows(sol, beneath, beyond)
    subtract = functools.partial(
        subtract_product,
        relative=relative,
        right_side=right_side,
        high=high,
        low=low,
        weights=jacobian_weights,
        supers=supers,
        size=size,
        spare=spare,
    )
    residual = subtract(jacobians, whole)
    if last:
        arrays, rest = places_of([*arrived, *last] if partial else last, 2 * supers, len(own[1]))
        rest = {owner: blocks for owner, blocks in rest.items() if owner not in whole}
        residual = subtract(arrays, rest, base=residual)
    return sol, residual


def solution(mesh):
    in_specs = (
        P("node", "rhs"),
        P("node", "rhs", None),
        P("node", "rhs", None),
        P("node", None, None),
        P("node", "rhs", None),
        P("node", None, None),
    )
    out_specs = (P("node", "rhs"), P("node", "rhs"))
    return jax.shard_map(on_device, mesh=mesh, in_specs=in_specs, out_specs=out_specs, check_vma=False)
```
